256 devices in a mesh: row: 8 (over z_hi, core), col: 32 (over x, z_lo, y).
Axes of the slice: x: 4, y: 4, z: 8 (z_hi: 4, z_lo: 2; z = z_hi * 2 + z_lo), core: 2. Of those that a mesh axis runs over, the one named last changes fastest.
Arguments:
- node_feats: bfloat16 [2048, 25, 128], P(('row', 'col')), may hold values from -6 to 6
- grad_out: bfloat16 [2048, 25, 128], P(('row', 'col')), may hold values from -6 to 6
- edge_src: int32 [8, 32, 512], P('row', 'col'), may hold values from 0 to 63
- edge_tgt: int32 [8, 32, 512], P('row', 'col'), may hold values from 0 to 255
- edge_counts: int32 [8, 32], P('row', 'col'), may hold values from 64 to 512, as said below
- wigner: bfloat16 [8, 32, 512, 475], P('row', 'col'), may hold values from -1 to 1, as said below
- w_zero: bfloat16 [1280, 640], replicated, may hold values from -0.15625 to 0.15625
- w_one: bfloat16 [2, 1024, 512], replicated, may hold values from -0.1875 to 0.1875
- w_two: bfloat16 [2, 768, 384], replicated, may hold values from -0.21875 to 0.21875
Outputs:
- grad_nodes: float32 [2048, 25, 128], P(('row', 'col'))
The draws below stay inside these ranges and needn't reach their ends.
Inputs may be any that keep to these rules, and one draw needn't show every extreme that they name: `edge_counts`: slots at or past a tile's count are ignored. In every row of tiles one tile holds exactly 512 edges. `edge_src`: slot values at or past the tile's count are arbitrary but in range. `edge_tgt`: slot values at or past the tile's count are arbitrary but in range. `wigner`: for every degree l, the rows of orders -2..2 (as far as l allows) hold the matching rows of an orthogonal (2l+1) x (2l+1) block in the columns of degree l, column index l*l + l + m; all other entries are zero.
All inputs are finite; a program needn't handle non-finite values.
Results may differ from the reference program's by a relative error of at most 0.015.
Values may be sent and summed in bfloat16 or wider, within the bound.
A program may use at most 64 MiB of HBM per device.

```python
import jax
import jax.numpy as jnp
from jax import lax

A_DEV = 8
E_CAP = 512
C = 128
COEF = 25
ROW_TILES = 8
COL_TILES = 32
TGT_TILE = 256
SRC_TILE = 64
ATOMS = 2048


rotated_order = ((0, 0), (1, 0), (2, 0), (3, 0), (4, 0), (1, 1), (2, 1), (3, 1), (4, 1), (1, -1), (2, -1), (3, -1), (4, -1), (2, 2), (3, 2), (4, 2), (2, -2), (3, -2), (4, -2))


def draw_edge_counts(key, part):
    spread = jax.random.randint(jax.random.fold_in(key, 1), (ROW_TILES, COL_TILES), E_CAP // 8, 3 * E_CAP // 4 + 1)
    full_column = jax.random.randint(jax.random.fold_in(key, 2), (ROW_TILES, 1), 0, COL_TILES)
    columns = jnp.arange(COL_TILES, dtype=jnp.int32)[None, :]
    return jnp.where(columns == full_column, E_CAP, spread).astype(jnp.int32)


def draw_wigner(key, part):
    leading = (ROW_TILES, COL_TILES, E_CAP)
    blocks = []
    for degree in range(5):
        block_width = 2 * degree + 1
        normal_block = jax.random.normal(jax.random.fold_in(key, 10 + degree), leading + (block_width, block_width), jnp.float32)
        orthogonal, triangle = jnp.linalg.qr(normal_block)
        blocks.append(orthogonal)
    rows_out = []
    for degree, order_m in rotated_order:
        block_width = 2 * degree + 1
        picked = blocks[degree][..., degree + order_m, :]
        before = jnp.zeros(leading + (degree * degree,), jnp.float32)
        behind = jnp.zeros(leading + (25 - degree * degree - block_width,), jnp.float32)
        rows_out.append(jnp.concatenate([before, picked, behind], axis=-1))
    return jnp.stack(rows_out, axis=-2).reshape(leading + (475,)).astype(jnp.bfloat16)


def with_ends(entries, key, low, top_value):
    shape = entries.shape
    index_at = [jax.random.randint(jax.random.fold_in(key, axis), (), 0, shape[axis]) for axis in range(len(shape))]
    entries = entries.at[tuple(index_at)].set(low)
    longest = shape.index(max(shape))
    index_at[longest] = (index_at[longest] + 1) % shape[longest]
    return entries.at[tuple(index_at)].set(top_value)


def block_scale(stream_key, extent, pieces, smallest, high):
    level = 1.0
    for axis_at, blocks in pieces:
        heights = jax.random.uniform(jax.random.fold_in(jax.random.fold_in(stream_key, 6), axis_at), (blocks,), jnp.float32, smallest / len(pieces), high / len(pieces))
        level = level * jnp.repeat(jnp.exp(heights), extent[axis_at] // blocks).reshape((-1,) + (1,) * (len(extent) - 1 - axis_at))
    return level


def normal_values(key, extent, width, reach, shards=(), kind=jnp.bfloat16):
    drawn = jax.random.normal(key, extent, jnp.float32) * width
    if len(shards) > 0:
        drawn = block_scale(key, extent, shards, -0.22, 0.18) * drawn
    return jnp.clip(drawn, min=-reach, max=reach).astype(kind)


def setup_inputs(seed: int = 0) -> dict:
    keys = jax.random.split(jax.random.key(seed), 10)
    return {
        "node_feats": normal_values(keys[0], (ATOMS, COEF, C), 1.0, 6.0, ((0, 256),)),
        "grad_out": normal_values(keys[1], (ATOMS, COEF, C), 1.0, 6.0, ((0, 256),)),
        "edge_src": with_ends(jax.random.randint(keys[2], (ROW_TILES, COL_TILES, E_CAP), 0, SRC_TILE), jax.random.fold_in(keys[2], 1), 0, SRC_TILE - 1).astype(jnp.int32),
        "edge_tgt": with_ends(jax.random.randint(keys[3], (ROW_TILES, COL_TILES, E_CAP), 0, TGT_TILE), jax.random.fold_in(keys[3], 1), 0, TGT_TILE - 1).astype(jnp.int32),
        "edge_counts": draw_edge_counts(jax.random.fold_in(keys[9], 71), 0),
        "wigner": draw_wigner(jax.random.fold_in(keys[9], 71), 0),
        "w_zero": normal_values(keys[6], (10 * C, 5 * C), (10 * C) ** -0.5, 0.15625),
        "w_one": normal_values(keys[7], (2, 8 * C, 4 * C), (8 * C) ** -0.5, 0.1875),
        "w_two": normal_values(keys[8], (2, 6 * C, 3 * C), (6 * C) ** -0.5, 0.21875),
    }


def so2_apply(edge_in, w_zero, w_one, w_two):
    edge_count = edge_in.shape[0]
    zero_part = jnp.dot(edge_in[:, 0:5].reshape(edge_count, -1).astype(jnp.float32), w_zero.astype(jnp.float32), preferred_element_type=jnp.float32)
    outputs = [zero_part.reshape(edge_count, 5, -1)]
    for first_row, row_count, weights in ((5, 4, w_one), (13, 3, w_two)):
        plus_part = edge_in[:, first_row:first_row + row_count].reshape(edge_count, -1)
        minus_part = edge_in[:, first_row + row_count:first_row + 2 * row_count].reshape(edge_count, -1)
        stacked = jnp.concatenate([plus_part, minus_part], axis=0)
        real_out = jnp.dot(stacked.astype(jnp.float32), weights[0].astype(jnp.float32), preferred_element_type=jnp.float32)
        imag_out = jnp.dot(stacked.astype(jnp.float32), weights[1].astype(jnp.float32), preferred_element_type=jnp.float32)
        outputs.append((real_out[:edge_count] - imag_out[edge_count:]).reshape(edge_count, row_count, -1))
        outputs.append((real_out[edge_count:] + imag_out[:edge_count]).reshape(edge_count, row_count, -1))
    return jnp.concatenate(outputs, axis=1)

def so2_transpose(grad_y, w_zero, w_one, w_two):
    edge_count = grad_y.shape[0]
    zero_part = jnp.dot(grad_y[:, 0:5].reshape(edge_count, -1).astype(jnp.float32), w_zero.T.astype(jnp.float32), preferred_element_type=jnp.float32)
    outputs = [zero_part.reshape(edge_count, 5, -1)]
    for first_row, row_count, weights in ((5, 4, w_one), (13, 3, w_two)):
        plus_grad = grad_y[:, first_row:first_row + row_count].reshape(edge_count, -1)
        minus_grad = grad_y[:, first_row + row_count:first_row + 2 * row_count].reshape(edge_count, -1)
        stacked = jnp.concatenate([plus_grad, minus_grad], axis=0)
        real_back = jnp.dot(stacked.astype(jnp.float32), weights[0].T.astype(jnp.float32), preferred_element_type=jnp.float32)
        imag_back = jnp.dot(stacked.astype(jnp.float32), weights[1].T.astype(jnp.float32), preferred_element_type=jnp.float32)
        outputs.append((real_back[:edge_count] + imag_back[edge_count:]).reshape(edge_count, row_count, -1))
        outputs.append((real_back[edge_count:] - imag_back[:edge_count]).reshape(edge_count, row_count, -1))
    return jnp.concatenate(outputs, axis=1)

def edge_grads(src_feats, tgt_feats, cotangent, rotation, w_zero, w_one, w_two):
    matrix = rotation.astype(jnp.float32)

    def rotate(values):
        return jnp.einsum('ekj,ejc->ekc', matrix, values.astype(jnp.float32))

    def unrotate(values):
        return jnp.einsum('ekj,ekc->ejc', matrix, values.astype(jnp.float32))
    edge_in = jnp.concatenate([rotate(src_feats), rotate(tgt_feats)], axis=2).astype(jnp.bfloat16)
    rotated_cot = rotate(cotangent).astype(jnp.bfloat16)
    output = so2_apply(edge_in, w_zero, w_one, w_two)
    scalar = output[:, 0]
    gating = jax.nn.sigmoid(scalar)
    gate_slope = gating * (1.0 - gating)
    higher = rotated_cot[:, 1:].astype(jnp.float32)
    gate_grad = jnp.sum(higher * output[:, 1:], axis=1)
    first_cot = rotated_cot[:, 0].astype(jnp.float32)
    scalar_grad = first_cot * (gating + scalar * gate_slope) + gate_grad * gate_slope
    grad_y = jnp.concatenate([scalar_grad[:, None], gating[:, None] * higher], axis=1).astype(jnp.bfloat16)
    grad_in = so2_transpose(grad_y, w_zero, w_one, w_two).astype(jnp.bfloat16)
    channels = cotangent.shape[2]
    grad_src = unrotate(grad_in[:, :, :channels]).astype(jnp.bfloat16)
    grad_tgt = unrotate(grad_in[:, :, channels:]).astype(jnp.bfloat16)
    return (grad_src, grad_tgt)

def rounded(values):
    narrow = lax.optimization_barrier(values.astype(jnp.bfloat16))
    return narrow.astype(jnp.float32)

def reference(node_feats, grad_out, edge_src, edge_tgt, edge_counts, wigner, w_zero, w_one, w_two):
    grid_feats = node_feats.reshape(ROW_TILES, COL_TILES, A_DEV, COEF, C)
    grid_cot = grad_out.reshape(ROW_TILES, COL_TILES, A_DEV, COEF, C)
    block_size = min(128, E_CAP)
    target_acc = jnp.zeros((ROW_TILES, TGT_TILE, COEF, C), jnp.float32)
    source_acc = jnp.zeros((COL_TILES, SRC_TILE, COEF, C), jnp.float32)

    def tile_step(totals, tile_index):
        target_acc, source_acc = totals
        row_index = tile_index // COL_TILES
        col_index = tile_index % COL_TILES
        tgt_feats_tile = grid_feats[row_index].reshape(TGT_TILE, COEF, C)
        tgt_cot_tile = grid_cot[row_index].reshape(TGT_TILE, COEF, C)
        src_feats_tile = jnp.take(grid_feats, col_index, axis=1).reshape(SRC_TILE, COEF, C)
        valid_count = edge_counts[row_index, col_index]
        block_count = (valid_count + block_size - 1) // block_size
        src_list = edge_src[row_index, col_index]
        tgt_list = edge_tgt[row_index, col_index]
        rot_list = wigner[row_index, col_index]

        def block_step(block_index, partial_value):
            tgt_part, src_part = partial_value
            start_slot = (block_index * block_size).astype(jnp.int32)
            source_rows = lax.dynamic_slice_in_dim(src_list, start_slot, block_size)
            target_rows = lax.dynamic_slice_in_dim(tgt_list, start_slot, block_size)
            rotation = lax.dynamic_slice_in_dim(rot_list, start_slot, block_size, 0).reshape(block_size, 19, 25)
            in_range = start_slot + jnp.arange(block_size, dtype=jnp.int32) < valid_count
            grad_src, grad_tgt = edge_grads(src_feats_tile[source_rows], tgt_feats_tile[target_rows], tgt_cot_tile[target_rows], rotation, w_zero, w_one, w_two)
            tgt_part = tgt_part.at[target_rows].add(jnp.where(in_range[:, None, None], grad_tgt.astype(jnp.float32), 0.0))
            src_part = src_part.at[source_rows].add(jnp.where(in_range[:, None, None], grad_src.astype(jnp.float32), 0.0))
            return (tgt_part, src_part)
        empty_tgt = jnp.zeros((TGT_TILE, COEF, C), jnp.float32)
        empty_src = jnp.zeros((SRC_TILE, COEF, C), jnp.float32)
        tgt_part, src_part = lax.fori_loop(0, block_count, block_step, (empty_tgt, empty_src))
        target_acc = target_acc.at[row_index].add(rounded(tgt_part))
        source_acc = source_acc.at[col_index].add(rounded(src_part))
        return ((target_acc, source_acc), None)
    totals, unused = lax.scan(tile_step, (target_acc, source_acc), jnp.arange(ROW_TILES * COL_TILES, dtype=jnp.int32))
    target_full = totals[0].reshape(ATOMS, COEF, C)
    source_full = totals[1].reshape(COL_TILES, ROW_TILES, A_DEV, COEF, C).transpose(1, 0, 2, 3, 4).reshape(ATOMS, COEF, C)
    return target_full + source_full
```

```python
import jax
import jax.numpy as jnp
from jax import lax
from jax.experimental import pallas as pl
from jax.experimental.pallas import tpu as pltpu
from jax.sharding import PartitionSpec as P

MESH = pl.DeviceIdType.MESH
F32 = jnp.float32
BF16 = jnp.bfloat16

ROWS = 8
COLS = 32
A = 8
E = 512
C = 128
COEF = 25
PAIRS = 13
FRAME = 19
GROUP = 16
BLOCK = 256
TGT = COLS * A
SRC = ROWS * A
VMEM_LIMIT = 58 * 1024 * 1024


def frame_rows(degree):
    rows = [degree]
    if degree >= 1:
        rows += [5 + degree - 1, 9 + degree - 1]
    if degree >= 2:
        rows += [13 + degree - 2, 16 + degree - 2]
    return rows


def degree_cols(degree):
    return list(range(degree * degree, (degree + 1) * (degree + 1)))


def greet():
    row = lax.axis_index("row")
    col = lax.axis_index("col")
    barrier = pltpu.get_barrier_semaphore()
    for step in range(1, COLS):
        pl.semaphore_signal(
            barrier, inc=1, device_id={"col": lax.rem(col + step, COLS)}, device_id_type=MESH
        )
    for step in range(1, ROWS):
        pl.semaphore_signal(
            barrier, inc=1, device_id={"row": lax.rem(row + step, ROWS)}, device_id_type=MESH
        )
    pl.semaphore_wait(barrier, COLS - 1 + ROWS - 1)
    return row, col


def gather_kernel(feats, cots, g_out, s_out, packed, col_send, col_recv, row_send, row_recv, own):
    packed[:, :, 0:C] = feats[...]
    packed[:, :, C : 2 * C] = cots[...]
    row, col = greet()
    copies = []
    for step in range(1, COLS):
        copies.append(
            pltpu.make_async_remote_copy(
                src_ref=packed,
                dst_ref=g_out.at[col],
                send_sem=col_send.at[step],
                recv_sem=col_recv.at[step],
                device_id={"col": lax.rem(col + step, COLS)},
                device_id_type=MESH,
            )
        )
        copies[-1].start()
    for step in range(1, ROWS):
        copies.append(
            pltpu.make_async_remote_copy(
                src_ref=feats,
                dst_ref=s_out.at[row],
                send_sem=row_send.at[step],
                recv_sem=row_recv.at[step],
                device_id={"row": lax.rem(row + step, ROWS)},
                device_id_type=MESH,
            )
        )
        copies[-1].start()
    mine = pltpu.make_async_copy(packed, g_out.at[col], own.at[0])
    also = pltpu.make_async_copy(feats, s_out.at[row], own.at[1])
    mine.start()
    also.start()
    mine.wait()
    also.wait()
    for copy in copies:
        copy.wait()


def gather(feats, cots):
    return pl.pallas_call(
        gather_kernel,
        out_shape=(
            jax.ShapeDtypeStruct((COLS, COEF, A, 2 * C), BF16),
            jax.ShapeDtypeStruct((ROWS, COEF, A, C), BF16),
        ),
        in_specs=[pl.BlockSpec(memory_space=pltpu.VMEM)] * 2,
        out_specs=(pl.BlockSpec(memory_space=pl.ANY),) * 2,
        scratch_shapes=[
            pltpu.VMEM((COEF, A, 2 * C), BF16),
            pltpu.SemaphoreType.DMA((COLS,)),
            pltpu.SemaphoreType.DMA((COLS,)),
            pltpu.SemaphoreType.DMA((ROWS,)),
            pltpu.SemaphoreType.DMA((ROWS,)),
            pltpu.SemaphoreType.DMA((2,)),
        ],
        compiler_params=pltpu.CompilerParams(
            collective_id=0, has_side_effects=True, vmem_limit_bytes=VMEM_LIMIT
        ),
        name="gather_blocks",
    )(feats, cots)


def reduce_kernel(tgt, src, out, tgt_in, src_in, col_send, col_recv, row_send, row_recv, own):
    row, col = greet()
    copies = []
    for step in range(1, COLS):
        there = lax.rem(col + step, COLS)
        copies.append(
            pltpu.make_async_remote_copy(
                src_ref=tgt.at[there],
                dst_ref=tgt_in.at[col],
                send_sem=col_send.at[step],
                recv_sem=col_recv.at[step],
                device_id={"col": there},
                device_id_type=MESH,
            )
        )
        copies[-1].start()
    for step in range(1, ROWS):
        there = lax.rem(row + step, ROWS)
        copies.append(
            pltpu.make_async_remote_copy(
                src_ref=src.at[there],
                dst_ref=src_in.at[row],
                send_sem=row_send.at[step],
                recv_sem=row_recv.at[step],
                device_id={"row": there},
                device_id_type=MESH,
            )
        )
        copies[-1].start()
    mine = pltpu.make_async_copy(tgt.at[col], tgt_in.at[col], own.at[0])
    also = pltpu.make_async_copy(src.at[row], src_in.at[row], own.at[1])
    mine.start()
    also.start()
    mine.wait()
    also.wait()
    for copy in copies:
        copy.wait()

    def add(j, carry):
        total = jnp.sum(tgt_in[:, j].astype(F32), axis=0)
        out[j] = total + jnp.sum(src_in[:, j].astype(F32), axis=0)
        return carry

    lax.fori_loop(0, COEF, add, 0)


def reduce(tgt, src):
    return pl.pallas_call(
        reduce_kernel,
        out_shape=jax.ShapeDtypeStruct((COEF, A, C), F32),
        in_specs=[pl.BlockSpec(memory_space=pl.ANY)] * 2,
        out_specs=pl.BlockSpec(memory_space=pltpu.VMEM),
        scratch_shapes=[
            pltpu.VMEM((COLS, COEF, A, C), BF16),
            pltpu.VMEM((ROWS, COEF, A, C), BF16),
            pltpu.SemaphoreType.DMA((COLS,)),
            pltpu.SemaphoreType.DMA((COLS,)),
            pltpu.SemaphoreType.DMA((ROWS,)),
            pltpu.SemaphoreType.DMA((ROWS,)),
            pltpu.SemaphoreType.DMA((2,)),
        ],
        compiler_params=pltpu.CompilerParams(
            collective_id=1, has_side_effects=True, vmem_limit_bytes=VMEM_LIMIT
        ),
        name="reduce_blocks",
    )(tgt, src)


def dot(x, y):
    return jnp.dot(x, y, preferred_element_type=F32)


def dot_t(x, y):
    return lax.dot_general(x, y, (((1,), (1,)), ((), ())), preferred_element_type=F32)


def edge_kernel(
    count, src_ids, tgt_ids, rot, g, s, w0, w1, w2, tgt_out, src_out,
    full1, full2, hot_t, hot_s, back_t, back_s, xt, xs, frame, cot, y,
):
    for weights, full in ((w1, full1), (w2, full2)):
        k, n = weights.shape[1:]
        full[0:k, 0:n] = weights[0]
        full[0:k, n : 2 * n] = weights[1]
        full[k : 2 * k, 0:n] = -weights[1]
        full[k : 2 * k, n : 2 * n] = weights[0]

    tgt_row = tgt_ids[...]
    src_row = src_ids[...]
    valid = lax.broadcasted_iota(jnp.int32, (1, E), 1) < count[0, 0]
    marked_t = jnp.where(valid, tgt_row, -1)
    marked_s = jnp.where(valid, src_row, -1)
    back_t[...] = (marked_t == lax.broadcasted_iota(jnp.int32, (TGT, E), 0)).astype(F32).astype(BF16)
    back_s[...] = (marked_s == lax.broadcasted_iota(jnp.int32, (SRC, E), 0)).astype(F32).astype(BF16)
    tgt_col = jnp.transpose(jnp.broadcast_to(tgt_row, (C, E)))
    src_col = jnp.transpose(jnp.broadcast_to(src_row, (C, E)))
    lane = lax.broadcasted_iota(jnp.int32, (E, C), 1)
    hot_t[:, 0:C] = (tgt_col == lane).astype(F32).astype(BF16)
    hot_t[:, C : 2 * C] = (tgt_col == lane + C).astype(F32).astype(BF16)
    hot_s[...] = (src_col == lane)[:, 0:SRC].astype(F32).astype(BF16)

    def gather_tgt(j, carry):
        block = g[:, j].astype(F32).reshape(TGT, 2 * C).astype(BF16)
        xt[j] = dot(hot_t[...], block).astype(BF16)
        return carry

    lax.fori_loop(0, COEF, gather_tgt, 0)

    def gather_src(p, carry):
        first = s[:, 2 * p].astype(F32).reshape(SRC, C)
        second = s[:, jnp.minimum(2 * p + 1, COEF - 1)].astype(F32).reshape(SRC, C)
        block = jnp.concatenate([first, second], axis=1).astype(BF16)
        xs[p] = dot(hot_s[...], block).astype(BF16)
        return carry

    lax.fori_loop(0, PAIRS, gather_src, 0)

    def half(j):
        return slice((j % 2) * C, (j % 2) * C + C)

    def rotate(i, carry):
        at = pl.ds(pl.multiple_of(i * GROUP, GROUP), GROUP)
        matrix = rot[at, :].astype(F32)
        for degree in range(5):
            cols = degree_cols(degree)
            from_src = [xs[j // 2, at, half(j)].astype(F32) for j in cols]
            from_tgt = [xt[j, at, 0:C].astype(F32) for j in cols]
            from_cot = [xt[j, at, C : 2 * C].astype(F32) for j in cols]
            for k in frame_rows(degree):
                sums = [None, None, None]
                for n, j in enumerate(cols):
                    entry = k * COEF + j
                    factor = jnp.broadcast_to(matrix[:, entry : entry + 1], (GROUP, C))
                    for which, values in enumerate((from_src, from_tgt, from_cot)):
                        term = factor * values[n]
                        sums[which] = term if sums[which] is None else sums[which] + term
                frame[at, 2 * k * C : (2 * k + 1) * C] = sums[0].astype(BF16)
                frame[at, (2 * k + 1) * C : (2 * k + 2) * C] = sums[1].astype(BF16)
                cot[at, k * C : (k + 1) * C] = sums[2].astype(BF16)
        return carry

    lax.fori_loop(0, E // GROUP, rotate, 0)

    parts = ((0, 5, w0), (5, 8, full1), (13, 6, full2))

    def forward(i, carry):
        at = pl.ds(pl.multiple_of(i * BLOCK, BLOCK), BLOCK)
        for first, rows, weights in parts:
            y[at, first * C : (first + rows) * C] = dot(
                frame[at, 2 * first * C : 2 * (first + rows) * C], weights[...]
            )
        return carry

    lax.fori_loop(0, E // BLOCK, forward, 0)

    def gate(i, carry):
        at = pl.ds(pl.multiple_of(i * GROUP, GROUP), GROUP)
        scalar = y[at, 0:C]
        gating = jax.nn.sigmoid(scalar)
        slope = gating * (1.0 - gating)
        total = jnp.zeros((GROUP, C), F32)
        for k in range(1, FRAME):
            piece = slice(k * C, (k + 1) * C)
            value = cot[at, piece].astype(F32)
            total = total + value * y[at, piece]
            cot[at, piece] = (gating * value).astype(BF16)
        first = cot[at, 0:C].astype(F32)
        cot[at, 0:C] = (first * (gating + scalar * slope) + total * slope).astype(BF16)
        return carry

    lax.fori_loop(0, E // GROUP, gate, 0)

    def backward(i, carry):
        at = pl.ds(pl.multiple_of(i * BLOCK, BLOCK), BLOCK)
        for first, rows, weights in parts:
            frame[at, 2 * first * C : 2 * (first + rows) * C] = dot_t(
                cot[at, first * C : (first + rows) * C], weights[...]
            ).astype(BF16)
        return carry

    lax.fori_loop(0, E // BLOCK, backward, 0)

    def unrotate(i, carry):
        at = pl.ds(pl.multiple_of(i * GROUP, GROUP), GROUP)
        matrix = rot[at, :].astype(F32)
        for degree in range(5):
            rows = frame_rows(degree)
            of_src = [frame[at, 2 * k * C : (2 * k + 1) * C].astype(F32) for k in rows]
            of_tgt = [frame[at, (2 * k + 1) * C : (2 * k + 2) * C].astype(F32) for k in rows]
            for j in degree_cols(degree):
                sums = [None, None]
                for n, k in enumerate(rows):
                    entry = k * COEF + j
                    factor = jnp.broadcast_to(matrix[:, entry : entry + 1], (GROUP, C))
                    for which, values in enumerate((of_src, of_tgt)):
                        term = factor * values[n]
                        sums[which] = term if sums[which] is None else sums[which] + term
                xs[j // 2, at, half(j)] = sums[0].astype(BF16)
                xt[j // 2, at, half(j)] = sums[1].astype(BF16)
        return carry

    lax.fori_loop(0, E // GROUP, unrotate, 0)

    for p in range(PAIRS):
        for back, grads, out, blocks in ((back_t, xt, tgt_out, COLS), (back_s, xs, src_out, ROWS)):
            both = dot(back[...], grads[p])
            for j in (2 * p, 2 * p + 1):
                if j < COEF:
                    out[:, j] = both[:, half(j)].reshape(blocks, A, C).astype(BF16)


def edges(count, src_ids, tgt_ids, rot, g, s, w0, w1, w2):
    vmem = pl.BlockSpec(memory_space=pltpu.VMEM)
    return pl.pallas_call(
        edge_kernel,
        out_shape=(
            jax.ShapeDtypeStruct((COLS, COEF, A, C), BF16),
            jax.ShapeDtypeStruct((ROWS, COEF, A, C), BF16),
        ),
        in_specs=[pl.BlockSpec(memory_space=pltpu.SMEM)] + [vmem] * 8,
        out_specs=(vmem, vmem),
        scratch_shapes=[
            pltpu.VMEM((2 * w1.shape[1], 2 * w1.shape[2]), BF16),
            pltpu.VMEM((2 * w2.shape[1], 2 * w2.shape[2]), BF16),
            pltpu.VMEM((E, TGT), BF16),
            pltpu.VMEM((E, SRC), BF16),
            pltpu.VMEM((TGT, E), BF16),
            pltpu.VMEM((SRC, E), BF16),
            pltpu.VMEM((COEF, E, 2 * C), BF16),
            pltpu.VMEM((PAIRS, E, 2 * C), BF16),
            pltpu.VMEM((E, FRAME * 2 * C), BF16),
            pltpu.VMEM((E, FRAME * C), BF16),
            pltpu.VMEM((E, FRAME * C), F32),
        ],
        compiler_params=pltpu.CompilerParams(vmem_limit_bytes=VMEM_LIMIT),
        cost_estimate=pl.CostEstimate(
            flops=12 * 10**9, bytes_accessed=12 * 10**6, transcendentals=E * C
        ),
        name="edge_gradients",
    )(count, src_ids, tgt_ids, rot, g, s, w0, w1, w2)


def local(node_feats, grad_out, edge_src, edge_tgt, edge_counts, wigner, w_zero, w_one, w_two):
    feats = jnp.transpose(node_feats, (1, 0, 2))
    cots = jnp.transpose(grad_out, (1, 0, 2))
    g, s = gather(feats, cots)
    tgt, src = edges(
        edge_counts, edge_src[0], edge_tgt[0], wigner[0, 0], g, s, w_zero, w_one, w_two
    )
    return jnp.transpose(reduce(tgt, src), (1, 0, 2))


def solution(mesh):
    placed = (
        P(("row", "col"), None, None),
        P(("row", "col"), None, None),
        P("row", "col", None),
        P("row", "col", None),
        P("row", "col"),
        P("row", "col", None, None),
        P(),
        P(),
        P(),
    )
    return jax.shard_map(
        local, mesh=mesh, in_specs=placed, out_specs=P(("row", "col"), None, None), check_vma=False
    )
```

```python
import jax
import jax.numpy as jnp
from jax import lax
from jax.experimental import pallas as pl
from jax.experimental.pallas import tpu as pltpu
from jax.sharding import PartitionSpec as P

MESH = pl.DeviceIdType.MESH
F32 = jnp.float32
BF16 = jnp.bfloat16

ROWS = 8
COLS = 32
A = 8
E = 512
C = 128
COEF = 25
PAIRS = 13
FRAME = 19
GROUP = 16
BLOCK = 256
TGT = COLS * A
SRC = ROWS * A
VMEM_LIMIT = 58 * 1024 * 1024


def frame_rows(degree):
    rows = [degree]
    if degree >= 1:
        rows += [5 + degree - 1, 9 + degree - 1]
    if degree >= 2:
        rows += [13 + degree - 2, 16 + degree - 2]
    return rows


def degree_cols(degree):
    return list(range(degree * degree, (degree + 1) * (degree + 1)))


def ring(value, step):
    return lax.rem(value + step, 4)


class Net:
    def __init__(self, send, recv):
        row = lax.axis_index("row")
        col = lax.axis_index("col")
        self.x = lax.div(col, 8)
        self.z = lax.rem(lax.div(col, 4), 2)
        self.y = lax.rem(col, 4)
        self.high = lax.div(row, 2)
        self.core = lax.rem(row, 2)
        self.send = send
        self.recv = recv
        self.copies = []

    def at(self, x=0, z=0, y=0):
        z_now = 1 - self.z if z else self.z
        return {"col": ring(self.x, x) * 8 + z_now * 4 + ring(self.y, y)}

    def peer(self, high=0, core=0):
        core_now = 1 - self.core if core else self.core
        return {"row": ring(self.high, high) * 2 + core_now}

    def greet(self):
        barrier = pltpu.get_barrier_semaphore()
        devices = [self.at(x=1), self.at(x=3), self.at(y=1), self.at(y=3), self.at(z=1)]
        devices += [self.peer(high=step) for step in (1, 2, 3)] + [self.peer(core=1)]
        for device in devices:
            pl.semaphore_signal(barrier, inc=1, device_id=device, device_id_type=MESH)
        pl.semaphore_wait(barrier, len(devices))

    def push(self, source, target, device):
        n = len(self.copies)
        copy = pltpu.make_async_remote_copy(
            src_ref=source,
            dst_ref=target,
            send_sem=self.send.at[n],
            recv_sem=self.recv.at[n],
            device_id=device,
            device_id_type=MESH,
        )
        copy.start()
        self.copies.append(copy)
        return copy


QUARTERS = ((0, 7), (7, 13), (13, 19), (19, 25))
HALVES = ((0, 13), (13, 25))
MESSAGES = 96


def span(bounds):
    return pl.ds(bounds[0], bounds[1] - bounds[0])


def gather_kernel(feats, cots, g, s, packed, send, recv, own):
    packed[:, :, 0:C] = feats[...]
    packed[:, :, C : 2 * C] = cots[...]
    net = Net(send, recv)
    net.greet()
    received = []

    def arrived(copy):
        copy.wait_recv()
        received.append(copy)

    def place(h, first, second, z, bounds):
        near, far = (second, first) if h == 0 else (first, second)
        z_now = 1 - net.z if z else net.z
        return g.at[ring(net.x, far), z_now, ring(net.y, near), span(bounds)]

    def step_to(h, phase, sign):
        along_y = (h == 0) == (phase == 0)
        return net.at(y=sign) if along_y else net.at(x=sign)

    def own_piece(bounds):
        return packed.at[span(bounds)]

    across = net.push(packed, g.at[net.x, net.z, net.y], net.at(z=1))
    inner = {}
    outer = {}
    for h in (0, 1):
        for sign in (1, 3):
            inner[h, 0, sign] = net.push(
                own_piece(HALVES[h]), place(h, 0, 0, 0, HALVES[h]), step_to(h, 0, sign)
            )
    sibling = [net.push(feats, s.at[net.high, net.core], net.peer(core=1))]
    rows = [net.push(feats, s.at[net.high, net.core], net.peer(high=step)) for step in (1, 3, 2)]
    for h in (0, 1):
        for sign in (1, 3):
            outer[h, 0, 0, sign] = net.push(
                own_piece(HALVES[h]), place(h, 0, 0, 0, HALVES[h]), step_to(h, 1, sign)
            )
    mine = pltpu.make_async_copy(packed, g.at[net.x, net.z, net.y], own.at[0])
    also = pltpu.make_async_copy(feats, s.at[net.high, net.core], own.at[1])
    mine.start()
    also.start()

    def spread(h, near, z):
        block = place(h, 0, near, z, HALVES[h])
        for sign in (1, 3):
            outer[h, z, near, sign] = net.push(block, block, step_to(h, 1, sign))

    arrived(across)
    for h in (0, 1):
        block = place(h, 0, 0, 1, HALVES[h])
        for sign in (1, 3):
            inner[h, 1, sign] = net.push(block, block, step_to(h, 0, sign))
    for h in (0, 1):
        spread(h, 0, 1)
    passed = {}
    for z in (0, 1):
        for sign, quarter in ((1, 0), (3, 1)):
            for h in (0, 1):
                arrived(inner[h, z, sign])
                bounds = QUARTERS[2 * h + quarter]
                block = place(h, 0, 4 - sign, z, bounds)
                passed[h, z, sign] = net.push(block, block, step_to(h, 0, sign))
                spread(h, 4 - sign, z)
    last = []

    def relay(h, z, near):
        for sign, quarter in ((1, 0), (3, 1)):
            arrived(outer[h, z, near, sign])
            block = place(h, 4 - sign, near, z, QUARTERS[2 * h + quarter])
            last.append(net.push(block, block, step_to(h, 1, sign)))

    for z in (0, 1):
        for h in (0, 1):
            relay(h, z, 0)
    for z in (0, 1):
        for h in (0, 1):
            arrived(passed[h, z, 1])
            arrived(passed[h, z, 3])
            spread(h, 2, z)
    for step, copy in zip((1, 3, 2), rows):
        arrived(copy)
        block = s.at[ring(net.high, 4 - step), net.core]
        sibling.append(net.push(block, block, net.peer(core=1)))
    for near in (3, 1, 2):
        for z in (0, 1):
            for h in (0, 1):
                relay(h, z, near)
    for copy in last + sibling:
        arrived(copy)
    mine.wait()
    also.wait()
    for copy in net.copies:
        copy.wait_send()


def gather(feats, cots):
    return pl.pallas_call(
        gather_kernel,
        out_shape=(
            jax.ShapeDtypeStruct((4, 2, 4, COEF, A, 2 * C), BF16),
            jax.ShapeDtypeStruct((4, 2, COEF, A, C), BF16),
        ),
        in_specs=[pl.BlockSpec(memory_space=pltpu.VMEM)] * 2,
        out_specs=(pl.BlockSpec(memory_space=pl.ANY),) * 2,
        scratch_shapes=[
            pltpu.VMEM((COEF, A, 2 * C), BF16),
            pltpu.SemaphoreType.DMA((MESSAGES,)),
            pltpu.SemaphoreType.DMA((MESSAGES,)),
            pltpu.SemaphoreType.DMA((2,)),
        ],
        compiler_params=pltpu.CompilerParams(
            collective_id=0, has_side_effects=True, vmem_limit_bytes=VMEM_LIMIT
        ),
        name="gather_blocks",
    )(feats, cots)


def length(bounds):
    return bounds[1] - bounds[0]


def reduce_kernel(tgt, src, out, *scratch):
    send, recv = scratch[-2:]
    row_in, row_sum, sib_in, z_in, z_out, kept = scratch[:6]
    halves = (scratch[6:18], scratch[18:30])
    net = Net(send, recv)
    net.greet()
    sib = net.push(src.at[:, 1 - net.core], sib_in, net.peer(core=1))

    def toward(h, phase, sign):
        along_x = (h == 0) == (phase == 0)
        return net.at(x=sign) if along_x else net.at(y=sign)

    def block(h, step, piece):
        bounds = QUARTERS[2 * h + piece]
        if h == 0:
            return tgt.at[ring(net.x, step), :, :, span(bounds)]
        return tgt.at[:, :, ring(net.y, step), span(bounds)]

    def tail(h, piece):
        first = QUARTERS[2 * h][0]
        bounds = QUARTERS[2 * h + piece]
        return pl.ds(bounds[0] - first, length(bounds))

    passing = {}
    direct = {}
    for h in (0, 1):
        in_p, in_m, up, um, end_p, end_m = halves[h][:6]
        passing[h, 1] = net.push(block(h, 2, 0), in_p, toward(h, 0, 1))
        passing[h, 3] = net.push(block(h, 2, 1), in_m, toward(h, 0, 3))
    for h in (0, 1):
        in_p, in_m, up, um, end_p, end_m = halves[h][:6]
        direct[h, 1] = net.push(block(h, 1, 1), end_p.at[:, :, tail(h, 1)], toward(h, 0, 1))
        direct[h, 3] = net.push(block(h, 3, 0), end_m.at[:, :, tail(h, 0)], toward(h, 0, 3))

    sib.wait_recv()
    for high in range(4):
        row_sum[high] = (src[high, net.core].astype(F32) + sib_in[high].astype(F32)).astype(BF16)
    rows = [
        net.push(row_sum.at[ring(net.high, step)], row_in.at[net.high], net.peer(high=step))
        for step in (2, 1, 3)
    ]

    joined = {}
    for sign, piece in ((1, 0), (3, 1)):
        for h in (0, 1):
            in_p, in_m, up, um, end_p, end_m = halves[h][:6]
            came, sums, end = (in_p, up, end_p) if sign == 1 else (in_m, um, end_m)
            passing[h, sign].wait_recv()
            mine = block(h, sign, piece)
            for i in range(came.shape[0]):
                for j in range(came.shape[1]):
                    sums[i, j] = (came[i, j].astype(F32) + mine[i, j].astype(F32)).astype(BF16)
            joined[h, sign] = net.push(sums, end.at[:, :, tail(h, piece)], toward(h, 0, sign))

    passing_2 = {}
    direct_2 = {}
    for h in (0, 1):
        in_p, in_m, up, um, end_p, end_m = halves[h][:6]
        total, in2_p, in2_m, up2, um2, ends = halves[h][6:12]
        for sign in (1, 3):
            direct[h, sign].wait_recv()
            joined[h, sign].wait_recv()
        for i in range(end_p.shape[0]):
            for j in range(end_p.shape[1]):
                if h == 0:
                    mine, to = tgt[net.x, i, j, 0:13], total.at[j, i]
                else:
                    mine, to = tgt[i, j, net.y, 13:25], total.at[i, j]
                to[...] = (
                    mine.astype(F32) + end_p[i, j].astype(F32) + end_m[i, j].astype(F32)
                ).astype(BF16)
        here = net.y if h == 0 else net.x
        passing_2[h, 1] = net.push(
            total.at[ring(here, 2), :, tail(h, 0)], in2_p, toward(h, 1, 1)
        )
        passing_2[h, 3] = net.push(
            total.at[ring(here, 2), :, tail(h, 1)], in2_m, toward(h, 1, 3)
        )
        direct_2[h, 1] = net.push(
            total.at[ring(here, 1), :, tail(h, 1)], ends.at[0, :, tail(h, 1)], toward(h, 1, 1)
        )
        direct_2[h, 3] = net.push(
            total.at[ring(here, 3), :, tail(h, 0)], ends.at[1, :, tail(h, 0)], toward(h, 1, 3)
        )
    joined_2 = {}
    for h in (0, 1):
        total, in2_p, in2_m, up2, um2, ends = halves[h][6:12]
        here = net.y if h == 0 else net.x
        for n, (sign, piece, came, sums) in enumerate(((1, 0, in2_p, up2), (3, 1, in2_m, um2))):
            passing_2[h, sign].wait_recv()
            for i in range(2):
                mine = total[ring(here, sign), i, tail(h, piece)]
                sums[i] = (came[i].astype(F32) + mine.astype(F32)).astype(BF16)
            joined_2[h, sign] = net.push(sums, ends.at[n, :, tail(h, piece)], toward(h, 1, sign))
    for copy in rows:
        copy.wait_recv()
    across = []
    for h in (0, 1):
        total, in2_p, in2_m, up2, um2, ends = halves[h][6:12]
        here = net.y if h == 0 else net.x
        for sign in (1, 3):
            direct_2[h, sign].wait_recv()
            joined_2[h, sign].wait_recv()
        at = span(HALVES[h])
        for z_now, to in ((1 - net.z, z_out), (net.z, kept)):
            value = total[here, z_now].astype(F32) + ends[0, z_now].astype(F32)
            value = value + ends[1, z_now].astype(F32)
            to[at] = value.astype(to.dtype)
        across.append(net.push(z_out.at[at], z_in.at[at], net.at(z=1)))
    value = kept[...] + row_sum[net.high].astype(F32)
    for step in (1, 2, 3):
        value = value + row_in[ring(net.high, step)].astype(F32)
    kept[...] = value
    for copy in across:
        copy.wait_recv()
    out[...] = kept[...] + z_in[...].astype(F32)
    for copy in net.copies:
        copy.wait_send()


def reduce(tgt, src):
    def buffer(*lead):
        return pltpu.VMEM(lead + (A, C), BF16)

    scratch = [
        buffer(4, COEF),
        buffer(4, COEF),
        buffer(4, COEF),
        buffer(COEF),
        buffer(COEF),
        pltpu.VMEM((COEF, A, C), F32),
    ]
    for h, lead in ((0, (2, 4)), (1, (4, 2))):
        whole = length(HALVES[h])
        plus, minus = length(QUARTERS[2 * h]), length(QUARTERS[2 * h + 1])
        scratch += [
            buffer(*lead, plus),
            buffer(*lead, minus),
            buffer(*lead, plus),
            buffer(*lead, minus),
            buffer(*lead, whole),
            buffer(*lead, whole),
            buffer(4, 2, whole),
            buffer(2, plus),
            buffer(2, minus),
            buffer(2, plus),
            buffer(2, minus),
            buffer(2, 2, whole),
        ]
    return pl.pallas_call(
        reduce_kernel,
        out_shape=jax.ShapeDtypeStruct((COEF, A, C), F32),
        in_specs=[pl.BlockSpec(memory_space=pltpu.VMEM)] * 2,
        out_specs=pl.BlockSpec(memory_space=pltpu.VMEM),
        scratch_shapes=scratch
        + [pltpu.SemaphoreType.DMA((MESSAGES,)), pltpu.SemaphoreType.DMA((MESSAGES,))],
        compiler_params=pltpu.CompilerParams(
            collective_id=1, has_side_effects=True, vmem_limit_bytes=VMEM_LIMIT
        ),
        name="reduce_blocks",
    )(tgt.reshape(4, 2, 4, COEF, A, C), src.reshape(4, 2, COEF, A, C))


def dot(x, y):
    return jnp.dot(x, y, preferred_element_type=F32)


def dot_t(x, y):
    return lax.dot_general(x, y, (((1,), (1,)), ((), ())), preferred_element_type=F32)


def edge_kernel(
    count, src_ids, tgt_ids, rot, g, s, w0, w1, w2, tgt_out, src_out,
    full1, full2, hot_t, hot_s, back_t, back_s, xt, xs, frame, cot, y,
):
    for weights, full in ((w1, full1), (w2, full2)):
        k, n = weights.shape[1:]
        full[0:k, 0:n] = weights[0]
        full[0:k, n : 2 * n] = weights[1]
        full[k : 2 * k, 0:n] = -weights[1]
        full[k : 2 * k, n : 2 * n] = weights[0]

    tgt_row = tgt_ids[...]
    src_row = src_ids[...]
    valid = lax.broadcasted_iota(jnp.int32, (1, E), 1) < count[0, 0]
    marked_t = jnp.where(valid, tgt_row, -1)
    marked_s = jnp.where(valid, src_row, -1)
    back_t[...] = (marked_t == lax.broadcasted_iota(jnp.int32, (TGT, E), 0)).astype(F32).astype(BF16)
    back_s[...] = (marked_s == lax.broadcasted_iota(jnp.int32, (SRC, E), 0)).astype(F32).astype(BF16)
    tgt_col = jnp.transpose(jnp.broadcast_to(tgt_row, (C, E)))
    src_col = jnp.transpose(jnp.broadcast_to(src_row, (C, E)))
    lane = lax.broadcasted_iota(jnp.int32, (E, C), 1)
    hot_t[:, 0:C] = (tgt_col == lane).astype(F32).astype(BF16)
    hot_t[:, C : 2 * C] = (tgt_col == lane + C).astype(F32).astype(BF16)
    hot_s[...] = (src_col == lane)[:, 0:SRC].astype(F32).astype(BF16)

    def gather_tgt(j, carry):
        block = g[:, j].astype(F32).reshape(TGT, 2 * C).astype(BF16)
        xt[j] = dot(hot_t[...], block).astype(BF16)
        return carry

    lax.fori_loop(0, COEF, gather_tgt, 0)

    def gather_src(p, carry):
        first = s[:, 2 * p].astype(F32).reshape(SRC, C)
        second = s[:, jnp.minimum(2 * p + 1, COEF - 1)].astype(F32).reshape(SRC, C)
        block = jnp.concatenate([first, second], axis=1).astype(BF16)
        xs[p] = dot(hot_s[...], block).astype(BF16)
        return carry

    lax.fori_loop(0, PAIRS, gather_src, 0)

    def half(j):
        return slice((j % 2) * C, (j % 2) * C + C)

    def rotate(i, carry):
        at = pl.ds(pl.multiple_of(i * GROUP, GROUP), GROUP)
        matrix = rot[at, :].astype(F32)
        for degree in range(5):
            cols = degree_cols(degree)
            from_src = [xs[j // 2, at, half(j)].astype(F32) for j in cols]
            from_tgt = [xt[j, at, 0:C].astype(F32) for j in cols]
            from_cot = [xt[j, at, C : 2 * C].astype(F32) for j in cols]
            for k in frame_rows(degree):
                sums = [None, None, None]
                for n, j in enumerate(cols):
                    entry = k * COEF + j
                    factor = jnp.broadcast_to(matrix[:, entry : entry + 1], (GROUP, C))
                    for which, values in enumerate((from_src, from_tgt, from_cot)):
                        term = factor * values[n]
                        sums[which] = term if sums[which] is None else sums[which] + term
                frame[at, 2 * k * C : (2 * k + 1) * C] = sums[0].astype(BF16)
                frame[at, (2 * k + 1) * C : (2 * k + 2) * C] = sums[1].astype(BF16)
                cot[at, k * C : (k + 1) * C] = sums[2].astype(BF16)
        return carry

    lax.fori_loop(0, E // GROUP, rotate, 0)

    parts = ((0, 5, w0), (5, 8, full1), (13, 6, full2))

    def forward(i, carry):
        at = pl.ds(pl.multiple_of(i * BLOCK, BLOCK), BLOCK)
        for first, rows, weights in parts:
            y[at, first * C : (first + rows) * C] = dot(
                frame[at, 2 * first * C : 2 * (first + rows) * C], weights[...]
            )
        return carry

    lax.fori_loop(0, E // BLOCK, forward, 0)

    def gate(i, carry):
        at = pl.ds(pl.multiple_of(i * GROUP, GROUP), GROUP)
        scalar = y[at, 0:C]
        gating = jax.nn.sigmoid(scalar)
        slope = gating * (1.0 - gating)
        total = jnp.zeros((GROUP, C), F32)
        for k in range(1, FRAME):
            piece = slice(k * C, (k + 1) * C)
            value = cot[at, piece].astype(F32)
            total = total + value * y[at, piece]
            cot[at, piece] = (gating * value).astype(BF16)
        first = cot[at, 0:C].astype(F32)
        cot[at, 0:C] = (first * (gating + scalar * slope) + total * slope).astype(BF16)
        return carry

    lax.fori_loop(0, E // GROUP, gate, 0)

    def backward(i, carry):
        at = pl.ds(pl.multiple_of(i * BLOCK, BLOCK), BLOCK)
        for first, rows, weights in parts:
            frame[at, 2 * first * C : 2 * (first + rows) * C] = dot_t(
                cot[at, first * C : (first + rows) * C], weights[...]
            ).astype(BF16)
        return carry

    lax.fori_loop(0, E // BLOCK, backward, 0)

    def unrotate(i, carry):
        at = pl.ds(pl.multiple_of(i * GROUP, GROUP), GROUP)
        matrix = rot[at, :].astype(F32)
        for degree in range(5):
            rows = frame_rows(degree)
            of_src = [frame[at, 2 * k * C : (2 * k + 1) * C].astype(F32) for k in rows]
            of_tgt = [frame[at, (2 * k + 1) * C : (2 * k + 2) * C].astype(F32) for k in rows]
            for j in degree_cols(degree):
                sums = [None, None]
                for n, k in enumerate(rows):
                    entry = k * COEF + j
                    factor = jnp.broadcast_to(matrix[:, entry : entry + 1], (GROUP, C))
                    for which, values in enumerate((of_src, of_tgt)):
                        term = factor * values[n]
                        sums[which] = term if sums[which] is None else sums[which] + term
                xs[j // 2, at, half(j)] = sums[0].astype(BF16)
                xt[j // 2, at, half(j)] = sums[1].astype(BF16)
        return carry

    lax.fori_loop(0, E // GROUP, unrotate, 0)

    for p in range(PAIRS):
        for back, grads, out, blocks in ((back_t, xt, tgt_out, COLS), (back_s, xs, src_out, ROWS)):
            both = dot(back[...], grads[p])
            for j in (2 * p, 2 * p + 1):
                if j < COEF:
                    out[:, j] = both[:, half(j)].reshape(blocks, A, C).astype(BF16)


def edges(count, src_ids, tgt_ids, rot, g, s, w0, w1, w2):
    vmem = pl.BlockSpec(memory_space=pltpu.VMEM)
    return pl.pallas_call(
        edge_kernel,
        out_shape=(
            jax.ShapeDtypeStruct((COLS, COEF, A, C), BF16),
            jax.ShapeDtypeStruct((ROWS, COEF, A, C), BF16),
        ),
        in_specs=[pl.BlockSpec(memory_space=pltpu.SMEM)] + [vmem] * 8,
        out_specs=(vmem, vmem),
        scratch_shapes=[
            pltpu.VMEM((2 * w1.shape[1], 2 * w1.shape[2]), BF16),
            pltpu.VMEM((2 * w2.shape[1], 2 * w2.shape[2]), BF16),
            pltpu.VMEM((E, TGT), BF16),
            pltpu.VMEM((E, SRC), BF16),
            pltpu.VMEM((TGT, E), BF16),
            pltpu.VMEM((SRC, E), BF16),
            pltpu.VMEM((COEF, E, 2 * C), BF16),
            pltpu.VMEM((PAIRS, E, 2 * C), BF16),
            pltpu.VMEM((E, FRAME * 2 * C), BF16),
            pltpu.VMEM((E, FRAME * C), BF16),
            pltpu.VMEM((E, FRAME * C), F32),
        ],
        compiler_params=pltpu.CompilerParams(vmem_limit_bytes=VMEM_LIMIT),
        cost_estimate=pl.CostEstimate(
            flops=12 * 10**9, bytes_accessed=12 * 10**6, transcendentals=E * C
        ),
        name="edge_gradients",
    )(count, src_ids, tgt_ids, rot, g, s, w0, w1, w2)


def local(node_feats, grad_out, edge_src, edge_tgt, edge_counts, wigner, w_zero, w_one, w_two):
    feats = jnp.transpose(node_feats, (1, 0, 2))
    cots = jnp.transpose(grad_out, (1, 0, 2))
    g, s = gather(feats, cots)
    g = g.reshape(COLS, COEF, A, 2 * C)
    s = s.reshape(ROWS, COEF, A, C)
    tgt, src = edges(
        edge_counts, edge_src[0], edge_tgt[0], wigner[0, 0], g, s, w_zero, w_one, w_two
    )
    return jnp.transpose(reduce(tgt, src), (1, 0, 2))


def solution(mesh):
    placed = (
        P(("row", "col"), None, None),
        P(("row", "col"), None, None),
        P("row", "col", None),
        P("row", "col", None),
        P("row", "col"),
        P("row", "col", None, None),
        P(),
        P(),
        P(),
    )
    return jax.shard_map(
        local, mesh=mesh, in_specs=placed, out_specs=P(("row", "col"), None, None), check_vma=False
    )
```

```python
import jax
import jax.numpy as jnp
from jax import lax
from jax.experimental import pallas as pl
from jax.experimental.pallas import tpu as pltpu
from jax.sharding import PartitionSpec as P

MESH = pl.DeviceIdType.MESH
F32 = jnp.float32
BF16 = jnp.bfloat16

ROWS = 8
COLS = 32
A = 8
E = 512
C = 128
COEF = 25
PAIRS = 13
FRAME = 19
GROUP = 16
BLOCK = 256
TGT = COLS * A
SRC = ROWS * A
VMEM_LIMIT = 58 * 1024 * 1024


def frame_rows(degree):
    rows = [degree]
    if degree >= 1:
        rows += [5 + degree - 1, 9 + degree - 1]
    if degree >= 2:
        rows += [13 + degree - 2, 16 + degree - 2]
    return rows


def degree_cols(degree):
    return list(range(degree * degree, (degree + 1) * (degree + 1)))


def ring(value, step):
    return lax.rem(value + step, 4)


class Net:
    def __init__(self, send, recv):
        row = lax.axis_index("row")
        col = lax.axis_index("col")
        self.x = lax.div(col, 8)
        self.z = lax.rem(lax.div(col, 4), 2)
        self.y = lax.rem(col, 4)
        self.high = lax.div(row, 2)
        self.core = lax.rem(row, 2)
        self.send = send
        self.recv = recv
        self.copies = []

    def at(self, x=0, z=0, y=0):
        z_now = 1 - self.z if z else self.z
        return {"col": ring(self.x, x) * 8 + z_now * 4 + ring(self.y, y)}

    def peer(self, high=0, core=0):
        core_now = 1 - self.core if core else self.core
        return {"row": ring(self.high, high) * 2 + core_now}

    def greet(self):
        barrier = pltpu.get_barrier_semaphore()
        devices = [self.at(x=1), self.at(x=3), self.at(y=1), self.at(y=3), self.at(z=1)]
        devices += [self.peer(high=step) for step in (1, 2, 3)] + [self.peer(core=1)]
        for device in devices:
            pl.semaphore_signal(barrier, inc=1, device_id=device, device_id_type=MESH)
        pl.semaphore_wait(barrier, len(devices))

    def push(self, source, target, device):
        n = len(self.copies)
        copy = pltpu.make_async_remote_copy(
            src_ref=source,
            dst_ref=target,
            send_sem=self.send.at[n],
            recv_sem=self.recv.at[n],
            device_id=device,
            device_id_type=MESH,
        )
        copy.start()
        self.copies.append(copy)
        return copy


QUARTERS = ((0, 7), (7, 13), (13, 19), (19, 25))
HALVES = ((0, 13), (13, 25))
MESSAGES = 160


def span(bounds):
    return pl.ds(bounds[0], bounds[1] - bounds[0])


def length(bounds):
    return bounds[1] - bounds[0]


def reduce_body(net, sib, tgt, src, out, scratch):
    row_in, row_sum, sib_in, z_in, z_out, kept = scratch[:6]
    halves = (scratch[6:18], scratch[18:30])

    def toward(h, phase, sign):
        along_x = (h == 0) == (phase == 0)
        return net.at(x=sign) if along_x else net.at(y=sign)

    def block(h, step, piece):
        bounds = QUARTERS[2 * h + piece]
        if h == 0:
            return tgt.at[ring(net.x, step), :, :, span(bounds)]
        return tgt.at[:, :, ring(net.y, step), span(bounds)]

    def tail(h, piece):
        first = QUARTERS[2 * h][0]
        bounds = QUARTERS[2 * h + piece]
        return pl.ds(bounds[0] - first, length(bounds))

    passing = {}
    direct = {}
    for h in (0, 1):
        in_p, in_m, up, um, end_p, end_m = halves[h][:6]
        passing[h, 1] = net.push(block(h, 2, 0), in_p, toward(h, 0, 1))
        passing[h, 3] = net.push(block(h, 2, 1), in_m, toward(h, 0, 3))
    for h in (0, 1):
        in_p, in_m, up, um, end_p, end_m = halves[h][:6]
        direct[h, 1] = net.push(block(h, 1, 1), end_p.at[:, :, tail(h, 1)], toward(h, 0, 1))
        direct[h, 3] = net.push(block(h, 3, 0), end_m.at[:, :, tail(h, 0)], toward(h, 0, 3))

    sib.wait_recv()
    for high in range(4):
        row_sum[high] = (src[high, net.core].astype(F32) + sib_in[high].astype(F32)).astype(BF16)
    rows = [
        net.push(row_sum.at[ring(net.high, step)], row_in.at[net.high], net.peer(high=step))
        for step in (2, 1, 3)
    ]

    joined = {}
    for sign, piece in ((1, 0), (3, 1)):
        for h in (0, 1):
            in_p, in_m, up, um, end_p, end_m = halves[h][:6]
            came, sums, end = (in_p, up, end_p) if sign == 1 else (in_m, um, end_m)
            passing[h, sign].wait_recv()
            mine = block(h, sign, piece)
            for i in range(came.shape[0]):
                for j in range(came.shape[1]):
                    sums[i, j] = (came[i, j].astype(F32) + mine[i, j].astype(F32)).astype(BF16)
            joined[h, sign] = net.push(sums, end.at[:, :, tail(h, piece)], toward(h, 0, sign))

    passing_2 = {}
    direct_2 = {}
    for h in (0, 1):
        in_p, in_m, up, um, end_p, end_m = halves[h][:6]
        total, in2_p, in2_m, up2, um2, ends = halves[h][6:12]
        for sign in (1, 3):
            direct[h, sign].wait_recv()
            joined[h, sign].wait_recv()
        for i in range(end_p.shape[0]):
            for j in range(end_p.shape[1]):
                if h == 0:
                    mine, to = tgt[net.x, i, j, 0:13], total.at[j, i]
                else:
                    mine, to = tgt[i, j, net.y, 13:25], total.at[i, j]
                to[...] = (
                    mine.astype(F32) + end_p[i, j].astype(F32) + end_m[i, j].astype(F32)
                ).astype(BF16)
        here = net.y if h == 0 else net.x
        passing_2[h, 1] = net.push(
            total.at[ring(here, 2), :, tail(h, 0)], in2_p, toward(h, 1, 1)
        )
        passing_2[h, 3] = net.push(
            total.at[ring(here, 2), :, tail(h, 1)], in2_m, toward(h, 1, 3)
        )
        direct_2[h, 1] = net.push(
            total.at[ring(here, 1), :, tail(h, 1)], ends.at[0, :, tail(h, 1)], toward(h, 1, 1)
        )
        direct_2[h, 3] = net.push(
            total.at[ring(here, 3), :, tail(h, 0)], ends.at[1, :, tail(h, 0)], toward(h, 1, 3)
        )
    joined_2 = {}
    for h in (0, 1):
        total, in2_p, in2_m, up2, um2, ends = halves[h][6:12]
        here = net.y if h == 0 else net.x
        for n, (sign, piece, came, sums) in enumerate(((1, 0, in2_p, up2), (3, 1, in2_m, um2))):
            passing_2[h, sign].wait_recv()
            for i in range(2):
                mine = total[ring(here, sign), i, tail(h, piece)]
                sums[i] = (came[i].astype(F32) + mine.astype(F32)).astype(BF16)
            joined_2[h, sign] = net.push(sums, ends.at[n, :, tail(h, piece)], toward(h, 1, sign))
    for copy in rows:
        copy.wait_recv()
    across = []
    for h in (0, 1):
        total, in2_p, in2_m, up2, um2, ends = halves[h][6:12]
        here = net.y if h == 0 else net.x
        for sign in (1, 3):
            direct_2[h, sign].wait_recv()
            joined_2[h, sign].wait_recv()
        at = span(HALVES[h])
        for z_now, to in ((1 - net.z, z_out), (net.z, kept)):
            value = total[here, z_now].astype(F32) + ends[0, z_now].astype(F32)
            value = value + ends[1, z_now].astype(F32)
            to[at] = value.astype(to.dtype)
        across.append(net.push(z_out.at[at], z_in.at[at], net.at(z=1)))
    value = kept[...] + row_sum[net.high].astype(F32)
    for step in (1, 2, 3):
        value = value + row_in[ring(net.high, step)].astype(F32)
    kept[...] = value
    for copy in across:
        copy.wait_recv()
    out[...] = kept[...] + z_in[...].astype(F32)


class Flow:
    def __init__(self, net, own, full):
        self.net = net
        self.own = own
        self.full = full
        self.inner = {}
        self.outer = {}
        self.passed = {}
        self.last = []

    def place(self, h, outer, inner, z, bounds):
        net = self.net
        near, far = (inner, outer) if h == 0 else (outer, inner)
        z_now = (net.z, 1 - net.z, slice(0, 2))[z]
        return self.full.at[ring(net.x, far), z_now, ring(net.y, near), span(bounds)]

    def step_to(self, h, phase, sign):
        along_y = (h == 0) == (phase == 0)
        return self.net.at(y=sign) if along_y else self.net.at(x=sign)

    def spread(self, h, inner, z):
        block = self.place(h, 0, inner, z, HALVES[h])
        source = self.own.at[span(HALVES[h])] if (inner, z) == (0, 0) else block
        for sign in (1, 3):
            self.outer[h, z, inner, sign] = self.net.push(source, block, self.step_to(h, 1, sign))

    def relay(self, h, z, inner):
        for sign, quarter in ((1, 0), (3, 1)):
            self.outer[h, z, inner, sign].wait_recv()
            block = self.place(h, 4 - sign, inner, z, QUARTERS[2 * h + quarter])
            self.last.append(self.net.push(block, block, self.step_to(h, 1, sign)))

    def send_own(self):
        net = self.net
        self.across = net.push(self.own, self.full.at[net.x, net.z, net.y], net.at(z=1))
        for h in (0, 1):
            for sign in (1, 3):
                self.inner[h, 0, sign] = net.push(
                    self.own.at[span(HALVES[h])],
                    self.place(h, 0, 0, 0, HALVES[h]),
                    self.step_to(h, 0, sign),
                )
        for h in (0, 1):
            self.spread(h, 0, 0)

    def send_partner(self):
        self.across.wait_recv()
        for h in (0, 1):
            block = self.place(h, 0, 0, 1, HALVES[h])
            for sign in (1, 3):
                self.inner[h, 1, sign] = self.net.push(block, block, self.step_to(h, 0, sign))
        for h in (0, 1):
            self.spread(h, 0, 1)

    def pass_on(self):
        for sign, quarter in ((1, 0), (3, 1)):
            for h in (0, 1):
                self.inner[h, 0, sign].wait_recv()
                self.inner[h, 1, sign].wait_recv()
                block = self.place(h, 0, 4 - sign, 2, QUARTERS[2 * h + quarter])
                self.passed[h, sign] = self.net.push(block, block, self.step_to(h, 0, sign))
                self.spread(h, 4 - sign, 2)

    def relay_first(self):
        for z in (0, 1):
            for h in (0, 1):
                self.relay(h, z, 0)

    def spread_far(self):
        for h in (0, 1):
            self.passed[h, 1].wait_recv()
            self.passed[h, 3].wait_recv()
            self.spread(h, 2, 2)

    def relay_rest(self, inner):
        for h in (0, 1):
            self.relay(h, 2, inner)

    def finish(self):
        for copy in self.last:
            copy.wait_recv()


def dot(x, y):
    return jnp.dot(x, y, preferred_element_type=F32)


def dot_t(x, y):
    return lax.dot_general(x, y, (((1,), (1,)), ((), ())), preferred_element_type=F32)


def half(j):
    return slice((j % 2) * C, (j % 2) * C + C)


def hot(ids, size, axis):
    return (ids == lax.broadcasted_iota(jnp.int32, size, axis)).astype(F32).astype(BF16)


def fused_kernel(
    count, src_ids, tgt_ids, rot, feats, cots, w0, w1, w2, out,
    gf, gc, gs, w0_in, full1, full2, turn, hot_t, hot_s, back_t, back_s,
    xf, xc, xs, frame, grad_y, y, tgt_sum, src_sum, local_sem, send, recv, *reduce_scratch,
):
    net = Net(send, recv)
    loads = [pltpu.make_async_copy(w0, w0_in, local_sem.at[0])]
    for n, (weights, full) in enumerate(((w1, full1), (w2, full2))):
        k, m = weights.shape[1:]
        for i in range(2):
            for j in range(2):
                loads.append(
                    pltpu.make_async_copy(
                        weights.at[(i + j) % 2],
                        full.at[pl.ds(i * k, k), pl.ds(j * m, m)],
                        local_sem.at[1 + 4 * n + 2 * i + j],
                    )
                )
    mine = [
        pltpu.make_async_copy(feats, gf.at[net.x, net.z, net.y], local_sem.at[9]),
        pltpu.make_async_copy(cots, gc.at[net.x, net.z, net.y], local_sem.at[10]),
        pltpu.make_async_copy(feats, gs.at[net.high, net.core], local_sem.at[11]),
    ]
    for copy in mine + loads:
        copy.start()
    net.greet()

    first = Flow(net, feats, gf)
    second = Flow(net, cots, gc)
    first.send_own()
    sibling = [net.push(feats, gs.at[net.high, net.core], net.peer(core=1))]
    rows = [net.push(feats, gs.at[net.high, net.core], net.peer(high=step)) for step in (1, 3, 2)]

    tgt_row = tgt_ids[...]
    src_row = src_ids[...]
    tgt_col = jnp.transpose(jnp.broadcast_to(tgt_row, (C, E)))
    src_col = jnp.transpose(jnp.broadcast_to(src_row, (C, E)))
    hot_t[:, 0:C] = hot(tgt_col, (E, C), 1)
    hot_t[:, C : 2 * C] = hot(tgt_col - C, (E, C), 1)
    hot_s[...] = hot(src_col, (E, C), 1)[:, 0:SRC]
    first.send_partner()
    valid = lax.broadcasted_iota(jnp.int32, (1, E), 1) < count[0, 0]
    back_t[...] = hot(jnp.where(valid, tgt_row, -1), (TGT, E), 0)
    back_s[...] = hot(jnp.where(valid, src_row, -1), (SRC, E), 0)
    first.pass_on()
    identity = hot(lax.broadcasted_iota(jnp.int32, (E, E), 0), (E, E), 1)
    turn[...] = dot_t(identity, rot[...])
    first.relay_first()
    first.spread_far()
    for step, copy in zip((1, 3, 2), rows):
        copy.wait_recv()
        block = gs.at[ring(net.high, 4 - step), net.core]
        sibling.append(net.push(block, block, net.peer(core=1)))
    second.send_own()
    first.relay_rest(3)
    first.relay_rest(1)
    first.relay_rest(2)
    second.send_partner()
    for copy in mine + loads:
        copy.wait()
    for weights, full in ((w1, full1), (w2, full2)):
        k, m = weights.shape[1:]
        full[k : 2 * k, 0:m] = -full[k : 2 * k, 0:m]
    for copy in sibling:
        copy.wait_recv()

    def pair_of(full, p, rows):
        both = []
        for j in (2 * p, jnp.minimum(2 * p + 1, COEF - 1)):
            piece = full[:, :, :, j] if full.ndim == 6 else full[:, :, j]
            both.append(piece.astype(F32).reshape(rows, C))
        return jnp.concatenate(both, axis=1).astype(BF16)

    def gather_some(items, start, stop):
        def body(p, carry):
            for marks, full, rows, to in items:
                to[p] = dot(marks[...], pair_of(full, p, rows)).astype(BF16)
            return carry

        lax.fori_loop(start, stop, body, 0)

    gather_some(((hot_s, gs, SRC, xs),), 0, PAIRS)
    second.pass_on()
    first.finish()
    second.relay_first()
    gather_some(((hot_t, gf, TGT, xf),), 0, PAIRS)
    second.spread_far()

    def factor_of(matrix, entry):
        return jnp.broadcast_to(matrix[:, entry : entry + 1], (GROUP, C))

    def rotate(i, carry):
        at = pl.ds(pl.multiple_of(i * GROUP, GROUP), GROUP)
        matrix = turn[at, :]
        for degree in range(5):
            cols = degree_cols(degree)
            from_src = [xs[j // 2, at, half(j)].astype(F32) for j in cols]
            from_tgt = [xf[j // 2, at, half(j)].astype(F32) for j in cols]
            for k in frame_rows(degree):
                sums = [None, None]
                for n, j in enumerate(cols):
                    factor = factor_of(matrix, k * COEF + j)
                    for which, values in enumerate((from_src, from_tgt)):
                        term = factor * values[n]
                        sums[which] = term if sums[which] is None else sums[which] + term
                frame[at, 2 * k * C : (2 * k + 1) * C] = sums[0].astype(BF16)
                frame[at, (2 * k + 1) * C : (2 * k + 2) * C] = sums[1].astype(BF16)
        return carry

    steps = E // GROUP
    lax.fori_loop(0, steps // 4, rotate, 0)
    second.relay_rest(3)
    second.relay_rest(1)
    lax.fori_loop(steps // 4, steps // 2, rotate, 0)
    second.relay_rest(2)
    lax.fori_loop(steps // 2, steps, rotate, 0)

    parts = ((0, 5, w0_in), (5, 8, full1), (13, 6, full2))

    def forward(i, carry):
        at = pl.ds(pl.multiple_of(i * BLOCK, BLOCK), BLOCK)
        for begin, rows, weights in parts:
            y[at, begin * C : (begin + rows) * C] = dot(
                frame[at, 2 * begin * C : 2 * (begin + rows) * C], weights[...]
            )
        return carry

    lax.fori_loop(0, E // BLOCK, forward, 0)
    second.finish()
    gather_some(((hot_t, gc, TGT, xc),), 0, PAIRS)

    def gate(i, carry):
        at = pl.ds(pl.multiple_of(i * GROUP, GROUP), GROUP)
        matrix = turn[at, :]
        scalar = y[at, 0:C]
        gating = jax.nn.sigmoid(scalar)
        slope = gating * (1.0 - gating)
        total = jnp.zeros((GROUP, C), F32)
        lowest = None
        for degree in range(5):
            cols = degree_cols(degree)
            values = [xc[j // 2, at, half(j)].astype(F32) for j in cols]
            for k in frame_rows(degree):
                value = None
                for n, j in enumerate(cols):
                    term = factor_of(matrix, k * COEF + j) * values[n]
                    value = term if value is None else value + term
                if k == 0:
                    lowest = value
                else:
                    total = total + value * y[at, k * C : (k + 1) * C]
                    grad_y[at, k * C : (k + 1) * C] = (gating * value).astype(BF16)
        grad_y[at, 0:C] = (lowest * (gating + scalar * slope) + total * slope).astype(BF16)
        return carry

    lax.fori_loop(0, steps, gate, 0)

    def backward(i, carry):
        at = pl.ds(pl.multiple_of(i * BLOCK, BLOCK), BLOCK)
        for begin, rows, weights in parts:
            frame[at, 2 * begin * C : 2 * (begin + rows) * C] = dot_t(
                grad_y[at, begin * C : (begin + rows) * C], weights[...]
            ).astype(BF16)
        return carry

    lax.fori_loop(0, E // BLOCK, backward, 0)

    def unrotate(i, carry):
        at = pl.ds(pl.multiple_of(i * GROUP, GROUP), GROUP)
        matrix = turn[at, :]
        for degree in range(5):
            rows = frame_rows(degree)
            of_src = [frame[at, 2 * k * C : (2 * k + 1) * C].astype(F32) for k in rows]
            of_tgt = [frame[at, (2 * k + 1) * C : (2 * k + 2) * C].astype(F32) for k in rows]
            for j in degree_cols(degree):
                sums = [None, None]
                for n, k in enumerate(rows):
                    factor = factor_of(matrix, k * COEF + j)
                    for which, values in enumerate((of_src, of_tgt)):
                        term = factor * values[n]
                        sums[which] = term if sums[which] is None else sums[which] + term
                xs[j // 2, at, half(j)] = sums[0].astype(BF16)
                xf[j // 2, at, half(j)] = sums[1].astype(BF16)
        return carry

    lax.fori_loop(0, steps, unrotate, 0)

    def scatter(marks, grads, to, lead):
        for p in range(PAIRS):
            both = dot(marks[...], grads[p])
            for j in (2 * p, 2 * p + 1):
                if j < COEF:
                    value = both[:, half(j)].reshape(lead + (A, C)).astype(BF16)
                    if len(lead) == 3:
                        to[:, :, :, j] = value
                    else:
                        to[:, :, j] = value

    scatter(back_s, xs, src_sum, (4, 2))
    sib = net.push(src_sum.at[:, 1 - net.core], reduce_scratch[2], net.peer(core=1))
    scatter(back_t, xf, tgt_sum, (4, 2, 4))
    reduce_body(net, sib, tgt_sum, src_sum, out, reduce_scratch)
    for copy in net.copies:
        copy.wait_send()


def fused(count, src_ids, tgt_ids, rot, feats, cots, w0, w1, w2):
    def buffer(*lead):
        return pltpu.VMEM(lead + (A, C), BF16)

    scratch = [
        buffer(4, 2, 4, COEF),
        buffer(4, 2, 4, COEF),
        buffer(4, 2, COEF),
        pltpu.VMEM(w0.shape, BF16),
        pltpu.VMEM((2 * w1.shape[1], 2 * w1.shape[2]), BF16),
        pltpu.VMEM((2 * w2.shape[1], 2 * w2.shape[2]), BF16),
        pltpu.VMEM((E, FRAME * COEF), F32),
        pltpu.VMEM((E, TGT), BF16),
        pltpu.VMEM((E, SRC), BF16),
        pltpu.VMEM((TGT, E), BF16),
        pltpu.VMEM((SRC, E), BF16),
        pltpu.VMEM((PAIRS, E, 2 * C), BF16),
        pltpu.VMEM((PAIRS, E, 2 * C), BF16),
        pltpu.VMEM((PAIRS, E, 2 * C), BF16),
        pltpu.VMEM((E, FRAME * 2 * C), BF16),
        pltpu.VMEM((E, FRAME * C), BF16),
        pltpu.VMEM((E, FRAME * C), F32),
        buffer(4, 2, 4, COEF),
        buffer(4, 2, COEF),
        pltpu.SemaphoreType.DMA((12,)),
        pltpu.SemaphoreType.DMA((MESSAGES,)),
        pltpu.SemaphoreType.DMA((MESSAGES,)),
        buffer(4, COEF),
        buffer(4, COEF),
        buffer(4, COEF),
        buffer(COEF),
        buffer(COEF),
        pltpu.VMEM((COEF, A, C), F32),
    ]
    for h, lead in ((0, (2, 4)), (1, (4, 2))):
        whole = length(HALVES[h])
        plus, minus = length(QUARTERS[2 * h]), length(QUARTERS[2 * h + 1])
        scratch += [
            buffer(*lead, plus),
            buffer(*lead, minus),
            buffer(*lead, plus),
            buffer(*lead, minus),
            buffer(*lead, whole),
            buffer(*lead, whole),
            buffer(4, 2, whole),
            buffer(2, plus),
            buffer(2, minus),
            buffer(2, plus),
            buffer(2, minus),
            buffer(2, 2, whole),
        ]
    vmem = pl.BlockSpec(memory_space=pltpu.VMEM)
    hbm = pl.BlockSpec(memory_space=pl.ANY)
    return pl.pallas_call(
        fused_kernel,
        out_shape=jax.ShapeDtypeStruct((COEF, A, C), F32),
        in_specs=[pl.BlockSpec(memory_space=pltpu.SMEM)] + [vmem] * 5 + [hbm] * 3,
        out_specs=vmem,
        scratch_shapes=scratch,
        compiler_params=pltpu.CompilerParams(
            collective_id=0, has_side_effects=True, vmem_limit_bytes=VMEM_LIMIT
        ),
        name="edge_gradients",
    )(count, src_ids, tgt_ids, rot, feats, cots, w0, w1, w2)


def local(node_feats, grad_out, edge_src, edge_tgt, edge_counts, wigner, w_zero, w_one, w_two):
    total = fused(
        edge_counts,
        edge_src[0],
        edge_tgt[0],
        jnp.transpose(wigner[0, 0]),
        jnp.transpose(node_feats, (1, 0, 2)),
        jnp.transpose(grad_out, (1, 0, 2)),
        w_zero,
        w_one,
        w_two,
    )
    return jnp.transpose(total, (1, 0, 2))


def solution(mesh):
    placed = (
        P(("row", "col"), None, None),
        P(("row", "col"), None, None),
        P("row", "col", None),
        P("row", "col", None),
        P("row", "col"),
        P("row", "col", None, None),
        P(),
        P(),
        P(),
    )
    return jax.shard_map(
        local, mesh=mesh, in_specs=placed, out_specs=P(("row", "col"), None, None), check_vma=False
    )
```

```python
import jax
import jax.numpy as jnp
from jax import lax
from jax.experimental import pallas as pl
from jax.experimental.pallas import tpu as pltpu
from jax.sharding import PartitionSpec as P

MESH = pl.DeviceIdType.MESH
F32 = jnp.float32
BF16 = jnp.bfloat16

ROWS = 8
COLS = 32
A = 8
E = 512
C = 128
COEF = 25
PAIRS = 13
FRAME = 19
GROUP = 16
BLOCK = 256
LANES = 128
TGT = COLS * A
SRC = ROWS * A
VMEM_LIMIT = 58 * 1024 * 1024


def frame_rows(degree):
    rows = [degree]
    if degree >= 1:
        rows += [5 + degree - 1, 9 + degree - 1]
    if degree >= 2:
        rows += [13 + degree - 2, 16 + degree - 2]
    return rows


def degree_cols(degree):
    return list(range(degree * degree, (degree + 1) * (degree + 1)))


def ring(value, step):
    return lax.rem(value + step, 4)


class Net:
    def __init__(self, send, recv):
        row = lax.axis_index("row")
        col = lax.axis_index("col")
        self.x = lax.div(col, 8)
        self.z = lax.rem(lax.div(col, 4), 2)
        self.y = lax.rem(col, 4)
        self.high = lax.div(row, 2)
        self.core = lax.rem(row, 2)
        self.send = send
        self.recv = recv
        self.copies = []

    def at(self, x=0, z=0, y=0):
        z_now = 1 - self.z if z else self.z
        return {"col": ring(self.x, x) * 8 + z_now * 4 + ring(self.y, y)}

    def peer(self, high=0, core=0):
        core_now = 1 - self.core if core else self.core
        return {"row": ring(self.high, high) * 2 + core_now}

    def greet(self):
        barrier = pltpu.get_barrier_semaphore()
        devices = [self.at(x=1), self.at(x=3), self.at(y=1), self.at(y=3), self.at(z=1)]
        devices += [self.peer(high=step) for step in (1, 2, 3)] + [self.peer(core=1)]
        for device in devices:
            pl.semaphore_signal(barrier, inc=1, device_id=device, device_id_type=MESH)
        pl.semaphore_wait(barrier, len(devices))

    def push(self, source, target, device):
        n = len(self.copies)
        copy = pltpu.make_async_remote_copy(
            src_ref=source,
            dst_ref=target,
            send_sem=self.send.at[n],
            recv_sem=self.recv.at[n],
            device_id=device,
            device_id_type=MESH,
        )
        copy.start()
        self.copies.append(copy)
        return copy


QUARTERS = ((0, 7), (7, 13), (13, 19), (19, 25))
HALVES = ((0, 13), (13, 25))
MESSAGES = 160


def span(bounds):
    return pl.ds(bounds[0], bounds[1] - bounds[0])


def length(bounds):
    return bounds[1] - bounds[0]


def reduce_body(net, sib, tgt, src, out, scratch):
    row_in, row_sum, sib_in, z_in, z_out, kept = scratch[:6]
    halves = (scratch[6:18], scratch[18:30])

    def toward(h, phase, sign):
        along_x = (h == 0) == (phase == 0)
        return net.at(x=sign) if along_x else net.at(y=sign)

    def block(h, step, piece):
        bounds = QUARTERS[2 * h + piece]
        if h == 0:
            return tgt.at[ring(net.x, step), :, :, span(bounds)]
        return tgt.at[:, :, ring(net.y, step), span(bounds)]

    def tail(h, piece):
        first = QUARTERS[2 * h][0]
        bounds = QUARTERS[2 * h + piece]
        return pl.ds(bounds[0] - first, length(bounds))

    passing = {}
    direct = {}
    for h in (0, 1):
        in_p, in_m, up, um, end_p, end_m = halves[h][:6]
        passing[h, 1] = net.push(block(h, 2, 0), in_p, toward(h, 0, 1))
        passing[h, 3] = net.push(block(h, 2, 1), in_m, toward(h, 0, 3))
    for h in (0, 1):
        in_p, in_m, up, um, end_p, end_m = halves[h][:6]
        direct[h, 1] = net.push(block(h, 1, 1), end_p.at[:, :, tail(h, 1)], toward(h, 0, 1))
        direct[h, 3] = net.push(block(h, 3, 0), end_m.at[:, :, tail(h, 0)], toward(h, 0, 3))

    sib.wait_recv()
    for high in range(4):
        row_sum[high] = (src[high, net.core].astype(F32) + sib_in[high].astype(F32)).astype(BF16)
    rows = [
        net.push(row_sum.at[ring(net.high, step)], row_in.at[net.high], net.peer(high=step))
        for step in (2, 1, 3)
    ]

    joined = {}
    for sign, piece in ((1, 0), (3, 1)):
        for h in (0, 1):
            in_p, in_m, up, um, end_p, end_m = halves[h][:6]
            came, sums, end = (in_p, up, end_p) if sign == 1 else (in_m, um, end_m)
            passing[h, sign].wait_recv()
            mine = block(h, sign, piece)
            for i in range(came.shape[0]):
                for j in range(came.shape[1]):
                    sums[i, j] = (came[i, j].astype(F32) + mine[i, j].astype(F32)).astype(BF16)
            joined[h, sign] = net.push(sums, end.at[:, :, tail(h, piece)], toward(h, 0, sign))

    passing_2 = {}
    direct_2 = {}
    for h in (0, 1):
        in_p, in_m, up, um, end_p, end_m = halves[h][:6]
        total, in2_p, in2_m, up2, um2, ends = halves[h][6:12]
        for sign in (1, 3):
            direct[h, sign].wait_recv()
            joined[h, sign].wait_recv()
        for i in range(end_p.shape[0]):
            for j in range(end_p.shape[1]):
                if h == 0:
                    mine, to = tgt[net.x, i, j, 0:13], total.at[j, i]
                else:
                    mine, to = tgt[i, j, net.y, 13:25], total.at[i, j]
                to[...] = (
                    mine.astype(F32) + end_p[i, j].astype(F32) + end_m[i, j].astype(F32)
                ).astype(BF16)
        here = net.y if h == 0 else net.x
        passing_2[h, 1] = net.push(
            total.at[ring(here, 2), :, tail(h, 0)], in2_p, toward(h, 1, 1)
        )
        passing_2[h, 3] = net.push(
            total.at[ring(here, 2), :, tail(h, 1)], in2_m, toward(h, 1, 3)
        )
        direct_2[h, 1] = net.push(
            total.at[ring(here, 1), :, tail(h, 1)], ends.at[0, :, tail(h, 1)], toward(h, 1, 1)
        )
        direct_2[h, 3] = net.push(
            total.at[ring(here, 3), :, tail(h, 0)], ends.at[1, :, tail(h, 0)], toward(h, 1, 3)
        )
    joined_2 = {}
    for h in (0, 1):
        total, in2_p, in2_m, up2, um2, ends = halves[h][6:12]
        here = net.y if h == 0 else net.x
        for n, (sign, piece, came, sums) in enumerate(((1, 0, in2_p, up2), (3, 1, in2_m, um2))):
            passing_2[h, sign].wait_recv()
            for i in range(2):
                mine = total[ring(here, sign), i, tail(h, piece)]
                sums[i] = (came[i].astype(F32) + mine.astype(F32)).astype(BF16)
            joined_2[h, sign] = net.push(sums, ends.at[n, :, tail(h, piece)], toward(h, 1, sign))
    for copy in rows:
        copy.wait_recv()
    across = []
    for h in (0, 1):
        total, in2_p, in2_m, up2, um2, ends = halves[h][6:12]
        here = net.y if h == 0 else net.x
        for sign in (1, 3):
            direct_2[h, sign].wait_recv()
            joined_2[h, sign].wait_recv()
        at = span(HALVES[h])
        for z_now, to in ((1 - net.z, z_out), (net.z, kept)):
            value = total[here, z_now].astype(F32) + ends[0, z_now].astype(F32)
            value = value + ends[1, z_now].astype(F32)
            to[at] = value.astype(to.dtype)
        across.append(net.push(z_out.at[at], z_in.at[at], net.at(z=1)))
    value = kept[...] + row_sum[net.high].astype(F32)
    for step in (1, 2, 3):
        value = value + row_in[ring(net.high, step)].astype(F32)
    kept[...] = value
    for copy in across:
        copy.wait_recv()
    out[...] = kept[...] + z_in[...].astype(F32)


class Flow:
    def __init__(self, net, own, full):
        self.net = net
        self.own = own
        self.full = full
        self.inner = {}
        self.outer = {}
        self.passed = {}
        self.last = []

    def place(self, h, outer, inner, z, bounds):
        net = self.net
        near, far = (inner, outer) if h == 0 else (outer, inner)
        z_now = (net.z, 1 - net.z, slice(0, 2))[z]
        return self.full.at[ring(net.x, far), z_now, ring(net.y, near), span(bounds)]

    def step_to(self, h, phase, sign):
        along_y = (h == 0) == (phase == 0)
        return self.net.at(y=sign) if along_y else self.net.at(x=sign)

    def spread(self, h, inner, z):
        block = self.place(h, 0, inner, z, HALVES[h])
        source = self.own.at[span(HALVES[h])] if (inner, z) == (0, 0) else block
        for sign in (1, 3):
            self.outer[h, z, inner, sign] = self.net.push(source, block, self.step_to(h, 1, sign))

    def relay(self, h, z, inner):
        for sign, quarter in ((1, 0), (3, 1)):
            self.outer[h, z, inner, sign].wait_recv()
            block = self.place(h, 4 - sign, inner, z, QUARTERS[2 * h + quarter])
            self.last.append(self.net.push(block, block, self.step_to(h, 1, sign)))

    def send_own(self):
        net = self.net
        self.across = net.push(self.own, self.full.at[net.x, net.z, net.y], net.at(z=1))
        for h in (0, 1):
            for sign in (1, 3):
                self.inner[h, 0, sign] = net.push(
                    self.own.at[span(HALVES[h])],
                    self.place(h, 0, 0, 0, HALVES[h]),
                    self.step_to(h, 0, sign),
                )
        for h in (0, 1):
            self.spread(h, 0, 0)

    def send_partner(self):
        self.across.wait_recv()
        for h in (0, 1):
            block = self.place(h, 0, 0, 1, HALVES[h])
            for sign in (1, 3):
                self.inner[h, 1, sign] = self.net.push(block, block, self.step_to(h, 0, sign))
        for h in (0, 1):
            self.spread(h, 0, 1)

    def pass_on(self):
        for sign, quarter in ((1, 0), (3, 1)):
            for h in (0, 1):
                self.inner[h, 0, sign].wait_recv()
                self.inner[h, 1, sign].wait_recv()
                block = self.place(h, 0, 4 - sign, 2, QUARTERS[2 * h + quarter])
                self.passed[h, sign] = self.net.push(block, block, self.step_to(h, 0, sign))
                self.spread(h, 4 - sign, 2)

    def relay_first(self):
        for z in (0, 1):
            for h in (0, 1):
                self.relay(h, z, 0)

    def spread_far(self):
        for h in (0, 1):
            self.passed[h, 1].wait_recv()
            self.passed[h, 3].wait_recv()
            self.spread(h, 2, 2)

    def relay_rest(self, inner):
        for h in (0, 1):
            self.relay(h, 2, inner)

    def finish(self):
        for copy in self.last:
            copy.wait_recv()


def dot(x, y):
    return jnp.dot(x, y, preferred_element_type=F32)


def dot_t(x, y):
    return lax.dot_general(x, y, (((1,), (1,)), ((), ())), preferred_element_type=F32)


def t_dot(x, y):
    return lax.dot_general(x, y, (((0,), (0,)), ((), ())), preferred_element_type=F32)


def flip(value):
    return jnp.transpose(value.astype(F32)).astype(BF16)


def hot(ids, size):
    return (ids == lax.broadcasted_iota(jnp.int32, size, 0)).astype(F32).astype(BF16)


def tile_at(i):
    lanes = pl.ds(pl.multiple_of(lax.div(i, C // GROUP) * LANES, LANES), LANES)
    shift = lax.rem(i, C // GROUP) * GROUP

    def rows(block):
        return pl.ds(pl.multiple_of(block * C + shift, GROUP), GROUP)

    return lanes, rows


def fused_kernel(
    count, src_ids, tgt_ids, rot, feats, cots, w0, w1, w2, out,
    gf, gc, gs, w0_in, full1, full2, w0_flip, flip1, flip2, rot_wide, mark_t, mark_s,
    xf, xc, xs, frame, grad_y, y, tgt_sum, src_sum, local_sem, send, recv, *reduce_scratch,
):
    net = Net(send, recv)
    loads = [pltpu.make_async_copy(w0, w0_in, local_sem.at[0])]
    for n, (weights, full) in enumerate(((w1, full1), (w2, full2))):
        k, m = weights.shape[1:]
        for i in range(2):
            for j in range(2):
                loads.append(
                    pltpu.make_async_copy(
                        weights.at[(i + j) % 2],
                        full.at[pl.ds(i * k, k), pl.ds(j * m, m)],
                        local_sem.at[1 + 4 * n + 2 * i + j],
                    )
                )
    mine = [
        pltpu.make_async_copy(feats, gf.at[net.x, net.z, net.y], local_sem.at[9]),
        pltpu.make_async_copy(cots, gc.at[net.x, net.z, net.y], local_sem.at[10]),
        pltpu.make_async_copy(feats, gs.at[net.high, net.core], local_sem.at[11]),
    ]
    for copy in mine + loads:
        copy.start()
    net.greet()

    first = Flow(net, feats, gf)
    second = Flow(net, cots, gc)
    first.send_own()
    sibling = [net.push(feats, gs.at[net.high, net.core], net.peer(core=1))]
    rows = [net.push(feats, gs.at[net.high, net.core], net.peer(high=step)) for step in (1, 3, 2)]

    valid = lax.broadcasted_iota(jnp.int32, (1, E), 1) < count[0, 0]
    mark_t[...] = hot(jnp.where(valid, tgt_ids[...], -1), (TGT, E))
    mark_s[...] = hot(jnp.where(valid, src_ids[...], -1), (SRC, E))
    first.send_partner()
    rot_wide[...] = rot[...].astype(F32)
    for copy in mine + loads:
        copy.wait()

    def flip_zero(r, carry):
        at = pl.ds(pl.multiple_of(r * BLOCK, BLOCK), BLOCK)
        w0_flip[:, at] = flip(w0_in[at, :])
        return carry

    lax.fori_loop(0, w0.shape[0] // BLOCK, flip_zero, 0)
    first.pass_on()

    def flip_order(weights, full, full_flip):
        k, m = weights.shape[1:]

        def body(r, carry):
            at = pl.ds(pl.multiple_of(r * BLOCK, BLOCK), BLOCK)
            below = pl.ds(pl.multiple_of(r * BLOCK + k, BLOCK), BLOCK)
            full[below, 0:m] = -full[below, 0:m]
            for j in range(2):
                value = flip(full[at, j * m : (j + 1) * m])
                full_flip[j * m : (j + 1) * m, at] = value
                full_flip[(1 - j) * m : (2 - j) * m, below] = -value if j else value
            return carry

        lax.fori_loop(0, k // BLOCK, body, 0)

    flip_order(w1, full1, flip1)
    first.relay_first()
    first.spread_far()
    for step, copy in zip((1, 3, 2), rows):
        copy.wait_recv()
        block = gs.at[ring(net.high, 4 - step), net.core]
        sibling.append(net.push(block, block, net.peer(core=1)))
    second.send_own()
    first.relay_rest(3)
    first.relay_rest(1)
    flip_order(w2, full2, flip2)
    first.relay_rest(2)
    second.send_partner()
    for copy in sibling:
        copy.wait_recv()

    def pair_of(full, p, rows):
        both = []
        for j in (2 * p, jnp.minimum(2 * p + 1, COEF - 1)):
            piece = full[:, :, :, j] if len(full.shape) == 6 else full[:, :, j]
            both.append(piece.astype(F32).reshape(rows, C))
        return jnp.concatenate(both, axis=1).astype(BF16)

    def gather_some(marks, full, rows, to):
        def body(p, carry):
            at = pl.ds(pl.multiple_of(p * 2 * C, 2 * C), 2 * C)
            to[at, :] = t_dot(pair_of(full, p, rows), marks[...]).astype(BF16)
            return carry

        lax.fori_loop(0, PAIRS, body, 0)

    gather_some(mark_s, gs, SRC, xs)
    second.pass_on()
    first.finish()
    second.relay_first()
    gather_some(mark_t, gf, TGT, xf)
    second.spread_far()

    def factor_of(entry, lanes):
        return jnp.broadcast_to(rot_wide[entry : entry + 1, lanes], (GROUP, LANES))

    def rotate(i, carry):
        lanes, rows = tile_at(i)
        for degree in range(5):
            cols = degree_cols(degree)
            from_src = [xs[rows(j), lanes].astype(F32) for j in cols]
            from_tgt = [xf[rows(j), lanes].astype(F32) for j in cols]
            for k in frame_rows(degree):
                sums = [None, None]
                for n, j in enumerate(cols):
                    factor = factor_of(k * COEF + j, lanes)
                    for which, values in enumerate((from_src, from_tgt)):
                        term = factor * values[n]
                        sums[which] = term if sums[which] is None else sums[which] + term
                frame[rows(2 * k), lanes] = sums[0].astype(BF16)
                frame[rows(2 * k + 1), lanes] = sums[1].astype(BF16)
        return carry

    steps = (E // LANES) * (C // GROUP)
    lax.fori_loop(0, steps // 4, rotate, 0)
    second.relay_rest(3)
    second.relay_rest(1)
    lax.fori_loop(steps // 4, steps // 2, rotate, 0)
    second.relay_rest(2)
    lax.fori_loop(steps // 2, steps, rotate, 0)

    def forward(i, carry):
        at = pl.ds(pl.multiple_of(i * BLOCK, BLOCK), BLOCK)
        for begin, rows, weights in ((0, 5, w0_flip), (5, 8, flip1), (13, 6, flip2)):
            y[begin * C : (begin + rows) * C, at] = dot(
                weights[...], frame[2 * begin * C : 2 * (begin + rows) * C, at]
            )
        return carry

    lax.fori_loop(0, E // BLOCK, forward, 0)
    second.finish()
    gather_some(mark_t, gc, TGT, xc)

    def gate(i, carry):
        lanes, rows = tile_at(i)
        scalar = y[rows(0), lanes]
        gating = jax.nn.sigmoid(scalar)
        slope = gating * (1.0 - gating)
        total = jnp.zeros((GROUP, LANES), F32)
        lowest = None
        for degree in range(5):
            cols = degree_cols(degree)
            values = [xc[rows(j), lanes].astype(F32) for j in cols]
            for k in frame_rows(degree):
                value = None
                for n, j in enumerate(cols):
                    term = factor_of(k * COEF + j, lanes) * values[n]
                    value = term if value is None else value + term
                if k == 0:
                    lowest = value
                else:
                    total = total + value * y[rows(k), lanes]
                    grad_y[rows(k), lanes] = (gating * value).astype(BF16)
        grad_y[rows(0), lanes] = (lowest * (gating + scalar * slope) + total * slope).astype(BF16)
        return carry

    lax.fori_loop(0, steps, gate, 0)

    def backward(i, carry):
        at = pl.ds(pl.multiple_of(i * BLOCK, BLOCK), BLOCK)
        for begin, rows, weights in ((0, 5, w0_in), (5, 8, full1), (13, 6, full2)):
            frame[2 * begin * C : 2 * (begin + rows) * C, at] = dot(
                weights[...], grad_y[begin * C : (begin + rows) * C, at]
            ).astype(BF16)
        return carry

    lax.fori_loop(0, E // BLOCK, backward, 0)

    def unrotate(i, carry):
        lanes, rows = tile_at(i)
        for degree in range(5):
            ks = frame_rows(degree)
            of_src = [frame[rows(2 * k), lanes].astype(F32) for k in ks]
            of_tgt = [frame[rows(2 * k + 1), lanes].astype(F32) for k in ks]
            for j in degree_cols(degree):
                sums = [None, None]
                for n, k in enumerate(ks):
                    factor = factor_of(k * COEF + j, lanes)
                    for which, values in enumerate((of_src, of_tgt)):
                        term = factor * values[n]
                        sums[which] = term if sums[which] is None else sums[which] + term
                xs[rows(j), lanes] = sums[0].astype(BF16)
                xf[rows(j), lanes] = sums[1].astype(BF16)
        return carry

    lax.fori_loop(0, steps, unrotate, 0)

    def scatter(marks, grads, to, lead):
        for p in range(PAIRS):
            both = dot_t(marks[...], grads[2 * p * C : 2 * (p + 1) * C, :])
            for j in (2 * p, 2 * p + 1):
                if j < COEF:
                    value = both[:, (j % 2) * C : (j % 2 + 1) * C]
                    value = value.reshape(lead + (A, C)).astype(BF16)
                    if len(lead) == 3:
                        to[:, :, :, j] = value
                    else:
                        to[:, :, j] = value

    scatter(mark_s, xs, src_sum, (4, 2))
    sib = net.push(src_sum.at[:, 1 - net.core], reduce_scratch[2], net.peer(core=1))
    scatter(mark_t, xf, tgt_sum, (4, 2, 4))
    reduce_body(net, sib, tgt_sum, src_sum, out, reduce_scratch)
    for copy in net.copies:
        copy.wait_send()


def fused(count, src_ids, tgt_ids, rot, feats, cots, w0, w1, w2):
    def buffer(*lead):
        return pltpu.VMEM(lead + (A, C), BF16)

    scratch = [
        buffer(4, 2, 4, COEF),
        buffer(4, 2, 4, COEF),
        buffer(4, 2, COEF),
        pltpu.VMEM(w0.shape, BF16),
        pltpu.VMEM((2 * w1.shape[1], 2 * w1.shape[2]), BF16),
        pltpu.VMEM((2 * w2.shape[1], 2 * w2.shape[2]), BF16),
        pltpu.VMEM(w0.shape[::-1], BF16),
        pltpu.VMEM((2 * w1.shape[2], 2 * w1.shape[1]), BF16),
        pltpu.VMEM((2 * w2.shape[2], 2 * w2.shape[1]), BF16),
        pltpu.VMEM((FRAME * COEF, E), F32),
        pltpu.VMEM((TGT, E), BF16),
        pltpu.VMEM((SRC, E), BF16),
        pltpu.VMEM((PAIRS * 2 * C, E), BF16),
        pltpu.VMEM((PAIRS * 2 * C, E), BF16),
        pltpu.VMEM((PAIRS * 2 * C, E), BF16),
        pltpu.VMEM((FRAME * 2 * C, E), BF16),
        pltpu.VMEM((FRAME * C, E), BF16),
        pltpu.VMEM((FRAME * C, E), F32),
        buffer(4, 2, 4, COEF),
        buffer(4, 2, COEF),
        pltpu.SemaphoreType.DMA((12,)),
        pltpu.SemaphoreType.DMA((MESSAGES,)),
        pltpu.SemaphoreType.DMA((MESSAGES,)),
        buffer(4, COEF),
        buffer(4, COEF),
        buffer(4, COEF),
        buffer(COEF),
        buffer(COEF),
        pltpu.VMEM((COEF, A, C), F32),
    ]
    for h, lead in ((0, (2, 4)), (1, (4, 2))):
        whole = length(HALVES[h])
        plus, minus = length(QUARTERS[2 * h]), length(QUARTERS[2 * h + 1])
        scratch += [
            buffer(*lead, plus),
            buffer(*lead, minus),
            buffer(*lead, plus),
            buffer(*lead, minus),
            buffer(*lead, whole),
            buffer(*lead, whole),
            buffer(4, 2, whole),
            buffer(2, plus),
            buffer(2, minus),
            buffer(2, plus),
            buffer(2, minus),
            buffer(2, 2, whole),
        ]
    vmem = pl.BlockSpec(memory_space=pltpu.VMEM)
    hbm = pl.BlockSpec(memory_space=pl.ANY)
    return pl.pallas_call(
        fused_kernel,
        out_shape=jax.ShapeDtypeStruct((COEF, A, C), F32),
        in_specs=[pl.BlockSpec(memory_space=pltpu.SMEM)] + [vmem] * 5 + [hbm] * 3,
        out_specs=vmem,
        scratch_shapes=scratch,
        compiler_params=pltpu.CompilerParams(
            collective_id=0, has_side_effects=True, vmem_limit_bytes=VMEM_LIMIT
        ),
        name="edge_gradients",
    )(count, src_ids, tgt_ids, rot, feats, cots, w0, w1, w2)


def local(node_feats, grad_out, edge_src, edge_tgt, edge_counts, wigner, w_zero, w_one, w_two):
    total = fused(
        edge_counts,
        edge_src[0],
        edge_tgt[0],
        jnp.transpose(wigner[0, 0]),
        jnp.transpose(node_feats, (1, 0, 2)),
        jnp.transpose(grad_out, (1, 0, 2)),
        w_zero,
        w_one,
        w_two,
    )
    return jnp.transpose(total, (1, 0, 2))


def solution(mesh):
    placed = (
        P(("row", "col"), None, None),
        P(("row", "col"), None, None),
        P("row", "col", None),
        P("row", "col", None),
        P("row", "col"),
        P("row", "col", None, None),
        P(),
        P(),
        P(),
    )
    return jax.shard_map(
        local, mesh=mesh, in_specs=placed, out_specs=P(("row", "col"), None, None), check_vma=False
    )
```

```python
import jax
import jax.numpy as jnp
from jax import lax
from jax.experimental import pallas as pl
from jax.experimental.pallas import tpu as pltpu
from jax.sharding import PartitionSpec as P

MESH = pl.DeviceIdType.MESH
F32 = jnp.float32
BF16 = jnp.bfloat16

ROWS = 8
COLS = 32
A = 8
E = 512
C = 128
COEF = 25
PAIRS = 13
FRAME = 19
GROUP = 16
BLOCK = 256
LANES = 128
TGT = COLS * A
SRC = ROWS * A
VMEM_LIMIT = 58 * 1024 * 1024


def frame_rows(degree):
    rows = [degree]
    if degree >= 1:
        rows += [5 + degree - 1, 9 + degree - 1]
    if degree >= 2:
        rows += [13 + degree - 2, 16 + degree - 2]
    return rows


def degree_cols(degree):
    return list(range(degree * degree, (degree + 1) * (degree + 1)))


class Net:
    def __init__(self, send, recv):
        row = lax.axis_index("row")
        col = lax.axis_index("col")
        self.x = x = lax.div(col, 8)
        self.z = z = lax.rem(lax.div(col, 4), 2)
        self.y = y = lax.rem(col, 4)
        self.high = high = lax.div(row, 2)
        self.core = core = lax.rem(row, 2)
        self.along_x = {
            step: (row, lax.rem(x + step, 4) * 8 + z * 4 + y) for step in (1, 3)
        }
        self.along_y = {
            step: (row, x * 8 + z * 4 + lax.rem(y + step, 4)) for step in (1, 3)
        }
        self.along_z = (row, x * 8 + (1 - z) * 4 + y)
        self.along_high = {
            step: (lax.rem(high + step, 4) * 2 + core, col) for step in (1, 2, 3)
        }
        self.sibling = (high * 2 + 1 - core, col)
        self.send = send
        self.recv = recv
        self.copies = []
        self.sent = 0

    def greet(self):
        barrier = pltpu.get_barrier_semaphore()
        devices = list(self.along_x.values()) + list(self.along_y.values()) + [self.along_z]
        devices += list(self.along_high.values()) + [self.sibling]
        for device in devices:
            pl.semaphore_signal(barrier, inc=1, device_id=device, device_id_type=MESH)
        pl.semaphore_wait(barrier, len(devices))

    def push(self, source, target, device):
        n = len(self.copies)
        copy = pltpu.make_async_remote_copy(
            src_ref=source,
            dst_ref=target,
            send_sem=self.send.at[n],
            recv_sem=self.recv.at[n],
            device_id=device,
            device_id_type=MESH,
        )
        copy.start()
        self.copies.append(copy)
        return copy

    def settle(self, count):
        for copy in self.copies[self.sent : count]:
            copy.wait_send()
        self.sent = count


QUARTERS = ((0, 7), (7, 13), (13, 19), (19, 25))
HALVES = ((0, 13), (13, 25))
MESSAGES = 160


def span(bounds):
    return pl.ds(bounds[0], bounds[1] - bounds[0])


def length(bounds):
    return bounds[1] - bounds[0]


def reduce_body(net, sib, tgt, src, out, scratch):
    row_in, row_sum, sib_in, z_in, z_out, kept = scratch[:6]
    halves = (scratch[6:18], scratch[18:30])
    before = len(net.copies) - 1

    def toward(h, phase, sign):
        along_x = (h == 0) == (phase == 0)
        return (net.along_x if along_x else net.along_y)[sign]

    def block(h, step, piece):
        bounds = QUARTERS[2 * h + piece]
        if h == 0:
            return tgt.at[step, :, :, span(bounds)]
        return tgt.at[:, :, step, span(bounds)]

    def tail(h, piece):
        first = QUARTERS[2 * h][0]
        bounds = QUARTERS[2 * h + piece]
        return pl.ds(bounds[0] - first, length(bounds))

    passing = {}
    direct = {}
    for h in (0, 1):
        in_p, in_m, up, um, end_p, end_m = halves[h][:6]
        passing[h, 1] = net.push(block(h, 2, 0), in_p, toward(h, 0, 1))
        passing[h, 3] = net.push(block(h, 2, 1), in_m, toward(h, 0, 3))
    for h in (0, 1):
        in_p, in_m, up, um, end_p, end_m = halves[h][:6]
        direct[h, 1] = net.push(block(h, 1, 1), end_p.at[:, :, tail(h, 1)], toward(h, 0, 1))
        direct[h, 3] = net.push(block(h, 3, 0), end_m.at[:, :, tail(h, 0)], toward(h, 0, 3))

    sib.wait_recv()
    for high in range(4):
        row_sum[high] = (src[high, 0].astype(F32) + sib_in[high].astype(F32)).astype(BF16)
    rows = [
        net.push(row_sum.at[step], row_in.at[4 - step], net.along_high[step]) for step in (2, 1, 3)
    ]
    net.settle(before)

    joined = {}
    for sign, piece in ((1, 0), (3, 1)):
        for h in (0, 1):
            in_p, in_m, up, um, end_p, end_m = halves[h][:6]
            came, sums, end = (in_p, up, end_p) if sign == 1 else (in_m, um, end_m)
            passing[h, sign].wait_recv()
            mine = block(h, sign, piece)
            for i in range(came.shape[0]):
                for j in range(came.shape[1]):
                    sums[i, j] = (came[i, j].astype(F32) + mine[i, j].astype(F32)).astype(BF16)
            joined[h, sign] = net.push(sums, end.at[:, :, tail(h, piece)], toward(h, 0, sign))

    passing_2 = {}
    direct_2 = {}
    for h in (0, 1):
        in_p, in_m, up, um, end_p, end_m = halves[h][:6]
        total, in2_p, in2_m, up2, um2, ends = halves[h][6:12]
        for sign in (1, 3):
            direct[h, sign].wait_recv()
            joined[h, sign].wait_recv()

        def add(first):
            for i in range(2):
                if h == 0:
                    mine, one, two = tgt[0, i, first, 0:13], end_p[i, first], end_m[i, first]
                else:
                    mine, one, two = tgt[first, i, 0, 13:25], end_p[first, i], end_m[first, i]
                total[first, i] = (
                    mine.astype(F32) + one.astype(F32) + two.astype(F32)
                ).astype(BF16)

        add(2)
        passing_2[h, 1] = net.push(total.at[2, :, tail(h, 0)], in2_p, toward(h, 1, 1))
        passing_2[h, 3] = net.push(total.at[2, :, tail(h, 1)], in2_m, toward(h, 1, 3))
        add(1)
        direct_2[h, 1] = net.push(
            total.at[1, :, tail(h, 1)], ends.at[0, :, tail(h, 1)], toward(h, 1, 1)
        )
        add(3)
        direct_2[h, 3] = net.push(
            total.at[3, :, tail(h, 0)], ends.at[1, :, tail(h, 0)], toward(h, 1, 3)
        )
        add(0)
    joined_2 = {}
    for h in (0, 1):
        total, in2_p, in2_m, up2, um2, ends = halves[h][6:12]
        for n, (sign, piece, came, sums) in enumerate(((1, 0, in2_p, up2), (3, 1, in2_m, um2))):
            passing_2[h, sign].wait_recv()
            for i in range(2):
                mine = total[sign, i, tail(h, piece)]
                sums[i] = (came[i].astype(F32) + mine.astype(F32)).astype(BF16)
            joined_2[h, sign] = net.push(sums, ends.at[n, :, tail(h, piece)], toward(h, 1, sign))
    for copy in rows:
        copy.wait_recv()
    value = row_sum[0].astype(F32)
    for step in (1, 2, 3):
        value = value + row_in[step].astype(F32)
    kept[...] = value
    across = []
    for h in (0, 1):
        total, in2_p, in2_m, up2, um2, ends = halves[h][6:12]
        for sign in (1, 3):
            direct_2[h, sign].wait_recv()
            joined_2[h, sign].wait_recv()
        at = span(HALVES[h])
        value = total[0, 1].astype(F32) + ends[0, 1].astype(F32) + ends[1, 1].astype(F32)
        z_out[at] = value.astype(BF16)
        across.append(net.push(z_out.at[at], z_in.at[at], net.along_z))
        value = total[0, 0].astype(F32) + ends[0, 0].astype(F32) + ends[1, 0].astype(F32)
        kept[at] = kept[at] + value
    net.settle(len(net.copies))
    for copy in across:
        copy.wait_recv()
    out[...] = kept[...] + z_in[...].astype(F32)


class Flow:
    def __init__(self, net, own, full, early):
        self.net = net
        self.own = own
        self.full = full
        self.early = early
        self.arrivals = {}
        self.passed = {}
        self.last = []

    def place(self, h, outer, inner, z, bounds):
        z_now = slice(0, 2) if z == 2 else z
        x, y = (outer, inner) if h == 0 else (inner, outer)
        return self.full.at[x, z_now, y, span(bounds)]

    def step_to(self, h, phase, sign):
        along_y = (h == 0) == (phase == 0)
        return (self.net.along_y if along_y else self.net.along_x)[sign]

    def inward(self, h, z):
        source = self.place(h, 0, 0, z, HALVES[h])
        if z == 0:
            source = self.own.at[span(HALVES[h])]
        for sign in (1, 3):
            target = self.place(h, 0, 4 - sign, z, HALVES[h])
            copy = self.net.push(source, target, self.step_to(h, 0, sign))
            self.arrivals.setdefault((h, "inner", sign), []).append(copy)

    def spread(self, h, inner, z):
        source = self.place(h, 0, inner, z, HALVES[h])
        if (inner, z) == (0, 0):
            source = self.own.at[span(HALVES[h])]
        for sign in (1, 3):
            target = self.place(h, 4 - sign, inner, z, HALVES[h])
            copy = self.net.push(source, target, self.step_to(h, 1, sign))
            self.arrivals.setdefault((h, inner, sign), []).append(copy)

    def arrive(self, *key):
        for copy in self.arrivals[key]:
            copy.wait_recv()

    def relay(self, inner):
        for sign, quarter in ((1, 0), (3, 1)):
            for h in (0, 1):
                self.arrive(h, inner, sign)
                bounds = QUARTERS[2 * h + quarter]
                copy = self.net.push(
                    self.place(h, 4 - sign, inner, 2, bounds),
                    self.place(h, 2, inner, 2, bounds),
                    self.step_to(h, 1, sign),
                )
                self.last.append(copy)

    def send_own(self):
        net = self.net
        self.across = net.push(self.own, self.full.at[0, 1, 0], net.along_z)
        if self.early:
            for h in (0, 1):
                self.inward(h, 0)
            for h in (0, 1):
                self.spread(h, 0, 0)

    def send_partner(self):
        self.across.wait_recv()
        which = 1 if self.early else 2
        for h in (0, 1):
            self.inward(h, which)
        for h in (0, 1):
            self.spread(h, 0, which)

    def pass_on(self):
        for sign, quarter in ((1, 0), (3, 1)):
            for h in (0, 1):
                self.arrive(h, "inner", sign)
                bounds = QUARTERS[2 * h + quarter]
                self.passed[h, sign] = self.net.push(
                    self.place(h, 0, 4 - sign, 2, bounds),
                    self.place(h, 0, 2, 2, bounds),
                    self.step_to(h, 0, sign),
                )
        for inner in (3, 1):
            for h in (0, 1):
                self.spread(h, inner, 2)

    def spread_far(self):
        for h in (0, 1):
            self.passed[h, 1].wait_recv()
            self.passed[h, 3].wait_recv()
            self.spread(h, 2, 2)

    def finish(self):
        for copy in self.last:
            copy.wait_recv()


def dot(x, y):
    return jnp.dot(x, y, preferred_element_type=F32)


def dot_t(x, y):
    return lax.dot_general(x, y, (((1,), (1,)), ((), ())), preferred_element_type=F32)


def t_dot(x, y):
    return lax.dot_general(x, y, (((0,), (0,)), ((), ())), preferred_element_type=F32)


def flip(value):
    return jnp.transpose(value.astype(F32)).astype(BF16)


def hot(ids, size):
    return (ids == lax.broadcasted_iota(jnp.int32, size, 0)).astype(F32).astype(BF16)


def tile_at(i):
    lanes = pl.ds(pl.multiple_of(lax.div(i, C // GROUP) * LANES, LANES), LANES)
    shift = lax.rem(i, C // GROUP) * GROUP

    def rows(block):
        return pl.ds(pl.multiple_of(block * C + shift, GROUP), GROUP)

    return lanes, rows


def fused_kernel(
    count, src_ids, tgt_ids, rot, feats, cots, w0, w1, w2, out,
    gf, gc, gs, w0_in, full1, full2, w0_flip, flip1, flip2, rot_wide, mark_t, mark_s,
    xf, xc, xs, frame, grad_y, y, tgt_sum, src_sum, local_sem, send, recv, *reduce_scratch,
):
    net = Net(send, recv)
    loads = [pltpu.make_async_copy(w0, w0_in, local_sem.at[0])]
    for n, (weights, full) in enumerate(((w1, full1), (w2, full2))):
        k, m = weights.shape[1:]
        for i in range(2):
            for j in range(2):
                loads.append(
                    pltpu.make_async_copy(
                        weights.at[(i + j) % 2],
                        full.at[pl.ds(i * k, k), pl.ds(j * m, m)],
                        local_sem.at[1 + 4 * n + 2 * i + j],
                    )
                )
    mine = [
        pltpu.make_async_copy(feats, gf.at[0, 0, 0], local_sem.at[9]),
        pltpu.make_async_copy(cots, gc.at[0, 0, 0], local_sem.at[10]),
        pltpu.make_async_copy(feats, gs.at[0, 0], local_sem.at[11]),
    ]
    for copy in mine + loads:
        copy.start()
    net.greet()

    first = Flow(net, feats, gf, True)
    second = Flow(net, cots, gc, False)
    first.send_own()
    sibling = [net.push(feats, gs.at[0, 1], net.sibling)]
    rows = [net.push(feats, gs.at[4 - step, 0], net.along_high[step]) for step in (1, 3, 2)]
    second.send_own()
    for copy in mine:
        copy.wait()

    valid = lax.broadcasted_iota(jnp.int32, (1, E), 1) < count[0, 0]
    ids = tgt_ids[...]
    near_x = ((ids >> 6) - net.x) & 3
    near_z = ((ids >> 5) & 1) ^ net.z
    near_y = ((ids >> 3) - net.y) & 3
    ids = near_x * 64 + near_z * 32 + near_y * 8 + (ids & 7)
    mark_t[...] = hot(jnp.where(valid, ids, -1), (TGT, E))
    ids = src_ids[...]
    near_high = ((ids >> 4) - net.high) & 3
    near_core = ((ids >> 3) & 1) ^ net.core
    ids = near_high * 16 + near_core * 8 + (ids & 7)
    mark_s[...] = hot(jnp.where(valid, ids, -1), (SRC, E))
    first.send_partner()
    rot_wide[...] = rot[...].astype(F32)
    first.pass_on()
    second.send_partner()
    for step, copy in zip((1, 3, 2), rows):
        copy.wait_recv()
        sibling.append(net.push(gs.at[4 - step, 0], gs.at[4 - step, 1], net.sibling))
    first.relay(0)
    first.spread_far()
    for copy in loads:
        copy.wait()

    def flip_zero(r, carry):
        at = pl.ds(pl.multiple_of(r * BLOCK, BLOCK), BLOCK)
        value = flip(w0_in[at, :])
        for part in range(2):
            to = pl.ds(pl.multiple_of(part * (w0.shape[0] // 2) + r * C, C), C)
            w0_flip[:, to] = value[:, part * C : (part + 1) * C]
        return carry

    def flip_order(weights, full, full_flip):
        k, m = weights.shape[1:]

        def body(r, carry):
            at = pl.ds(pl.multiple_of(r * BLOCK, BLOCK), BLOCK)
            below = pl.ds(pl.multiple_of(r * BLOCK + k, BLOCK), BLOCK)
            full[below, 0:m] = -full[below, 0:m]
            for j in range(2):
                value = flip(full[at, j * m : (j + 1) * m])
                for part in range(2):
                    piece = value[:, part * C : (part + 1) * C]
                    to = pl.ds(pl.multiple_of(part * k + r * C, C), C)
                    full_flip[j * m : (j + 1) * m, to] = piece
                    to = pl.ds(pl.multiple_of(part * k + k // 2 + r * C, C), C)
                    full_flip[(1 - j) * m : (2 - j) * m, to] = -piece if j else piece
            return carry

        lax.fori_loop(0, k // BLOCK, body, 0)

    def gather_some(marks, full, rows, to):
        for p in range(PAIRS):
            both = []
            for j in (2 * p, min(2 * p + 1, COEF - 1)):
                piece = full[:, :, :, j] if len(full.shape) == 6 else full[:, :, j]
                both.append(piece.astype(F32).reshape(rows, C))
            block = jnp.concatenate(both, axis=1).astype(BF16)
            to[2 * p * C : 2 * (p + 1) * C, :] = t_dot(block, marks[...]).astype(BF16)

    def factor_of(entry, lanes):
        return jnp.broadcast_to(rot_wide[entry : entry + 1, lanes], (GROUP, LANES))

    def rotate_from(source, base):
        def rotate(i, carry):
            lanes, rows = tile_at(i)
            for degree in range(5):
                cols = degree_cols(degree)
                values = [source[rows(j), lanes].astype(F32) for j in cols]
                for k in frame_rows(degree):
                    value = None
                    for n, j in enumerate(cols):
                        term = factor_of(k * COEF + j, lanes) * values[n]
                        value = term if value is None else value + term
                    frame[rows(base + k), lanes] = value.astype(BF16)
            return carry

        return rotate

    steps = (E // LANES) * (C // GROUP)
    parts = ((0, 5, w0_in, w0_flip), (5, 8, full1, flip1), (13, 6, full2, flip2))

    def forward_from(side):
        def forward(i, carry):
            at = pl.ds(pl.multiple_of(i * BLOCK, BLOCK), BLOCK)
            for begin, rows, plain, turned in parts:
                into = slice(begin * C, (begin + rows) * C)
                base = side * FRAME * C
                value = dot(
                    turned[:, side * rows * C : (side + 1) * rows * C],
                    frame[base + begin * C : base + (begin + rows) * C, at],
                )
                y[into, at] = y[into, at] + value if side else value
            return carry

        return forward

    rotate_src, rotate_tgt = rotate_from(xs, 0), rotate_from(xf, FRAME)
    forward_src, forward_tgt = forward_from(0), forward_from(1)

    lax.fori_loop(0, w0.shape[0] // BLOCK, flip_zero, 0)
    first.relay(3)
    second.pass_on()
    first.relay(1)
    for copy in sibling:
        copy.wait_recv()
    gather_some(mark_s, gs, SRC, xs)
    first.relay(2)
    second.relay(0)
    second.spread_far()
    flip_order(w1, full1, flip1)
    second.relay(3)
    second.relay(1)
    lax.fori_loop(0, steps, rotate_src, 0)
    second.relay(2)
    flip_order(w2, full2, flip2)
    lax.fori_loop(0, E // BLOCK, forward_src, 0)
    first.finish()
    gather_some(mark_t, gf, TGT, xf)
    lax.fori_loop(0, steps, rotate_tgt, 0)
    lax.fori_loop(0, E // BLOCK, forward_tgt, 0)
    second.finish()
    gather_some(mark_t, gc, TGT, xc)

    def gate(i, carry):
        lanes, rows = tile_at(i)
        scalar = y[rows(0), lanes]
        gating = jax.nn.sigmoid(scalar)
        slope = gating * (1.0 - gating)
        total = jnp.zeros((GROUP, LANES), F32)
        lowest = None
        for degree in range(5):
            cols = degree_cols(degree)
            values = [xc[rows(j), lanes].astype(F32) for j in cols]
            for k in frame_rows(degree):
                value = None
                for n, j in enumerate(cols):
                    term = factor_of(k * COEF + j, lanes) * values[n]
                    value = term if value is None else value + term
                if k == 0:
                    lowest = value
                else:
                    total = total + value * y[rows(k), lanes]
                    grad_y[rows(k), lanes] = (gating * value).astype(BF16)
        grad_y[rows(0), lanes] = (lowest * (gating + scalar * slope) + total * slope).astype(BF16)
        return carry

    lax.fori_loop(0, steps, gate, 0)

    def backward(i, carry):
        at = pl.ds(pl.multiple_of(i * BLOCK, BLOCK), BLOCK)
        for begin, rows, weights, turned in parts:
            frame[2 * begin * C : 2 * (begin + rows) * C, at] = dot(
                weights[...], grad_y[begin * C : (begin + rows) * C, at]
            ).astype(BF16)
        return carry

    lax.fori_loop(0, E // BLOCK, backward, 0)

    def unrotate(i, carry):
        lanes, rows = tile_at(i)
        for degree in range(5):
            ks = frame_rows(degree)
            of_src = [frame[rows(2 * k), lanes].astype(F32) for k in ks]
            of_tgt = [frame[rows(2 * k + 1), lanes].astype(F32) for k in ks]
            for j in degree_cols(degree):
                sums = [None, None]
                for n, k in enumerate(ks):
                    factor = factor_of(k * COEF + j, lanes)
                    for which, values in enumerate((of_src, of_tgt)):
                        term = factor * values[n]
                        sums[which] = term if sums[which] is None else sums[which] + term
                xs[rows(j), lanes] = sums[0].astype(BF16)
                xf[rows(j), lanes] = sums[1].astype(BF16)
        return carry

    lax.fori_loop(0, steps, unrotate, 0)

    def scatter(marks, grads, to, lead):
        for p in range(PAIRS):
            both = dot_t(marks[...], grads[2 * p * C : 2 * (p + 1) * C, :])
            for j in (2 * p, 2 * p + 1):
                if j < COEF:
                    value = both[:, (j % 2) * C : (j % 2 + 1) * C]
                    value = value.reshape(lead + (A, C)).astype(BF16)
                    if len(lead) == 3:
                        to[:, :, :, j] = value
                    else:
                        to[:, :, j] = value

    scatter(mark_s, xs, src_sum, (4, 2))
    sib = net.push(src_sum.at[:, 1], reduce_scratch[2], net.sibling)
    scatter(mark_t, xf, tgt_sum, (4, 2, 4))
    reduce_body(net, sib, tgt_sum, src_sum, out, reduce_scratch)


def fused(count, src_ids, tgt_ids, rot, feats, cots, w0, w1, w2):
    def buffer(*lead):
        return pltpu.VMEM(lead + (A, C), BF16)

    scratch = [
        buffer(4, 2, 4, COEF),
        buffer(4, 2, 4, COEF),
        buffer(4, 2, COEF),
        pltpu.VMEM(w0.shape, BF16),
        pltpu.VMEM((2 * w1.shape[1], 2 * w1.shape[2]), BF16),
        pltpu.VMEM((2 * w2.shape[1], 2 * w2.shape[2]), BF16),
        pltpu.VMEM(w0.shape[::-1], BF16),
        pltpu.VMEM((2 * w1.shape[2], 2 * w1.shape[1]), BF16),
        pltpu.VMEM((2 * w2.shape[2], 2 * w2.shape[1]), BF16),
        pltpu.VMEM((FRAME * COEF, E), F32),
        pltpu.VMEM((TGT, E), BF16),
        pltpu.VMEM((SRC, E), BF16),
        pltpu.VMEM((PAIRS * 2 * C, E), BF16),
        pltpu.VMEM((PAIRS * 2 * C, E), BF16),
        pltpu.VMEM((PAIRS * 2 * C, E), BF16),
        pltpu.VMEM((FRAME * 2 * C, E), BF16),
        pltpu.VMEM((FRAME * C, E), BF16),
        pltpu.VMEM((FRAME * C, E), F32),
        buffer(4, 2, 4, COEF),
        buffer(4, 2, COEF),
        pltpu.SemaphoreType.DMA((12,)),
        pltpu.SemaphoreType.DMA((MESSAGES,)),
        pltpu.SemaphoreType.DMA((MESSAGES,)),
        buffer(4, COEF),
        buffer(4, COEF),
        buffer(4, COEF),
        buffer(COEF),
        buffer(COEF),
        pltpu.VMEM((COEF, A, C), F32),
    ]
    for h, lead in ((0, (2, 4)), (1, (4, 2))):
        whole = length(HALVES[h])
        plus, minus = length(QUARTERS[2 * h]), length(QUARTERS[2 * h + 1])
        scratch += [
            buffer(*lead, plus),
            buffer(*lead, minus),
            buffer(*lead, plus),
            buffer(*lead, minus),
            buffer(*lead, whole),
            buffer(*lead, whole),
            buffer(4, 2, whole),
            buffer(2, plus),
            buffer(2, minus),
            buffer(2, plus),
            buffer(2, minus),
            buffer(2, 2, whole),
        ]
    vmem = pl.BlockSpec(memory_space=pltpu.VMEM)
    hbm = pl.BlockSpec(memory_space=pl.ANY)
    return pl.pallas_call(
        fused_kernel,
        out_shape=jax.ShapeDtypeStruct((COEF, A, C), F32),
        in_specs=[pl.BlockSpec(memory_space=pltpu.SMEM)] + [vmem] * 5 + [hbm] * 3,
        out_specs=vmem,
        scratch_shapes=scratch,
        compiler_params=pltpu.CompilerParams(
            collective_id=0, has_side_effects=True, vmem_limit_bytes=VMEM_LIMIT
        ),
        name="edge_gradients",
    )(count, src_ids, tgt_ids, rot, feats, cots, w0, w1, w2)


def local(node_feats, grad_out, edge_src, edge_tgt, edge_counts, wigner, w_zero, w_one, w_two):
    total = fused(
        edge_counts,
        edge_src[0],
        edge_tgt[0],
        jnp.transpose(wigner[0, 0]),
        jnp.transpose(node_feats, (1, 0, 2)),
        jnp.transpose(grad_out, (1, 0, 2)),
        w_zero,
        w_one,
        w_two,
    )
    return jnp.transpose(total, (1, 0, 2))


def solution(mesh):
    placed = (
        P(("row", "col"), None, None),
        P(("row", "col"), None, None),
        P("row", "col", None),
        P("row", "col", None),
        P("row", "col"),
        P("row", "col", None, None),
        P(),
        P(),
        P(),
    )
    return jax.shard_map(
        local, mesh=mesh, in_specs=placed, out_specs=P(("row", "col"), None, None), check_vma=False
    )
```

```python
import jax
import jax.numpy as jnp
from jax import lax
from jax.experimental import pallas as pl
from jax.experimental.pallas import tpu as pltpu
from jax.sharding import PartitionSpec as P

MESH = pl.DeviceIdType.MESH
F32 = jnp.float32
BF16 = jnp.bfloat16

ROWS = 8
COLS = 32
A = 8
E = 512
C = 128
COEF = 25
PAIRS = 13
FRAME = 19
GROUP = 16
BLOCK = 256
LANES = 128
TGT = COLS * A
SRC = ROWS * A
VMEM_LIMIT = 58 * 1024 * 1024


def frame_rows(degree):
    rows = [degree]
    if degree >= 1:
        rows += [5 + degree - 1, 9 + degree - 1]
    if degree >= 2:
        rows += [13 + degree - 2, 16 + degree - 2]
    return rows


def degree_cols(degree):
    return list(range(degree * degree, (degree + 1) * (degree + 1)))


class Net:
    def __init__(self, send, recv):
        row = lax.axis_index("row")
        col = lax.axis_index("col")
        self.x = x = lax.div(col, 8)
        self.z = z = lax.rem(lax.div(col, 4), 2)
        self.y = y = lax.rem(col, 4)
        self.high = high = lax.div(row, 2)
        self.core = core = lax.rem(row, 2)
        zs = (z, 1 - z)
        self.plane = {}
        for far in (0, 1):
            for step in range(4):
                if step or far:
                    self.plane[0, step, far] = (row, x * 8 + zs[far] * 4 + lax.rem(y + step, 4))
                    self.plane[1, step, far] = (row, lax.rem(x + step, 4) * 8 + zs[far] * 4 + y)
        self.along_high = {
            step: (lax.rem(high + step, 4) * 2 + core, col) for step in (1, 2, 3)
        }
        self.sibling = (high * 2 + 1 - core, col)
        self.send = send
        self.recv = recv
        self.copies = []
        self.sent = 0

    def greet(self):
        barrier = pltpu.get_barrier_semaphore()
        devices = [self.plane[key] for key in self.plane if key != (1, 0, 1)]
        devices += list(self.along_high.values()) + [self.sibling]
        for device in devices:
            pl.semaphore_signal(barrier, inc=1, device_id=device, device_id_type=MESH)
        pl.semaphore_wait(barrier, len(devices))

    def push(self, source, target, device):
        n = len(self.copies)
        copy = pltpu.make_async_remote_copy(
            src_ref=source,
            dst_ref=target,
            send_sem=self.send.at[n],
            recv_sem=self.recv.at[n],
            device_id=device,
            device_id_type=MESH,
        )
        copy.start()
        self.copies.append(copy)
        return copy

    def settle(self, count):
        for copy in self.copies[self.sent : count]:
            copy.wait_send()
        self.sent = count


QUARTERS = ((0, 7), (7, 13), (13, 19), (19, 25))
HALVES = ((0, 13), (13, 25))
MESSAGES = 160


def span(bounds):
    return pl.ds(bounds[0], bounds[1] - bounds[0])


def length(bounds):
    return bounds[1] - bounds[0]


def reduce_body(net, sib, tgt, src, out, scratch):
    row_in, row_sum, sib_in, kept = scratch[:4]
    halves = (scratch[4:12], scratch[12:20])
    before = len(net.copies) - 1

    def toward(h, sign):
        return net.plane[1 - h, sign, 0]

    def block(h, step, piece):
        bounds = QUARTERS[2 * h + piece]
        if h == 0:
            return tgt.at[step, :, :, span(bounds)]
        return tgt.at[:, :, step, span(bounds)]

    def tail(h, piece):
        first = QUARTERS[2 * h][0]
        bounds = QUARTERS[2 * h + piece]
        return pl.ds(bounds[0] - first, length(bounds))

    passing = {}
    direct = {}
    for h in (0, 1):
        in_p, in_m, up, um, end_p, end_m = halves[h][:6]
        passing[h, 1] = net.push(block(h, 2, 0), in_p, toward(h, 1))
        passing[h, 3] = net.push(block(h, 2, 1), in_m, toward(h, 3))
    for h in (0, 1):
        in_p, in_m, up, um, end_p, end_m = halves[h][:6]
        direct[h, 1] = net.push(block(h, 1, 1), end_p.at[:, :, tail(h, 1)], toward(h, 1))
        direct[h, 3] = net.push(block(h, 3, 0), end_m.at[:, :, tail(h, 0)], toward(h, 3))

    sib.wait_recv()
    for high in range(4):
        row_sum[high] = (src[high, 0].astype(F32) + sib_in[high].astype(F32)).astype(BF16)
    rows = [
        net.push(row_sum.at[step], row_in.at[4 - step], net.along_high[step]) for step in (2, 1, 3)
    ]
    net.settle(before)

    joined = {}
    for sign, piece in ((1, 0), (3, 1)):
        for h in (0, 1):
            in_p, in_m, up, um, end_p, end_m = halves[h][:6]
            came, sums, end = (in_p, up, end_p) if sign == 1 else (in_m, um, end_m)
            passing[h, sign].wait_recv()
            mine = block(h, sign, piece)
            for i in range(came.shape[0]):
                for j in range(came.shape[1]):
                    sums[i, j] = (came[i, j].astype(F32) + mine[i, j].astype(F32)).astype(BF16)
            joined[h, sign] = net.push(sums, end.at[:, :, tail(h, piece)], toward(h, sign))

    final = []
    for h in (0, 1):
        in_p, in_m, up, um, end_p, end_m, total, ends = halves[h]
        for sign in (1, 3):
            direct[h, sign].wait_recv()
            joined[h, sign].wait_recv()
        for step in (2, 1, 3, 0):
            for far in (1, 0):
                if h == 0:
                    mine, one, two = tgt[0, far, step, 0:13], end_p[far, step], end_m[far, step]
                else:
                    mine, one, two = tgt[step, far, 0, 13:25], end_p[step, far], end_m[step, far]
                value = mine.astype(F32) + one.astype(F32) + two.astype(F32)
                if step or far:
                    total[step, far] = value.astype(BF16)
                    final.append(
                        net.push(
                            total.at[step, far],
                            ends.at[(4 - step) % 4, far],
                            net.plane[h, step, far],
                        )
                    )
                else:
                    kept[span(HALVES[h])] = value
    for copy in rows:
        copy.wait_recv()
    value = kept[...] + row_sum[0].astype(F32)
    for step in (1, 2, 3):
        value = value + row_in[step].astype(F32)
    kept[...] = value
    net.settle(len(net.copies))
    for copy in final:
        copy.wait_recv()
    for h in (0, 1):
        ends = halves[h][7]
        at = span(HALVES[h])
        value = kept[at]
        for step in range(4):
            for far in (0, 1):
                if step or far:
                    value = value + ends[step, far].astype(F32)
        out[at] = value


class Flow:
    def __init__(self, net, own, full):
        self.net = net
        self.own = own
        self.full = full
        self.arrivals = {}
        self.outer = {}
        self.last = []

    def place(self, h, outer, inner, z, bounds):
        z_now = slice(0, 2) if z == 2 else z
        x, y = (outer, inner) if h == 0 else (inner, outer)
        return self.full.at[x, z_now, y, span(bounds)]

    def send_own(self):
        for step, far in ((0, 1), (1, 0), (3, 0), (1, 1), (3, 1), (2, 0), (2, 1)):
            for h in (0, 1):
                inner = (4 - step) % 4
                self.arrivals[h, inner, far] = self.net.push(
                    self.own.at[span(HALVES[h])],
                    self.place(h, 0, inner, far, HALVES[h]),
                    self.net.plane[h, step, far],
                )
            if step == 3 and not far:
                self.spread(0, 0)

    def spread(self, inner, z):
        for h in (0, 1):
            for far in (0, 1) if z == 2 else (z,):
                if inner or far:
                    self.arrivals[h, inner, far].wait_recv()
            source = self.place(h, 0, inner, z, HALVES[h])
            if (inner, z) == (0, 0):
                source = self.own.at[span(HALVES[h])]
            for sign in (1, 3):
                target = self.place(h, 4 - sign, inner, z, HALVES[h])
                copy = self.net.push(source, target, self.net.plane[1 - h, sign, 0])
                self.outer.setdefault((h, inner, sign), []).append(copy)

    def relay(self, inner):
        for sign, quarter in ((1, 0), (3, 1)):
            for h in (0, 1):
                for copy in self.outer[h, inner, sign]:
                    copy.wait_recv()
                bounds = QUARTERS[2 * h + quarter]
                copy = self.net.push(
                    self.place(h, 4 - sign, inner, 2, bounds),
                    self.place(h, 2, inner, 2, bounds),
                    self.net.plane[1 - h, sign, 0],
                )
                self.last.append(copy)

    def finish(self):
        for copy in self.last:
            copy.wait_recv()


def dot(x, y):
    return jnp.dot(x, y, preferred_element_type=F32)


def dot_t(x, y):
    return lax.dot_general(x, y, (((1,), (1,)), ((), ())), preferred_element_type=F32)


def t_dot(x, y):
    return lax.dot_general(x, y, (((0,), (0,)), ((), ())), preferred_element_type=F32)


def flip(value):
    return jnp.transpose(value.astype(F32)).astype(BF16)


def hot(ids, size):
    return (ids == lax.broadcasted_iota(jnp.int32, size, 0)).astype(F32).astype(BF16)


def tile_at(i):
    lanes = pl.ds(pl.multiple_of(lax.div(i, C // GROUP) * LANES, LANES), LANES)
    shift = lax.rem(i, C // GROUP) * GROUP

    def rows(block):
        return pl.ds(pl.multiple_of(block * C + shift, GROUP), GROUP)

    return lanes, rows


def fused_kernel(
    count, src_ids, tgt_ids, rot, feats, cots, w0, w1, w2, out,
    gf, gc, gs, w0_in, full1, full2, w0_flip, flip1, flip2, rot_wide, mark_t, mark_s,
    xf, xc, xs, frame, grad_y, y, tgt_sum, src_sum, local_sem, send, recv, *reduce_scratch,
):
    net = Net(send, recv)
    loads = [pltpu.make_async_copy(w0, w0_in, local_sem.at[0])]
    for n, (weights, full) in enumerate(((w1, full1), (w2, full2))):
        k, m = weights.shape[1:]
        for i in range(2):
            for j in range(2):
                loads.append(
                    pltpu.make_async_copy(
                        weights.at[(i + j) % 2],
                        full.at[pl.ds(i * k, k), pl.ds(j * m, m)],
                        local_sem.at[1 + 4 * n + 2 * i + j],
                    )
                )
    mine = [
        pltpu.make_async_copy(feats, gf.at[0, 0, 0], local_sem.at[9]),
        pltpu.make_async_copy(cots, gc.at[0, 0, 0], local_sem.at[10]),
        pltpu.make_async_copy(feats, gs.at[0, 0], local_sem.at[11]),
    ]
    for copy in mine + loads:
        copy.start()
    net.greet()

    first = Flow(net, feats, gf)
    second = Flow(net, cots, gc)
    first.send_own()
    sibling = [net.push(feats, gs.at[0, 1], net.sibling)]
    rows = [net.push(feats, gs.at[4 - step, 0], net.along_high[step]) for step in (1, 3, 2)]
    for copy in mine:
        copy.wait()

    valid = lax.broadcasted_iota(jnp.int32, (1, E), 1) < count[0, 0]
    ids = tgt_ids[...]
    near_x = ((ids >> 6) - net.x) & 3
    near_z = ((ids >> 5) & 1) ^ net.z
    near_y = ((ids >> 3) - net.y) & 3
    ids = near_x * 64 + near_z * 32 + near_y * 8 + (ids & 7)
    mark_t[...] = hot(jnp.where(valid, ids, -1), (TGT, E))
    ids = src_ids[...]
    near_high = ((ids >> 4) - net.high) & 3
    near_core = ((ids >> 3) & 1) ^ net.core
    ids = near_high * 16 + near_core * 8 + (ids & 7)
    mark_s[...] = hot(jnp.where(valid, ids, -1), (SRC, E))
    first.spread(0, 1)
    first.spread(3, 2)
    first.spread(1, 2)
    rot_wide[...] = rot[...].astype(F32)
    first.spread(2, 2)
    second.send_own()
    for step, copy in zip((1, 3, 2), rows):
        copy.wait_recv()
        sibling.append(net.push(gs.at[4 - step, 0], gs.at[4 - step, 1], net.sibling))
    first.relay(0)
    for copy in loads:
        copy.wait()

    def flip_zero(r, carry):
        at = pl.ds(pl.multiple_of(r * BLOCK, BLOCK), BLOCK)
        value = flip(w0_in[at, :])
        for part in range(2):
            to = pl.ds(pl.multiple_of(part * (w0.shape[0] // 2) + r * C, C), C)
            w0_flip[:, to] = value[:, part * C : (part + 1) * C]
        return carry

    def flip_order(weights, full, full_flip):
        k, m = weights.shape[1:]

        def body(r, carry):
            at = pl.ds(pl.multiple_of(r * BLOCK, BLOCK), BLOCK)
            below = pl.ds(pl.multiple_of(r * BLOCK + k, BLOCK), BLOCK)
            full[below, 0:m] = -full[below, 0:m]
            for j in range(2):
                value = flip(full[at, j * m : (j + 1) * m])
                for part in range(2):
                    piece = value[:, part * C : (part + 1) * C]
                    to = pl.ds(pl.multiple_of(part * k + r * C, C), C)
                    full_flip[j * m : (j + 1) * m, to] = piece
                    to = pl.ds(pl.multiple_of(part * k + k // 2 + r * C, C), C)
                    full_flip[(1 - j) * m : (2 - j) * m, to] = -piece if j else piece
            return carry

        lax.fori_loop(0, k // BLOCK, body, 0)

    def gather_some(marks, full, rows, to):
        for p in range(PAIRS):
            both = []
            for j in (2 * p, min(2 * p + 1, COEF - 1)):
                piece = full[:, :, :, j] if len(full.shape) == 6 else full[:, :, j]
                both.append(piece.astype(F32).reshape(rows, C))
            block = jnp.concatenate(both, axis=1).astype(BF16)
            to[2 * p * C : 2 * (p + 1) * C, :] = t_dot(block, marks[...]).astype(BF16)

    def factor_of(entry, lanes):
        return jnp.broadcast_to(rot_wide[entry : entry + 1, lanes], (GROUP, LANES))

    def rotate_from(source, base):
        def rotate(i, carry):
            lanes, rows = tile_at(i)
            for degree in range(5):
                cols = degree_cols(degree)
                values = [source[rows(j), lanes].astype(F32) for j in cols]
                for k in frame_rows(degree):
                    value = None
                    for n, j in enumerate(cols):
                        term = factor_of(k * COEF + j, lanes) * values[n]
                        value = term if value is None else value + term
                    frame[rows(base + k), lanes] = value.astype(BF16)
            return carry

        return rotate

    steps = (E // LANES) * (C // GROUP)
    parts = ((0, 5, w0_in, w0_flip), (5, 8, full1, flip1), (13, 6, full2, flip2))

    def forward_from(side):
        def forward(i, carry):
            at = pl.ds(pl.multiple_of(i * BLOCK, BLOCK), BLOCK)
            for begin, rows, plain, turned in parts:
                into = slice(begin * C, (begin + rows) * C)
                base = side * FRAME * C
                value = dot(
                    turned[:, side * rows * C : (side + 1) * rows * C],
                    frame[base + begin * C : base + (begin + rows) * C, at],
                )
                y[into, at] = y[into, at] + value if side else value
            return carry

        return forward

    rotate_src, rotate_tgt = rotate_from(xs, 0), rotate_from(xf, FRAME)
    forward_src, forward_tgt = forward_from(0), forward_from(1)

    lax.fori_loop(0, w0.shape[0] // BLOCK, flip_zero, 0)
    first.relay(3)
    first.relay(1)
    second.spread(0, 1)
    for copy in sibling:
        copy.wait_recv()
    gather_some(mark_s, gs, SRC, xs)
    first.relay(2)
    for inner in (3, 1, 2):
        second.spread(inner, 2)
    second.relay(0)
    flip_order(w1, full1, flip1)
    second.relay(3)
    second.relay(1)
    lax.fori_loop(0, steps, rotate_src, 0)
    second.relay(2)
    flip_order(w2, full2, flip2)
    lax.fori_loop(0, E // BLOCK, forward_src, 0)
    first.finish()
    gather_some(mark_t, gf, TGT, xf)
    lax.fori_loop(0, steps, rotate_tgt, 0)
    lax.fori_loop(0, E // BLOCK, forward_tgt, 0)
    second.finish()
    gather_some(mark_t, gc, TGT, xc)

    def gate(i, carry):
        lanes, rows = tile_at(i)
        scalar = y[rows(0), lanes]
        gating = jax.nn.sigmoid(scalar)
        slope = gating * (1.0 - gating)
        total = jnp.zeros((GROUP, LANES), F32)
        lowest = None
        for degree in range(5):
            cols = degree_cols(degree)
            values = [xc[rows(j), lanes].astype(F32) for j in cols]
            for k in frame_rows(degree):
                value = None
                for n, j in enumerate(cols):
                    term = factor_of(k * COEF + j, lanes) * values[n]
                    value = term if value is None else value + term
                if k == 0:
                    lowest = value
                else:
                    total = total + value * y[rows(k), lanes]
                    grad_y[rows(k), lanes] = (gating * value).astype(BF16)
        grad_y[rows(0), lanes] = (lowest * (gating + scalar * slope) + total * slope).astype(BF16)
        return carry

    lax.fori_loop(0, steps, gate, 0)

    def backward(i, carry):
        at = pl.ds(pl.multiple_of(i * BLOCK, BLOCK), BLOCK)
        for begin, rows, weights, turned in parts:
            frame[2 * begin * C : 2 * (begin + rows) * C, at] = dot(
                weights[...], grad_y[begin * C : (begin + rows) * C, at]
            ).astype(BF16)
        return carry

    lax.fori_loop(0, E // BLOCK, backward, 0)

    def unrotate(i, carry):
        lanes, rows = tile_at(i)
        for degree in range(5):
            ks = frame_rows(degree)
            of_src = [frame[rows(2 * k), lanes].astype(F32) for k in ks]
            of_tgt = [frame[rows(2 * k + 1), lanes].astype(F32) for k in ks]
            for j in degree_cols(degree):
                sums = [None, None]
                for n, k in enumerate(ks):
                    factor = factor_of(k * COEF + j, lanes)
                    for which, values in enumerate((of_src, of_tgt)):
                        term = factor * values[n]
                        sums[which] = term if sums[which] is None else sums[which] + term
                xs[rows(j), lanes] = sums[0].astype(BF16)
                xf[rows(j), lanes] = sums[1].astype(BF16)
        return carry

    lax.fori_loop(0, steps, unrotate, 0)

    def scatter(marks, grads, to, lead):
        for p in range(PAIRS):
            both = dot_t(marks[...], grads[2 * p * C : 2 * (p + 1) * C, :])
            for j in (2 * p, 2 * p + 1):
                if j < COEF:
                    value = both[:, (j % 2) * C : (j % 2 + 1) * C]
                    value = value.reshape(lead + (A, C)).astype(BF16)
                    if len(lead) == 3:
                        to[:, :, :, j] = value
                    else:
                        to[:, :, j] = value

    scatter(mark_s, xs, src_sum, (4, 2))
    sib = net.push(src_sum.at[:, 1], reduce_scratch[2], net.sibling)
    scatter(mark_t, xf, tgt_sum, (4, 2, 4))
    reduce_body(net, sib, tgt_sum, src_sum, out, reduce_scratch)


def fused(count, src_ids, tgt_ids, rot, feats, cots, w0, w1, w2):
    def buffer(*lead):
        return pltpu.VMEM(lead + (A, C), BF16)

    scratch = [
        buffer(4, 2, 4, COEF),
        buffer(4, 2, 4, COEF),
        buffer(4, 2, COEF),
        pltpu.VMEM(w0.shape, BF16),
        pltpu.VMEM((2 * w1.shape[1], 2 * w1.shape[2]), BF16),
        pltpu.VMEM((2 * w2.shape[1], 2 * w2.shape[2]), BF16),
        pltpu.VMEM(w0.shape[::-1], BF16),
        pltpu.VMEM((2 * w1.shape[2], 2 * w1.shape[1]), BF16),
        pltpu.VMEM((2 * w2.shape[2], 2 * w2.shape[1]), BF16),
        pltpu.VMEM((FRAME * COEF, E), F32),
        pltpu.VMEM((TGT, E), BF16),
        pltpu.VMEM((SRC, E), BF16),
        pltpu.VMEM((PAIRS * 2 * C, E), BF16),
        pltpu.VMEM((PAIRS * 2 * C, E), BF16),
        pltpu.VMEM((PAIRS * 2 * C, E), BF16),
        pltpu.VMEM((FRAME * 2 * C, E), BF16),
        pltpu.VMEM((FRAME * C, E), BF16),
        pltpu.VMEM((FRAME * C, E), F32),
        buffer(4, 2, 4, COEF),
        buffer(4, 2, COEF),
        pltpu.SemaphoreType.DMA((12,)),
        pltpu.SemaphoreType.DMA((MESSAGES,)),
        pltpu.SemaphoreType.DMA((MESSAGES,)),
        buffer(4, COEF),
        buffer(4, COEF),
        buffer(4, COEF),
        pltpu.VMEM((COEF, A, C), F32),
    ]
    for h, lead in ((0, (2, 4)), (1, (4, 2))):
        whole = length(HALVES[h])
        plus, minus = length(QUARTERS[2 * h]), length(QUARTERS[2 * h + 1])
        scratch += [
            buffer(*lead, plus),
            buffer(*lead, minus),
            buffer(*lead, plus),
            buffer(*lead, minus),
            buffer(*lead, whole),
            buffer(*lead, whole),
            buffer(4, 2, whole),
            buffer(4, 2, whole),
        ]
    vmem = pl.BlockSpec(memory_space=pltpu.VMEM)
    hbm = pl.BlockSpec(memory_space=pl.ANY)
    return pl.pallas_call(
        fused_kernel,
        out_shape=jax.ShapeDtypeStruct((COEF, A, C), F32),
        in_specs=[pl.BlockSpec(memory_space=pltpu.SMEM)] + [vmem] * 5 + [hbm] * 3,
        out_specs=vmem,
        scratch_shapes=scratch,
        compiler_params=pltpu.CompilerParams(
            collective_id=0, has_side_effects=True, vmem_limit_bytes=VMEM_LIMIT
        ),
        name="edge_gradients",
    )(count, src_ids, tgt_ids, rot, feats, cots, w0, w1, w2)


def local(node_feats, grad_out, edge_src, edge_tgt, edge_counts, wigner, w_zero, w_one, w_two):
    total = fused(
        edge_counts,
        edge_src[0],
        edge_tgt[0],
        jnp.transpose(wigner[0, 0]),
        jnp.transpose(node_feats, (1, 0, 2)),
        jnp.transpose(grad_out, (1, 0, 2)),
        w_zero,
        w_one,
        w_two,
    )
    return jnp.transpose(total, (1, 0, 2))


def solution(mesh):
    placed = (
        P(("row", "col"), None, None),
        P(("row", "col"), None, None),
        P("row", "col", None),
        P("row", "col", None),
        P("row", "col"),
        P("row", "col", None, None),
        P(),
        P(),
        P(),
    )
    return jax.shard_map(
        local, mesh=mesh, in_specs=placed, out_specs=P(("row", "col"), None, None), check_vma=False
    )
```

```python
import jax
import jax.numpy as jnp
from jax import lax
from jax.experimental import pallas as pl
from jax.experimental.pallas import tpu as pltpu
from jax.sharding import PartitionSpec as P

MESH = pl.DeviceIdType.MESH
F32 = jnp.float32
BF16 = jnp.bfloat16

ROWS = 8
COLS = 32
A = 8
E = 512
C = 128
COEF = 25
PAIRS = 13
FRAME = 19
GROUP = 16
BLOCK = 256
LANES = 128
TGT = COLS * A
SRC = ROWS * A
VMEM_LIMIT = 58 * 1024 * 1024


def frame_rows(degree):
    rows = [degree]
    if degree >= 1:
        rows += [5 + degree - 1, 9 + degree - 1]
    if degree >= 2:
        rows += [13 + degree - 2, 16 + degree - 2]
    return rows


def degree_cols(degree):
    return list(range(degree * degree, (degree + 1) * (degree + 1)))


class Net:
    def __init__(self, send, recv):
        row = lax.axis_index("row")
        col = lax.axis_index("col")
        self.x = x = lax.div(col, 8)
        self.z = z = lax.rem(lax.div(col, 4), 2)
        self.y = y = lax.rem(col, 4)
        self.high = high = lax.div(row, 2)
        self.core = core = lax.rem(row, 2)
        zs = (z, 1 - z)
        self.plane = {}
        for far in (0, 1):
            for step in range(4):
                if step or far:
                    self.plane[0, step, far] = (row, x * 8 + zs[far] * 4 + lax.rem(y + step, 4))
                    self.plane[1, step, far] = (row, lax.rem(x + step, 4) * 8 + zs[far] * 4 + y)
        self.along_high = {
            step: (lax.rem(high + step, 4) * 2 + core, col) for step in (1, 2, 3)
        }
        self.sibling = (high * 2 + 1 - core, col)
        self.send = send
        self.recv = recv
        self.copies = []
        self.sent = 0

    def greet(self):
        barrier = pltpu.get_barrier_semaphore()
        devices = [self.plane[key] for key in self.plane if key != (1, 0, 1)]
        devices += list(self.along_high.values()) + [self.sibling]
        for device in devices:
            pl.semaphore_signal(barrier, inc=1, device_id=device, device_id_type=MESH)
        pl.semaphore_wait(barrier, len(devices))

    def push(self, source, target, device):
        n = len(self.copies)
        copy = pltpu.make_async_remote_copy(
            src_ref=source,
            dst_ref=target,
            send_sem=self.send.at[n],
            recv_sem=self.recv.at[n],
            device_id=device,
            device_id_type=MESH,
        )
        copy.start()
        self.copies.append(copy)
        return copy

    def settle(self, count):
        for copy in self.copies[self.sent : count]:
            copy.wait_send()
        self.sent = count


QUARTERS = ((0, 6), (6, 12), (12, 18), (18, 25))
HALVES = ((0, 12), (12, 25))
MESSAGES = 160


def span(bounds):
    return pl.ds(bounds[0], bounds[1] - bounds[0])


def length(bounds):
    return bounds[1] - bounds[0]


class Reduction:
    def __init__(self, net, tgt, src, out, scratch):
        self.net = net
        self.tgt = tgt
        self.src = src
        self.out = out
        self.row_in, self.row_sum, self.sib_in, self.kept = scratch[:4]
        self.halves = (scratch[4:12], scratch[12:20])
        self.passing = {}
        self.direct = {}

    def toward(self, h, sign):
        return self.net.plane[1 - h, sign, 0]

    def block(self, h, step, piece):
        bounds = QUARTERS[2 * h + piece]
        if h == 0:
            return self.tgt.at[step, :, :, span(bounds)]
        return self.tgt.at[:, :, step, span(bounds)]

    def tail(self, h, piece):
        first = QUARTERS[2 * h][0]
        bounds = QUARTERS[2 * h + piece]
        return pl.ds(bounds[0] - first, length(bounds))

    def start_rows(self):
        self.before = len(self.net.copies)
        self.sib = self.net.push(self.src.at[:, 1], self.sib_in, self.net.sibling)

    def send_rows(self):
        self.sib.wait_recv()
        for high in range(4):
            value = self.src[high, 0].astype(F32) + self.sib_in[high].astype(F32)
            self.row_sum[high] = value.astype(BF16)
        self.rows = [
            self.net.push(
                self.row_sum.at[step], self.row_in.at[4 - step], self.net.along_high[step]
            )
            for step in (2, 1, 3)
        ]

    def start(self, h):
        in_p, in_m, up, um, end_p, end_m = self.halves[h][:6]
        push, block, tail, toward = self.net.push, self.block, self.tail, self.toward
        self.passing[h, 1] = push(block(h, 2, 0), in_p, toward(h, 1))
        self.passing[h, 3] = push(block(h, 2, 1), in_m, toward(h, 3))
        self.direct[h, 1] = push(block(h, 1, 1), end_p.at[:, :, tail(h, 1)], toward(h, 1))
        self.direct[h, 3] = push(block(h, 3, 0), end_m.at[:, :, tail(h, 0)], toward(h, 3))

    def join(self, h):
        in_p, in_m, up, um, end_p, end_m = self.halves[h][:6]
        for sign, piece, came, sums, end in ((1, 0, in_p, up, end_p), (3, 1, in_m, um, end_m)):
            self.passing[h, sign].wait_recv()
            mine = self.block(h, sign, piece)
            for i in range(came.shape[0]):
                for j in range(came.shape[1]):
                    sums[i, j] = (came[i, j].astype(F32) + mine[i, j].astype(F32)).astype(BF16)
            target = end.at[:, :, self.tail(h, piece)]
            self.passing[h, sign] = self.net.push(sums, target, self.toward(h, sign))

    def spread(self, h):
        in_p, in_m, up, um, end_p, end_m, total, ends = self.halves[h]
        for sign in (1, 3):
            self.direct[h, sign].wait_recv()
            self.passing[h, sign].wait_recv()
        at = slice(*HALVES[h])
        final = []
        for step in (2, 1, 3, 0):
            for far in (1, 0):
                if h == 0:
                    mine, one, two = self.tgt[0, far, step, at], end_p[far, step], end_m[far, step]
                else:
                    mine, one, two = self.tgt[step, far, 0, at], end_p[step, far], end_m[step, far]
                value = mine.astype(F32) + one.astype(F32) + two.astype(F32)
                if step or far:
                    total[step, far] = value.astype(BF16)
                    target = ends.at[(4 - step) % 4, far]
                    device = self.net.plane[h, step, far]
                    final.append(self.net.push(total.at[step, far], target, device))
                else:
                    self.kept[at] = value
        return final

    def add_rows(self):
        for copy in self.rows:
            copy.wait_recv()
        value = self.kept[...] + self.row_sum[0].astype(F32)
        for step in (1, 2, 3):
            value = value + self.row_in[step].astype(F32)
        self.kept[...] = value

    def close(self, h, final):
        for copy in final:
            copy.wait_recv()
        ends = self.halves[h][7]
        at = slice(*HALVES[h])
        value = self.kept[at]
        for step in range(4):
            for far in (0, 1):
                if step or far:
                    value = value + ends[step, far].astype(F32)
        self.out[at] = value


class Flow:
    def __init__(self, net, own, full):
        self.net = net
        self.own = own
        self.full = full
        self.arrivals = {}
        self.outer = {}
        self.last = []

    def place(self, h, outer, inner, z, bounds):
        z_now = slice(0, 2) if z == 2 else z
        x, y = (outer, inner) if h == 0 else (inner, outer)
        return self.full.at[x, z_now, y, span(bounds)]

    def send_own(self):
        for step, far in ((0, 1), (1, 0), (3, 0), (1, 1), (3, 1), (2, 0), (2, 1)):
            for h in (0, 1):
                inner = (4 - step) % 4
                self.arrivals[h, inner, far] = self.net.push(
                    self.own.at[span(HALVES[h])],
                    self.place(h, 0, inner, far, HALVES[h]),
                    self.net.plane[h, step, far],
                )
            if step == 3 and not far:
                self.spread(0, 0)

    def spread(self, inner, z):
        for h in (0, 1):
            for far in (0, 1) if z == 2 else (z,):
                if inner or far:
                    self.arrivals[h, inner, far].wait_recv()
            source = self.place(h, 0, inner, z, HALVES[h])
            if (inner, z) == (0, 0):
                source = self.own.at[span(HALVES[h])]
            for sign in (1, 3):
                target = self.place(h, 4 - sign, inner, z, HALVES[h])
                copy = self.net.push(source, target, self.net.plane[1 - h, sign, 0])
                self.outer.setdefault((h, inner, sign), []).append(copy)

    def relay(self, inner):
        for sign, quarter in ((1, 0), (3, 1)):
            for h in (0, 1):
                for copy in self.outer[h, inner, sign]:
                    copy.wait_recv()
                bounds = QUARTERS[2 * h + quarter]
                copy = self.net.push(
                    self.place(h, 4 - sign, inner, 2, bounds),
                    self.place(h, 2, inner, 2, bounds),
                    self.net.plane[1 - h, sign, 0],
                )
                self.last.append(copy)

    def finish(self):
        for copy in self.last:
            copy.wait_recv()


def dot(x, y):
    return jnp.dot(x, y, preferred_element_type=F32)


def dot_t(x, y):
    return lax.dot_general(x, y, (((1,), (1,)), ((), ())), preferred_element_type=F32)


def t_dot(x, y):
    return lax.dot_general(x, y, (((0,), (0,)), ((), ())), preferred_element_type=F32)


def flip(value):
    return jnp.transpose(value.astype(F32)).astype(BF16)


def hot(ids, size):
    return (ids == lax.broadcasted_iota(jnp.int32, size, 0)).astype(F32).astype(BF16)


def tile_at(i):
    lanes = pl.ds(pl.multiple_of(lax.div(i, C // GROUP) * LANES, LANES), LANES)
    shift = lax.rem(i, C // GROUP) * GROUP

    def rows(block):
        return pl.ds(pl.multiple_of(block * C + shift, GROUP), GROUP)

    return lanes, rows


def fused_kernel(
    count, src_ids, tgt_ids, rot, feats, cots, w0, w1, w2, out,
    gf, gc, gs, w0_in, full1, full2, w0_flip, flip1, flip2, rot_wide, mark_t, mark_s,
    xf, xc, xs, frame, grad_y, y, tgt_sum, src_sum, local_sem, send, recv, *reduce_scratch,
):
    net = Net(send, recv)
    loads = [pltpu.make_async_copy(w0, w0_in, local_sem.at[0])]
    for n, (weights, full) in enumerate(((w1, full1), (w2, full2))):
        k, m = weights.shape[1:]
        for i in range(2):
            for j in range(2):
                loads.append(
                    pltpu.make_async_copy(
                        weights.at[(i + j) % 2],
                        full.at[pl.ds(i * k, k), pl.ds(j * m, m)],
                        local_sem.at[1 + 4 * n + 2 * i + j],
                    )
                )
    mine = [
        pltpu.make_async_copy(feats, gf.at[0, 0, 0], local_sem.at[9]),
        pltpu.make_async_copy(cots, gc.at[0, 0, 0], local_sem.at[10]),
        pltpu.make_async_copy(feats, gs.at[0, 0], local_sem.at[11]),
    ]
    for copy in mine + loads:
        copy.start()
    net.greet()

    first = Flow(net, feats, gf)
    second = Flow(net, cots, gc)
    first.send_own()
    sibling = [net.push(feats, gs.at[0, 1], net.sibling)]
    rows = [net.push(feats, gs.at[4 - step, 0], net.along_high[step]) for step in (1, 3, 2)]
    for copy in mine:
        copy.wait()

    valid = lax.broadcasted_iota(jnp.int32, (1, E), 1) < count[0, 0]
    ids = tgt_ids[...]
    near_x = ((ids >> 6) - net.x) & 3
    near_z = ((ids >> 5) & 1) ^ net.z
    near_y = ((ids >> 3) - net.y) & 3
    ids = near_x * 64 + near_z * 32 + near_y * 8 + (ids & 7)
    mark_t[...] = hot(jnp.where(valid, ids, -1), (TGT, E))
    ids = src_ids[...]
    near_high = ((ids >> 4) - net.high) & 3
    near_core = ((ids >> 3) & 1) ^ net.core
    ids = near_high * 16 + near_core * 8 + (ids & 7)
    mark_s[...] = hot(jnp.where(valid, ids, -1), (SRC, E))
    first.spread(0, 1)
    rot_wide[...] = rot[...].astype(F32)
    for inner in (3, 1, 2):
        first.spread(inner, 2)
    second.send_own()

    def flip_zero(r, carry):
        at = pl.ds(pl.multiple_of(r * BLOCK, BLOCK), BLOCK)
        value = flip(w0_in[at, :])
        for part in range(2):
            to = pl.ds(pl.multiple_of(part * (w0.shape[0] // 2) + r * C, C), C)
            w0_flip[:, to] = value[:, part * C : (part + 1) * C]
        return carry

    def flip_order(weights, full, full_flip):
        k, m = weights.shape[1:]

        def body(r, carry):
            at = pl.ds(pl.multiple_of(r * BLOCK, BLOCK), BLOCK)
            below = pl.ds(pl.multiple_of(r * BLOCK + k, BLOCK), BLOCK)
            full[below, 0:m] = -full[below, 0:m]
            for j in range(2):
                value = flip(full[at, j * m : (j + 1) * m])
                for part in range(2):
                    piece = value[:, part * C : (part + 1) * C]
                    to = pl.ds(pl.multiple_of(part * k + r * C, C), C)
                    full_flip[j * m : (j + 1) * m, to] = piece
                    to = pl.ds(pl.multiple_of(part * k + k // 2 + r * C, C), C)
                    full_flip[(1 - j) * m : (2 - j) * m, to] = -piece if j else piece
            return carry

        lax.fori_loop(0, k // BLOCK, body, 0)

    def gather_some(marks, full, rows, to):
        for p in range(PAIRS):
            both = []
            for j in (2 * p, min(2 * p + 1, COEF - 1)):
                piece = full[:, :, :, j] if len(full.shape) == 6 else full[:, :, j]
                both.append(piece.astype(F32).reshape(rows, C))
            block = jnp.concatenate(both, axis=1).astype(BF16)
            to[2 * p * C : 2 * (p + 1) * C, :] = t_dot(block, marks[...]).astype(BF16)

    def factor_of(entry, lanes):
        return jnp.broadcast_to(rot_wide[entry : entry + 1, lanes], (GROUP, LANES))

    def rotate_from(source, base):
        def rotate(i, carry):
            lanes, rows = tile_at(i)
            for degree in range(5):
                cols = degree_cols(degree)
                values = [source[rows(j), lanes].astype(F32) for j in cols]
                for k in frame_rows(degree):
                    value = None
                    for n, j in enumerate(cols):
                        term = factor_of(k * COEF + j, lanes) * values[n]
                        value = term if value is None else value + term
                    frame[rows(base + k), lanes] = value.astype(BF16)
            return carry

        return rotate

    steps = (E // LANES) * (C // GROUP)
    parts = ((0, 5, w0_in, w0_flip), (5, 8, full1, flip1), (13, 6, full2, flip2))

    def forward_from(side):
        def forward(i, carry):
            at = pl.ds(pl.multiple_of(i * BLOCK, BLOCK), BLOCK)
            for begin, rows, plain, turned in parts:
                into = slice(begin * C, (begin + rows) * C)
                base = side * FRAME * C
                value = dot(
                    turned[:, side * rows * C : (side + 1) * rows * C],
                    frame[base + begin * C : base + (begin + rows) * C, at],
                )
                y[into, at] = y[into, at] + value if side else value
            return carry

        return forward

    rotate_src, rotate_tgt = rotate_from(xs, 0), rotate_from(xf, FRAME)
    forward_src, forward_tgt = forward_from(0), forward_from(1)

    for copy in loads:
        copy.wait()
    lax.fori_loop(0, w0.shape[0] // BLOCK, flip_zero, 0)
    first.relay(0)
    for step, copy in zip((1, 3, 2), rows):
        copy.wait_recv()
        sibling.append(net.push(gs.at[4 - step, 0], gs.at[4 - step, 1], net.sibling))
    first.relay(3)
    first.relay(1)
    second.spread(0, 1)
    flip_order(w2, full2, flip2)
    first.relay(2)
    for inner in (3, 1, 2):
        second.spread(inner, 2)
    flip_order(w1, full1, flip1)
    second.relay(0)
    for copy in sibling:
        copy.wait_recv()
    gather_some(mark_s, gs, SRC, xs)
    second.relay(3)
    second.relay(1)
    lax.fori_loop(0, steps, rotate_src, 0)
    second.relay(2)
    lax.fori_loop(0, E // BLOCK, forward_src, 0)
    first.finish()
    gather_some(mark_t, gf, TGT, xf)
    lax.fori_loop(0, steps, rotate_tgt, 0)
    lax.fori_loop(0, E // BLOCK, forward_tgt, 0)
    second.finish()
    gather_some(mark_t, gc, TGT, xc)

    def gate(i, carry):
        lanes, rows = tile_at(i)
        scalar = y[rows(0), lanes]
        gating = jax.nn.sigmoid(scalar)
        slope = gating * (1.0 - gating)
        total = jnp.zeros((GROUP, LANES), F32)
        lowest = None
        for degree in range(5):
            cols = degree_cols(degree)
            values = [xc[rows(j), lanes].astype(F32) for j in cols]
            for k in frame_rows(degree):
                value = None
                for n, j in enumerate(cols):
                    term = factor_of(k * COEF + j, lanes) * values[n]
                    value = term if value is None else value + term
                if k == 0:
                    lowest = value
                else:
                    total = total + value * y[rows(k), lanes]
                    grad_y[rows(k), lanes] = (gating * value).astype(BF16)
        grad_y[rows(0), lanes] = (lowest * (gating + scalar * slope) + total * slope).astype(BF16)
        return carry

    lax.fori_loop(0, steps, gate, 0)

    def backward(i, carry):
        at = pl.ds(pl.multiple_of(i * BLOCK, BLOCK), BLOCK)
        for begin, rows, weights, turned in parts:
            frame[2 * begin * C : 2 * (begin + rows) * C, at] = dot(
                weights[...], grad_y[begin * C : (begin + rows) * C, at]
            ).astype(BF16)
        return carry

    lax.fori_loop(0, E // BLOCK, backward, 0)

    def unrotate_into(grads, side, first_j, last_j):
        def unrotate(i, carry):
            lanes, rows = tile_at(i)
            for degree in range(5):
                js = [j for j in degree_cols(degree) if first_j <= j < last_j]
                if not js:
                    continue
                ks = frame_rows(degree)
                values = [frame[rows(2 * k + side), lanes].astype(F32) for k in ks]
                for j in js:
                    value = None
                    for n, k in enumerate(ks):
                        term = factor_of(k * COEF + j, lanes) * values[n]
                        value = term if value is None else value + term
                    grads[rows(j), lanes] = value.astype(BF16)
            return carry

        return unrotate

    def scatter(marks, grads, to, lead, first_j, last_j):
        for p in range(first_j // 2, (last_j + 1) // 2):
            both = dot_t(marks[...], grads[2 * p * C : 2 * (p + 1) * C, :])
            for j in (2 * p, 2 * p + 1):
                if j < COEF:
                    value = both[:, (j % 2) * C : (j % 2 + 1) * C]
                    value = value.reshape(lead + (A, C)).astype(BF16)
                    if len(lead) == 3:
                        to[:, :, :, j] = value
                    else:
                        to[:, :, j] = value

    unrotate_src = unrotate_into(xs, 0, 0, COEF)
    unrotate_high = unrotate_into(xf, 1, *HALVES[1])
    unrotate_low = unrotate_into(xf, 1, *HALVES[0])
    back = Reduction(net, tgt_sum, src_sum, out, reduce_scratch)
    lax.fori_loop(0, steps, unrotate_src, 0)
    scatter(mark_s, xs, src_sum, (4, 2), 0, COEF)
    back.start_rows()
    lax.fori_loop(0, steps, unrotate_high, 0)
    scatter(mark_t, xf, tgt_sum, (4, 2, 4), *HALVES[1])
    back.start(1)
    lax.fori_loop(0, steps, unrotate_low, 0)
    back.send_rows()
    scatter(mark_t, xf, tgt_sum, (4, 2, 4), *HALVES[0])
    back.start(0)
    back.join(1)
    net.settle(back.before)
    back.join(0)
    final_high = back.spread(1)
    final_low = back.spread(0)
    back.add_rows()
    net.settle(len(net.copies))
    back.close(1, final_high)
    back.close(0, final_low)


def fused(count, src_ids, tgt_ids, rot, feats, cots, w0, w1, w2):
    def buffer(*lead):
        return pltpu.VMEM(lead + (A, C), BF16)

    scratch = [
        buffer(4, 2, 4, COEF),
        buffer(4, 2, 4, COEF),
        buffer(4, 2, COEF),
        pltpu.VMEM(w0.shape, BF16),
        pltpu.VMEM((2 * w1.shape[1], 2 * w1.shape[2]), BF16),
        pltpu.VMEM((2 * w2.shape[1], 2 * w2.shape[2]), BF16),
        pltpu.VMEM(w0.shape[::-1], BF16),
        pltpu.VMEM((2 * w1.shape[2], 2 * w1.shape[1]), BF16),
        pltpu.VMEM((2 * w2.shape[2], 2 * w2.shape[1]), BF16),
        pltpu.VMEM((FRAME * COEF, E), F32),
        pltpu.VMEM((TGT, E), BF16),
        pltpu.VMEM((SRC, E), BF16),
        pltpu.VMEM((PAIRS * 2 * C, E), BF16),
        pltpu.VMEM((PAIRS * 2 * C, E), BF16),
        pltpu.VMEM((PAIRS * 2 * C, E), BF16),
        pltpu.VMEM((FRAME * 2 * C, E), BF16),
        pltpu.VMEM((FRAME * C, E), BF16),
        pltpu.VMEM((FRAME * C, E), F32),
        buffer(4, 2, 4, COEF),
        buffer(4, 2, COEF),
        pltpu.SemaphoreType.DMA((12,)),
        pltpu.SemaphoreType.DMA((MESSAGES,)),
        pltpu.SemaphoreType.DMA((MESSAGES,)),
        buffer(4, COEF),
        buffer(4, COEF),
        buffer(4, COEF),
        pltpu.VMEM((COEF, A, C), F32),
    ]
    for h, lead in ((0, (2, 4)), (1, (4, 2))):
        whole = length(HALVES[h])
        plus, minus = length(QUARTERS[2 * h]), length(QUARTERS[2 * h + 1])
        scratch += [
            buffer(*lead, plus),
            buffer(*lead, minus),
            buffer(*lead, plus),
            buffer(*lead, minus),
            buffer(*lead, whole),
            buffer(*lead, whole),
            buffer(4, 2, whole),
            buffer(4, 2, whole),
        ]
    vmem = pl.BlockSpec(memory_space=pltpu.VMEM)
    hbm = pl.BlockSpec(memory_space=pl.ANY)
    return pl.pallas_call(
        fused_kernel,
        out_shape=jax.ShapeDtypeStruct((COEF, A, C), F32),
        in_specs=[pl.BlockSpec(memory_space=pltpu.SMEM)] + [vmem] * 5 + [hbm] * 3,
        out_specs=vmem,
        scratch_shapes=scratch,
        compiler_params=pltpu.CompilerParams(
            collective_id=0, has_side_effects=True, vmem_limit_bytes=VMEM_LIMIT
        ),
        name="edge_gradients",
    )(count, src_ids, tgt_ids, rot, feats, cots, w0, w1, w2)


def local(node_feats, grad_out, edge_src, edge_tgt, edge_counts, wigner, w_zero, w_one, w_two):
    total = fused(
        edge_counts,
        edge_src[0],
        edge_tgt[0],
        jnp.transpose(wigner[0, 0]),
        jnp.transpose(node_feats, (1, 0, 2)),
        jnp.transpose(grad_out, (1, 0, 2)),
        w_zero,
        w_one,
        w_two,
    )
    return jnp.transpose(total, (1, 0, 2))


def solution(mesh):
    placed = (
        P(("row", "col"), None, None),
        P(("row", "col"), None, None),
        P("row", "col", None),
        P("row", "col", None),
        P("row", "col"),
        P("row", "col", None, None),
        P(),
        P(),
        P(),
    )
    return jax.shard_map(
        local, mesh=mesh, in_specs=placed, out_specs=P(("row", "col"), None, None), check_vma=False
    )
```

```python
import jax
import jax.numpy as jnp
from jax import lax
from jax.experimental import pallas as pl
from jax.experimental.pallas import tpu as pltpu
from jax.sharding import PartitionSpec as P

MESH = pl.DeviceIdType.MESH
F32 = jnp.float32
BF16 = jnp.bfloat16

ROWS = 8
COLS = 32
A = 8
E = 512
C = 128
COEF = 25
PAIRS = 13
FRAME = 19
GROUP = 16
BLOCK = 256
LANES = 128
TGT = COLS * A
SRC = ROWS * A
VMEM_LIMIT = 58 * 1024 * 1024


def frame_rows(degree):
    rows = [degree]
    if degree >= 1:
        rows += [5 + degree - 1, 9 + degree - 1]
    if degree >= 2:
        rows += [13 + degree - 2, 16 + degree - 2]
    return rows


def degree_cols(degree):
    return list(range(degree * degree, (degree + 1) * (degree + 1)))


class Net:
    def __init__(self, send, recv):
        row = lax.axis_index("row")
        col = lax.axis_index("col")
        self.x = x = lax.div(col, 8)
        self.z = z = lax.rem(lax.div(col, 4), 2)
        self.y = y = lax.rem(col, 4)
        self.high = high = lax.div(row, 2)
        self.core = core = lax.rem(row, 2)
        zs = (z, 1 - z)
        self.plane = {}
        for far in (0, 1):
            for step in range(4):
                if step or far:
                    self.plane[0, step, far] = (row, x * 8 + zs[far] * 4 + lax.rem(y + step, 4))
                    self.plane[1, step, far] = (row, lax.rem(x + step, 4) * 8 + zs[far] * 4 + y)
        self.along_high = {
            step: (lax.rem(high + step, 4) * 2 + core, col) for step in (1, 2, 3)
        }
        self.sibling = (high * 2 + 1 - core, col)
        self.send = send
        self.recv = recv
        self.copies = []
        self.sent = 0

    def greet(self):
        barrier = pltpu.get_barrier_semaphore()
        devices = [self.plane[key] for key in self.plane if key != (1, 0, 1)]
        devices += list(self.along_high.values()) + [self.sibling]
        for device in devices:
            pl.semaphore_signal(barrier, inc=1, device_id=device, device_id_type=MESH)
        pl.semaphore_wait(barrier, len(devices))

    def push(self, source, target, device):
        n = len(self.copies)
        copy = pltpu.make_async_remote_copy(
            src_ref=source,
            dst_ref=target,
            send_sem=self.send.at[n],
            recv_sem=self.recv.at[n],
            device_id=device,
            device_id_type=MESH,
        )
        copy.start()
        self.copies.append(copy)
        return copy

    def settle(self, count):
        for copy in self.copies[self.sent : count]:
            copy.wait_send()
        self.sent = count


QUARTERS = ((0, 6), (6, 12), (12, 18), (18, 25))
HALVES = ((0, 12), (12, 25))
MESSAGES = 160


def span(bounds):
    return pl.ds(bounds[0], bounds[1] - bounds[0])


def length(bounds):
    return bounds[1] - bounds[0]


class Reduction:
    def __init__(self, net, tgt, src, out, scratch):
        self.net = net
        self.tgt = tgt
        self.src = src
        self.out = out
        self.row_in, self.row_sum, self.sib_in, self.kept = scratch[:4]
        self.halves = (scratch[4:12], scratch[12:20])
        self.passing = {}
        self.direct = {}

    def toward(self, h, sign):
        return self.net.plane[1 - h, sign, 0]

    def block(self, h, step, piece):
        bounds = QUARTERS[2 * h + piece]
        if h == 0:
            return self.tgt.at[step, :, :, span(bounds)]
        return self.tgt.at[:, :, step, span(bounds)]

    def tail(self, h, piece):
        first = QUARTERS[2 * h][0]
        bounds = QUARTERS[2 * h + piece]
        return pl.ds(bounds[0] - first, length(bounds))

    def start_rows(self):
        self.before = len(self.net.copies)
        self.sib = self.net.push(self.src.at[:, 1], self.sib_in, self.net.sibling)

    def send_rows(self):
        self.sib.wait_recv()
        for high in range(4):
            value = self.src[high, 0].astype(F32) + self.sib_in[high].astype(F32)
            self.row_sum[high] = value.astype(BF16)
        self.rows = [
            self.net.push(
                self.row_sum.at[step], self.row_in.at[4 - step], self.net.along_high[step]
            )
            for step in (2, 1, 3)
        ]

    def start(self, h):
        in_p, in_m, up, um, end_p, end_m = self.halves[h][:6]
        push, block, tail, toward = self.net.push, self.block, self.tail, self.toward
        self.passing[h, 1] = push(block(h, 2, 0), in_p, toward(h, 1))
        self.passing[h, 3] = push(block(h, 2, 1), in_m, toward(h, 3))
        self.direct[h, 1] = push(block(h, 1, 1), end_p.at[:, :, tail(h, 1)], toward(h, 1))
        self.direct[h, 3] = push(block(h, 3, 0), end_m.at[:, :, tail(h, 0)], toward(h, 3))

    def join(self, h):
        in_p, in_m, up, um, end_p, end_m = self.halves[h][:6]
        for sign, piece, came, sums, end in ((1, 0, in_p, up, end_p), (3, 1, in_m, um, end_m)):
            self.passing[h, sign].wait_recv()
            mine = self.block(h, sign, piece)
            for i in range(came.shape[0]):
                for j in range(came.shape[1]):
                    sums[i, j] = (came[i, j].astype(F32) + mine[i, j].astype(F32)).astype(BF16)
            target = end.at[:, :, self.tail(h, piece)]
            self.passing[h, sign] = self.net.push(sums, target, self.toward(h, sign))

    def spread(self, h):
        in_p, in_m, up, um, end_p, end_m, total, ends = self.halves[h]
        for sign in (1, 3):
            self.direct[h, sign].wait_recv()
            self.passing[h, sign].wait_recv()
        at = slice(*HALVES[h])
        final = []
        for step in (2, 1, 3, 0):
            for far in (1, 0):
                if h == 0:
                    mine, one, two = self.tgt[0, far, step, at], end_p[far, step], end_m[far, step]
                else:
                    mine, one, two = self.tgt[step, far, 0, at], end_p[step, far], end_m[step, far]
                value = mine.astype(F32) + one.astype(F32) + two.astype(F32)
                if step or far:
                    total[step, far] = value.astype(BF16)
                    target = ends.at[(4 - step) % 4, far]
                    device = self.net.plane[h, step, far]
                    final.append(self.net.push(total.at[step, far], target, device))
                else:
                    self.kept[at] = value
        return final

    def add_rows(self):
        for copy in self.rows:
            copy.wait_recv()
        value = self.kept[...] + self.row_sum[0].astype(F32)
        for step in (1, 2, 3):
            value = value + self.row_in[step].astype(F32)
        self.kept[...] = value

    def close(self, h, final):
        for copy in final:
            copy.wait_recv()
        ends = self.halves[h][7]
        at = slice(*HALVES[h])
        value = self.kept[at]
        for step in range(4):
            for far in (0, 1):
                if step or far:
                    value = value + ends[step, far].astype(F32)
        self.out[at] = value


class Flow:
    def __init__(self, net, own, full):
        self.net = net
        self.own = own
        self.full = full
        self.arrivals = {}
        self.outer = {}
        self.last = []

    def place(self, h, outer, inner, z, bounds):
        z_now = slice(0, 2) if z == 2 else z
        x, y = (outer, inner) if h == 0 else (inner, outer)
        return self.full.at[x, z_now, y, span(bounds)]

    def send_own(self):
        for step, far in ((0, 1), (1, 0), (3, 0), (1, 1), (3, 1), (2, 0), (2, 1)):
            for h in (0, 1):
                inner = (4 - step) % 4
                self.arrivals[h, inner, far] = self.net.push(
                    self.own.at[span(HALVES[h])],
                    self.place(h, 0, inner, far, HALVES[h]),
                    self.net.plane[h, step, far],
                )
            if step == 3 and not far:
                self.spread(0, 0)

    def spread(self, inner, z):
        for h in (0, 1):
            for far in (0, 1) if z == 2 else (z,):
                if inner or far:
                    self.arrivals[h, inner, far].wait_recv()
            source = self.place(h, 0, inner, z, HALVES[h])
            if (inner, z) == (0, 0):
                source = self.own.at[span(HALVES[h])]
            for sign in (1, 3):
                target = self.place(h, 4 - sign, inner, z, HALVES[h])
                copy = self.net.push(source, target, self.net.plane[1 - h, sign, 0])
                self.outer.setdefault((h, inner, sign), []).append(copy)

    def relay(self, inner):
        for sign, quarter in ((1, 0), (3, 1)):
            for h in (0, 1):
                for copy in self.outer[h, inner, sign]:
                    copy.wait_recv()
                bounds = QUARTERS[2 * h + quarter]
                copy = self.net.push(
                    self.place(h, 4 - sign, inner, 2, bounds),
                    self.place(h, 2, inner, 2, bounds),
                    self.net.plane[1 - h, sign, 0],
                )
                self.last.append(copy)

    def finish(self):
        for copy in self.last:
            copy.wait_recv()


def dot(x, y):
    return jnp.dot(x, y, preferred_element_type=F32)


def dot_t(x, y):
    return lax.dot_general(x, y, (((1,), (1,)), ((), ())), preferred_element_type=F32)


def t_dot(x, y):
    return lax.dot_general(x, y, (((0,), (0,)), ((), ())), preferred_element_type=F32)


def flip(value):
    return jnp.transpose(value.astype(F32)).astype(BF16)


def hot(ids, size):
    return (ids == lax.broadcasted_iota(jnp.int32, size, 0)).astype(F32).astype(BF16)


def tile_at(i):
    lanes = pl.ds(pl.multiple_of(lax.div(i, C // GROUP) * LANES, LANES), LANES)
    shift = lax.rem(i, C // GROUP) * GROUP

    def rows(block):
        return pl.ds(pl.multiple_of(block * C + shift, GROUP), GROUP)

    return lanes, rows


def fused_kernel(
    count, src_ids, tgt_ids, rot, feats, cots, w0, w1, w2, out,
    g, gs, w0_in, full1, full2, w0_flip, flip1, flip2, rot_wide, mark_t, mark_s,
    xf, xc, xs, frame, grad_y, y, tgt_sum, src_sum, local_sem, send, recv, *reduce_scratch,
):
    net = Net(send, recv)
    loads = [pltpu.make_async_copy(w0, w0_in, local_sem.at[0])]
    for n, (weights, full) in enumerate(((w1, full1), (w2, full2))):
        k, m = weights.shape[1:]
        for i in range(2):
            for j in range(2):
                loads.append(
                    pltpu.make_async_copy(
                        weights.at[(i + j) % 2],
                        full.at[pl.ds(i * k, k), pl.ds(j * m, m)],
                        local_sem.at[1 + 4 * n + 2 * i + j],
                    )
                )
    mine = [
        pltpu.make_async_copy(feats, gs.at[0, 0], local_sem.at[9]),
    ]
    for copy in mine + loads:
        copy.start()
    g[0, 0, 0, :, :, 0:C] = feats[...]
    g[0, 0, 0, :, :, C : 2 * C] = cots[...]
    net.greet()

    flow = Flow(net, g.at[0, 0, 0], g)
    flow.send_own()
    sibling = [net.push(feats, gs.at[0, 1], net.sibling)]
    rows = [net.push(feats, gs.at[4 - step, 0], net.along_high[step]) for step in (1, 3, 2)]
    for copy in mine:
        copy.wait()

    valid = lax.broadcasted_iota(jnp.int32, (1, E), 1) < count[0, 0]
    ids = tgt_ids[...]
    near_x = ((ids >> 6) - net.x) & 3
    near_z = ((ids >> 5) & 1) ^ net.z
    near_y = ((ids >> 3) - net.y) & 3
    ids = near_x * 64 + near_z * 32 + near_y * 8 + (ids & 7)
    mark_t[...] = hot(jnp.where(valid, ids, -1), (TGT, E))
    ids = src_ids[...]
    near_high = ((ids >> 4) - net.high) & 3
    near_core = ((ids >> 3) & 1) ^ net.core
    ids = near_high * 16 + near_core * 8 + (ids & 7)
    mark_s[...] = hot(jnp.where(valid, ids, -1), (SRC, E))
    flow.spread(0, 1)
    rot_wide[...] = rot[...].astype(F32)
    for inner in (3, 1, 2):
        flow.spread(inner, 2)

    def flip_zero(r, carry):
        at = pl.ds(pl.multiple_of(r * BLOCK, BLOCK), BLOCK)
        value = flip(w0_in[at, :])
        for part in range(2):
            to = pl.ds(pl.multiple_of(part * (w0.shape[0] // 2) + r * C, C), C)
            w0_flip[:, to] = value[:, part * C : (part + 1) * C]
        return carry

    def flip_order(weights, full, full_flip):
        k, m = weights.shape[1:]

        def body(r, carry):
            at = pl.ds(pl.multiple_of(r * BLOCK, BLOCK), BLOCK)
            below = pl.ds(pl.multiple_of(r * BLOCK + k, BLOCK), BLOCK)
            full[below, 0:m] = -full[below, 0:m]
            for j in range(2):
                value = flip(full[at, j * m : (j + 1) * m])
                for part in range(2):
                    piece = value[:, part * C : (part + 1) * C]
                    to = pl.ds(pl.multiple_of(part * k + r * C, C), C)
                    full_flip[j * m : (j + 1) * m, to] = piece
                    to = pl.ds(pl.multiple_of(part * k + k // 2 + r * C, C), C)
                    full_flip[(1 - j) * m : (2 - j) * m, to] = -piece if j else piece
            return carry

        lax.fori_loop(0, k // BLOCK, body, 0)

    def gather_src():
        for p in range(PAIRS):
            both = [
                gs[:, :, j].astype(F32).reshape(SRC, C) for j in (2 * p, min(2 * p + 1, COEF - 1))
            ]
            block = jnp.concatenate(both, axis=1).astype(BF16)
            xs[2 * p * C : 2 * (p + 1) * C, :] = t_dot(block, mark_s[...]).astype(BF16)

    def gather_tgt():
        for j in range(COEF):
            block = g[:, :, :, j].astype(F32).reshape(TGT, 2 * C).astype(BF16)
            both = t_dot(block, mark_t[...]).astype(BF16)
            xf[j * C : (j + 1) * C, :] = both[0:C]
            xc[j * C : (j + 1) * C, :] = both[C : 2 * C]

    def factor_of(entry, lanes):
        return jnp.broadcast_to(rot_wide[entry : entry + 1, lanes], (GROUP, LANES))

    def rotate_from(source, base):
        def rotate(i, carry):
            lanes, rows = tile_at(i)
            for degree in range(5):
                cols = degree_cols(degree)
                values = [source[rows(j), lanes].astype(F32) for j in cols]
                for k in frame_rows(degree):
                    value = None
                    for n, j in enumerate(cols):
                        term = factor_of(k * COEF + j, lanes) * values[n]
                        value = term if value is None else value + term
                    frame[rows(base + k), lanes] = value.astype(BF16)
            return carry

        return rotate

    steps = (E // LANES) * (C // GROUP)
    parts = ((0, 5, w0_in, w0_flip), (5, 8, full1, flip1), (13, 6, full2, flip2))

    def forward_from(side):
        def forward(i, carry):
            at = pl.ds(pl.multiple_of(i * BLOCK, BLOCK), BLOCK)
            for begin, rows, plain, turned in parts:
                into = slice(begin * C, (begin + rows) * C)
                base = side * FRAME * C
                value = dot(
                    turned[:, side * rows * C : (side + 1) * rows * C],
                    frame[base + begin * C : base + (begin + rows) * C, at],
                )
                y[into, at] = y[into, at] + value if side else value
            return carry

        return forward

    rotate_src, rotate_tgt = rotate_from(xs, 0), rotate_from(xf, FRAME)
    forward_src, forward_tgt = forward_from(0), forward_from(1)

    for copy in loads:
        copy.wait()
    lax.fori_loop(0, w0.shape[0] // BLOCK, flip_zero, 0)
    flow.relay(0)
    for step, copy in zip((1, 3, 2), rows):
        copy.wait_recv()
        sibling.append(net.push(gs.at[4 - step, 0], gs.at[4 - step, 1], net.sibling))
    flip_order(w2, full2, flip2)
    flow.relay(3)
    flow.relay(1)
    flip_order(w1, full1, flip1)
    for copy in sibling:
        copy.wait_recv()
    gather_src()
    flow.relay(2)
    lax.fori_loop(0, steps, rotate_src, 0)
    lax.fori_loop(0, E // BLOCK, forward_src, 0)
    flow.finish()
    gather_tgt()
    lax.fori_loop(0, steps, rotate_tgt, 0)
    lax.fori_loop(0, E // BLOCK, forward_tgt, 0)

    def gate(i, carry):
        lanes, rows = tile_at(i)
        scalar = y[rows(0), lanes]
        gating = jax.nn.sigmoid(scalar)
        slope = gating * (1.0 - gating)
        total = jnp.zeros((GROUP, LANES), F32)
        lowest = None
        for degree in range(5):
            cols = degree_cols(degree)
            values = [xc[rows(j), lanes].astype(F32) for j in cols]
            for k in frame_rows(degree):
                value = None
                for n, j in enumerate(cols):
                    term = factor_of(k * COEF + j, lanes) * values[n]
                    value = term if value is None else value + term
                if k == 0:
                    lowest = value
                else:
                    total = total + value * y[rows(k), lanes]
                    grad_y[rows(k), lanes] = (gating * value).astype(BF16)
        grad_y[rows(0), lanes] = (lowest * (gating + scalar * slope) + total * slope).astype(BF16)
        return carry

    lax.fori_loop(0, steps, gate, 0)

    def backward(i, carry):
        at = pl.ds(pl.multiple_of(i * BLOCK, BLOCK), BLOCK)
        for begin, rows, weights, turned in parts:
            frame[2 * begin * C : 2 * (begin + rows) * C, at] = dot(
                weights[...], grad_y[begin * C : (begin + rows) * C, at]
            ).astype(BF16)
        return carry

    lax.fori_loop(0, E // BLOCK, backward, 0)

    def unrotate_into(grads, side, first_j, last_j):
        def unrotate(i, carry):
            lanes, rows = tile_at(i)
            for degree in range(5):
                js = [j for j in degree_cols(degree) if first_j <= j < last_j]
                if not js:
                    continue
                ks = frame_rows(degree)
                values = [frame[rows(2 * k + side), lanes].astype(F32) for k in ks]
                for j in js:
                    value = None
                    for n, k in enumerate(ks):
                        term = factor_of(k * COEF + j, lanes) * values[n]
                        value = term if value is None else value + term
                    grads[rows(j), lanes] = value.astype(BF16)
            return carry

        return unrotate

    def scatter(marks, grads, to, lead, first_j, last_j):
        for p in range(first_j // 2, (last_j + 1) // 2):
            both = dot_t(marks[...], grads[2 * p * C : 2 * (p + 1) * C, :])
            for j in (2 * p, 2 * p + 1):
                if j < COEF:
                    value = both[:, (j % 2) * C : (j % 2 + 1) * C]
                    value = value.reshape(lead + (A, C)).astype(BF16)
                    if len(lead) == 3:
                        to[:, :, :, j] = value
                    else:
                        to[:, :, j] = value

    unrotate_src = unrotate_into(xs, 0, 0, COEF)
    unrotate_high = unrotate_into(xf, 1, *HALVES[1])
    unrotate_low = unrotate_into(xf, 1, *HALVES[0])
    back = Reduction(net, tgt_sum, src_sum, out, reduce_scratch)
    lax.fori_loop(0, steps, unrotate_src, 0)
    scatter(mark_s, xs, src_sum, (4, 2), 0, COEF)
    back.start_rows()
    lax.fori_loop(0, steps, unrotate_high, 0)
    scatter(mark_t, xf, tgt_sum, (4, 2, 4), *HALVES[1])
    back.start(1)
    lax.fori_loop(0, steps, unrotate_low, 0)
    back.send_rows()
    scatter(mark_t, xf, tgt_sum, (4, 2, 4), *HALVES[0])
    back.start(0)
    back.join(1)
    net.settle(back.before)
    back.join(0)
    final_high = back.spread(1)
    final_low = back.spread(0)
    back.add_rows()
    net.settle(len(net.copies))
    back.close(1, final_high)
    back.close(0, final_low)


def fused(count, src_ids, tgt_ids, rot, feats, cots, w0, w1, w2):
    def buffer(*lead):
        return pltpu.VMEM(lead + (A, C), BF16)

    scratch = [
        pltpu.VMEM((4, 2, 4, COEF, A, 2 * C), BF16),
        buffer(4, 2, COEF),
        pltpu.VMEM(w0.shape, BF16),
        pltpu.VMEM((2 * w1.shape[1], 2 * w1.shape[2]), BF16),
        pltpu.VMEM((2 * w2.shape[1], 2 * w2.shape[2]), BF16),
        pltpu.VMEM(w0.shape[::-1], BF16),
        pltpu.VMEM((2 * w1.shape[2], 2 * w1.shape[1]), BF16),
        pltpu.VMEM((2 * w2.shape[2], 2 * w2.shape[1]), BF16),
        pltpu.VMEM((FRAME * COEF, E), F32),
        pltpu.VMEM((TGT, E), BF16),
        pltpu.VMEM((SRC, E), BF16),
        pltpu.VMEM((PAIRS * 2 * C, E), BF16),
        pltpu.VMEM((PAIRS * 2 * C, E), BF16),
        pltpu.VMEM((PAIRS * 2 * C, E), BF16),
        pltpu.VMEM((FRAME * 2 * C, E), BF16),
        pltpu.VMEM((FRAME * C, E), BF16),
        pltpu.VMEM((FRAME * C, E), F32),
        buffer(4, 2, 4, COEF),
        buffer(4, 2, COEF),
        pltpu.SemaphoreType.DMA((12,)),
        pltpu.SemaphoreType.DMA((MESSAGES,)),
        pltpu.SemaphoreType.DMA((MESSAGES,)),
        buffer(4, COEF),
        buffer(4, COEF),
        buffer(4, COEF),
        pltpu.VMEM((COEF, A, C), F32),
    ]
    for h, lead in ((0, (2, 4)), (1, (4, 2))):
        whole = length(HALVES[h])
        plus, minus = length(QUARTERS[2 * h]), length(QUARTERS[2 * h + 1])
        scratch += [
            buffer(*lead, plus),
            buffer(*lead, minus),
            buffer(*lead, plus),
            buffer(*lead, minus),
            buffer(*lead, whole),
            buffer(*lead, whole),
            buffer(4, 2, whole),
            buffer(4, 2, whole),
        ]
    vmem = pl.BlockSpec(memory_space=pltpu.VMEM)
    hbm = pl.BlockSpec(memory_space=pl.ANY)
    return pl.pallas_call(
        fused_kernel,
        out_shape=jax.ShapeDtypeStruct((COEF, A, C), F32),
        in_specs=[pl.BlockSpec(memory_space=pltpu.SMEM)] + [vmem] * 5 + [hbm] * 3,
        out_specs=vmem,
        scratch_shapes=scratch,
        compiler_params=pltpu.CompilerParams(
            collective_id=0, has_side_effects=True, vmem_limit_bytes=VMEM_LIMIT
        ),
        name="edge_gradients",
    )(count, src_ids, tgt_ids, rot, feats, cots, w0, w1, w2)


def local(node_feats, grad_out, edge_src, edge_tgt, edge_counts, wigner, w_zero, w_one, w_two):
    total = fused(
        edge_counts,
        edge_src[0],
        edge_tgt[0],
        jnp.transpose(wigner[0, 0]),
        jnp.transpose(node_feats, (1, 0, 2)),
        jnp.transpose(grad_out, (1, 0, 2)),
        w_zero,
        w_one,
        w_two,
    )
    return jnp.transpose(total, (1, 0, 2))


def solution(mesh):
    placed = (
        P(("row", "col"), None, None),
        P(("row", "col"), None, None),
        P("row", "col", None),
        P("row", "col", None),
        P("row", "col"),
        P("row", "col", None, None),
        P(),
        P(),
        P(),
    )
    return jax.shard_map(
        local, mesh=mesh, in_specs=placed, out_specs=P(("row", "col"), None, None), check_vma=False
    )
```

```python
import jax
import jax.numpy as jnp
from jax import lax
from jax.experimental import pallas as pl
from jax.experimental.pallas import tpu as pltpu
from jax.sharding import PartitionSpec as P

MESH = pl.DeviceIdType.MESH
F32 = jnp.float32
BF16 = jnp.bfloat16

ROWS = 8
COLS = 32
A = 8
E = 512
C = 128
COEF = 25
PAIRS = 13
FRAME = 19
GROUP = 16
BLOCK = 256
WIDE = 512
LANES = 128
TGT = COLS * A
SRC = ROWS * A
VMEM_LIMIT = 58 * 1024 * 1024


def frame_rows(degree):
    rows = [degree]
    if degree >= 1:
        rows += [5 + degree - 1, 9 + degree - 1]
    if degree >= 2:
        rows += [13 + degree - 2, 16 + degree - 2]
    return rows


def degree_cols(degree):
    return list(range(degree * degree, (degree + 1) * (degree + 1)))


class Net:
    def __init__(self, send, recv):
        row = lax.axis_index("row")
        col = lax.axis_index("col")
        self.x = x = lax.div(col, 8)
        self.z = z = lax.rem(lax.div(col, 4), 2)
        self.y = y = lax.rem(col, 4)
        self.high = high = lax.div(row, 2)
        self.core = core = lax.rem(row, 2)
        zs = (z, 1 - z)
        self.plane = {}
        for far in (0, 1):
            for step in range(4):
                if step or far:
                    self.plane[0, step, far] = (row, x * 8 + zs[far] * 4 + lax.rem(y + step, 4))
                    self.plane[1, step, far] = (row, lax.rem(x + step, 4) * 8 + zs[far] * 4 + y)
        self.along_high = {
            step: (lax.rem(high + step, 4) * 2 + core, col) for step in (1, 2, 3)
        }
        self.sibling = (high * 2 + 1 - core, col)
        self.send = send
        self.recv = recv
        self.copies = []
        self.sent = 0

    def greet(self):
        barrier = pltpu.get_barrier_semaphore()
        devices = [self.plane[key] for key in self.plane if key != (1, 0, 1)]
        devices += list(self.along_high.values()) + [self.sibling]
        for device in devices:
            pl.semaphore_signal(barrier, inc=1, device_id=device, device_id_type=MESH)
        pl.semaphore_wait(barrier, len(devices))

    def push(self, source, target, device):
        n = len(self.copies)
        copy = pltpu.make_async_remote_copy(
            src_ref=source,
            dst_ref=target,
            send_sem=self.send.at[n],
            recv_sem=self.recv.at[n],
            device_id=device,
            device_id_type=MESH,
        )
        copy.start()
        self.copies.append(copy)
        return copy

    def settle(self, count):
        for copy in self.copies[self.sent : count]:
            copy.wait_send()
        self.sent = count


QUARTERS = ((0, 6), (6, 12), (12, 18), (18, 25))
HALVES = ((0, 12), (12, 25))
MESSAGES = 160


def span(bounds):
    return pl.ds(bounds[0], bounds[1] - bounds[0])


def length(bounds):
    return bounds[1] - bounds[0]


class Reduction:
    def __init__(self, net, tgt, src, out, scratch):
        self.net = net
        self.tgt = tgt
        self.src = src
        self.out = out
        self.row_in, self.row_sum, self.sib_in, self.kept = scratch[:4]
        self.halves = (scratch[4:12], scratch[12:20])
        self.passing = {}
        self.direct = {}

    def toward(self, h, sign):
        return self.net.plane[1 - h, sign, 0]

    def block(self, h, step, piece):
        bounds = QUARTERS[2 * h + piece]
        if h == 0:
            return self.tgt.at[step, :, :, span(bounds)]
        return self.tgt.at[:, :, step, span(bounds)]

    def tail(self, h, piece):
        first = QUARTERS[2 * h][0]
        bounds = QUARTERS[2 * h + piece]
        return pl.ds(bounds[0] - first, length(bounds))

    def start_rows(self):
        self.before = len(self.net.copies)
        self.sib = self.net.push(self.src.at[:, 1], self.sib_in, self.net.sibling)

    def send_rows(self):
        self.sib.wait_recv()
        for high in range(4):
            value = self.src[high, 0].astype(F32) + self.sib_in[high].astype(F32)
            self.row_sum[high] = value.astype(BF16)
        self.rows = [
            self.net.push(
                self.row_sum.at[step], self.row_in.at[4 - step], self.net.along_high[step]
            )
            for step in (2, 1, 3)
        ]

    def start(self, h):
        in_p, in_m, up, um, end_p, end_m = self.halves[h][:6]
        push, block, tail, toward = self.net.push, self.block, self.tail, self.toward
        self.passing[h, 1] = push(block(h, 2, 0), in_p, toward(h, 1))
        self.passing[h, 3] = push(block(h, 2, 1), in_m, toward(h, 3))
        self.direct[h, 1] = push(block(h, 1, 1), end_p.at[:, :, tail(h, 1)], toward(h, 1))
        self.direct[h, 3] = push(block(h, 3, 0), end_m.at[:, :, tail(h, 0)], toward(h, 3))

    def join(self, h):
        in_p, in_m, up, um, end_p, end_m = self.halves[h][:6]
        for sign, piece, came, sums, end in ((1, 0, in_p, up, end_p), (3, 1, in_m, um, end_m)):
            self.passing[h, sign].wait_recv()
            mine = self.block(h, sign, piece)
            for i in range(came.shape[0]):
                for j in range(came.shape[1]):
                    sums[i, j] = (came[i, j].astype(F32) + mine[i, j].astype(F32)).astype(BF16)
            target = end.at[:, :, self.tail(h, piece)]
            self.passing[h, sign] = self.net.push(sums, target, self.toward(h, sign))

    def spread(self, h):
        in_p, in_m, up, um, end_p, end_m, total, ends = self.halves[h]
        for sign in (1, 3):
            self.direct[h, sign].wait_recv()
            self.passing[h, sign].wait_recv()
        at = slice(*HALVES[h])
        final = []
        for step in (2, 1, 3, 0):
            for far in (1, 0):
                if h == 0:
                    mine, one, two = self.tgt[0, far, step, at], end_p[far, step], end_m[far, step]
                else:
                    mine, one, two = self.tgt[step, far, 0, at], end_p[step, far], end_m[step, far]
                value = mine.astype(F32) + one.astype(F32) + two.astype(F32)
                if step or far:
                    total[step, far] = value.astype(BF16)
                    target = ends.at[(4 - step) % 4, far]
                    device = self.net.plane[h, step, far]
                    final.append(self.net.push(total.at[step, far], target, device))
                else:
                    self.kept[at] = value
        return final

    def add_rows(self):
        for copy in self.rows:
            copy.wait_recv()
        value = self.kept[...] + self.row_sum[0].astype(F32)
        for step in (1, 2, 3):
            value = value + self.row_in[step].astype(F32)
        self.kept[...] = value

    def close(self, h, final):
        for copy in final:
            copy.wait_recv()
        ends = self.halves[h][7]
        at = slice(*HALVES[h])
        value = self.kept[at]
        for step in range(4):
            for far in (0, 1):
                if step or far:
                    value = value + ends[step, far].astype(F32)
        self.out[at] = value


class Flow:
    def __init__(self, net, own, full):
        self.net = net
        self.own = own
        self.full = full
        self.arrivals = {}
        self.outer = {}
        self.last = []

    def place(self, h, outer, inner, z, bounds):
        z_now = slice(0, 2) if z == 2 else z
        x, y = (outer, inner) if h == 0 else (inner, outer)
        return self.full.at[x, z_now, y, span(bounds)]

    def send_own(self):
        for step, far in ((0, 1), (1, 0), (3, 0), (1, 1), (3, 1), (2, 0), (2, 1)):
            for h in (0, 1):
                inner = (4 - step) % 4
                self.arrivals[h, inner, far] = self.net.push(
                    self.own.at[span(HALVES[h])],
                    self.place(h, 0, inner, far, HALVES[h]),
                    self.net.plane[h, step, far],
                )
            if step == 3 and not far:
                self.spread(0, 0)

    def spread(self, inner, z):
        for h in (0, 1):
            for far in (0, 1) if z == 2 else (z,):
                if inner or far:
                    self.arrivals[h, inner, far].wait_recv()
            source = self.place(h, 0, inner, z, HALVES[h])
            if (inner, z) == (0, 0):
                source = self.own.at[span(HALVES[h])]
            for sign in (1, 3):
                target = self.place(h, 4 - sign, inner, z, HALVES[h])
                copy = self.net.push(source, target, self.net.plane[1 - h, sign, 0])
                self.outer.setdefault((h, inner, sign), []).append(copy)

    def relay(self, inner):
        for sign, quarter in ((1, 0), (3, 1)):
            for h in (0, 1):
                for copy in self.outer[h, inner, sign]:
                    copy.wait_recv()
                bounds = QUARTERS[2 * h + quarter]
                copy = self.net.push(
                    self.place(h, 4 - sign, inner, 2, bounds),
                    self.place(h, 2, inner, 2, bounds),
                    self.net.plane[1 - h, sign, 0],
                )
                self.last.append(copy)

    def finish(self):
        for copy in self.last:
            copy.wait_recv()


def dot(x, y):
    return jnp.dot(x, y, preferred_element_type=F32)


def dot_t(x, y):
    return lax.dot_general(x, y, (((1,), (1,)), ((), ())), preferred_element_type=F32)


def t_dot(x, y):
    return lax.dot_general(x, y, (((0,), (0,)), ((), ())), preferred_element_type=F32)


def flip(value):
    return jnp.transpose(value.astype(F32)).astype(BF16)


def hot(ids, size):
    return (ids == lax.broadcasted_iota(jnp.int32, size, 0)).astype(F32).astype(BF16)


def tile_at(i):
    lanes = pl.ds(pl.multiple_of(lax.div(i, C // GROUP) * LANES, LANES), LANES)
    shift = lax.rem(i, C // GROUP) * GROUP

    def rows(block):
        return pl.ds(pl.multiple_of(block * C + shift, GROUP), GROUP)

    return lanes, rows


def fused_kernel(
    count, src_ids, tgt_ids, rot, feats, cots, w0, w1, w2, out,
    g, gs, w0_in, full1, full2, w0_flip, flip1, flip2, rot_wide, mark_t, mark_s,
    xf, xc, xs, frame, grad_y, y, tgt_sum, src_sum, local_sem, send, recv, *reduce_scratch,
):
    net = Net(send, recv)
    loads = [pltpu.make_async_copy(w0, w0_in, local_sem.at[0])]
    for n, (weights, full) in enumerate(((w1, full1), (w2, full2))):
        k, m = weights.shape[1:]
        for i in range(2):
            for j in range(2):
                loads.append(
                    pltpu.make_async_copy(
                        weights.at[(i + j) % 2],
                        full.at[pl.ds(i * k, k), pl.ds(j * m, m)],
                        local_sem.at[1 + 4 * n + 2 * i + j],
                    )
                )
    mine = [
        pltpu.make_async_copy(feats, gs.at[0, 0], local_sem.at[9]),
    ]
    for copy in mine + loads:
        copy.start()
    g[0, 0, 0, :, :, 0:C] = feats[...]
    g[0, 0, 0, :, :, C : 2 * C] = cots[...]
    net.greet()

    flow = Flow(net, g.at[0, 0, 0], g)
    flow.send_own()
    sibling = [net.push(feats, gs.at[0, 1], net.sibling)]
    rows = [net.push(feats, gs.at[4 - step, 0], net.along_high[step]) for step in (1, 3, 2)]
    for copy in mine:
        copy.wait()

    valid = lax.broadcasted_iota(jnp.int32, (1, E), 1) < count[0, 0]
    ids = tgt_ids[...]
    near_x = ((ids >> 6) - net.x) & 3
    near_z = ((ids >> 5) & 1) ^ net.z
    near_y = ((ids >> 3) - net.y) & 3
    ids = near_x * 64 + near_z * 32 + near_y * 8 + (ids & 7)
    mark_t[...] = hot(jnp.where(valid, ids, -1), (TGT, E))
    ids = src_ids[...]
    near_high = ((ids >> 4) - net.high) & 3
    near_core = ((ids >> 3) & 1) ^ net.core
    ids = near_high * 16 + near_core * 8 + (ids & 7)
    mark_s[...] = hot(jnp.where(valid, ids, -1), (SRC, E))
    flow.spread(0, 1)
    rot_wide[...] = rot[...].astype(F32)
    for inner in (3, 1, 2):
        flow.spread(inner, 2)

    def flip_zero(r, carry):
        at = pl.ds(pl.multiple_of(r * BLOCK, BLOCK), BLOCK)
        value = flip(w0_in[at, :])
        for part in range(2):
            to = pl.ds(pl.multiple_of(part * (w0.shape[0] // 2) + r * C, C), C)
            w0_flip[:, to] = value[:, part * C : (part + 1) * C]
        return carry

    def flip_order(weights, full, full_flip):
        k, m = weights.shape[1:]

        def body(r, carry):
            at = pl.ds(pl.multiple_of(r * BLOCK, BLOCK), BLOCK)
            below = pl.ds(pl.multiple_of(r * BLOCK + k, BLOCK), BLOCK)
            full[below, 0:m] = -full[below, 0:m]
            for j in range(2):
                value = flip(full[at, j * m : (j + 1) * m])
                for part in range(2):
                    piece = value[:, part * C : (part + 1) * C]
                    to = pl.ds(pl.multiple_of(part * k + r * C, C), C)
                    full_flip[j * m : (j + 1) * m, to] = piece
                    to = pl.ds(pl.multiple_of(part * k + k // 2 + r * C, C), C)
                    full_flip[(1 - j) * m : (2 - j) * m, to] = -piece if j else piece
            return carry

        lax.fori_loop(0, k // BLOCK, body, 0)

    def gather_src():
        for p in range(PAIRS):
            both = [
                gs[:, :, j].astype(F32).reshape(SRC, C) for j in (2 * p, min(2 * p + 1, COEF - 1))
            ]
            block = jnp.concatenate(both, axis=1).astype(BF16)
            xs[2 * p * C : 2 * (p + 1) * C, :] = t_dot(block, mark_s[...]).astype(BF16)

    def gather_tgt():
        for j in range(COEF):
            block = g[:, :, :, j].astype(F32).reshape(TGT, 2 * C).astype(BF16)
            both = t_dot(block, mark_t[...]).astype(BF16)
            xf[j * C : (j + 1) * C, :] = both[0:C]
            xc[j * C : (j + 1) * C, :] = both[C : 2 * C]

    def factor_of(entry, lanes):
        return jnp.broadcast_to(rot_wide[entry : entry + 1, lanes], (GROUP, LANES))

    def rotate_from(source, base):
        def rotate(i, carry):
            lanes, rows = tile_at(i)
            for degree in range(5):
                cols = degree_cols(degree)
                values = [source[rows(j), lanes].astype(F32) for j in cols]
                for k in frame_rows(degree):
                    value = None
                    for n, j in enumerate(cols):
                        term = factor_of(k * COEF + j, lanes) * values[n]
                        value = term if value is None else value + term
                    frame[rows(base + k), lanes] = value.astype(BF16)
            return carry

        return rotate

    steps = (E // LANES) * (C // GROUP)
    parts = ((0, 5, w0_in, w0_flip), (5, 8, full1, flip1), (13, 6, full2, flip2))

    def forward_from(side):
        def forward(i, carry):
            at = pl.ds(pl.multiple_of(i * WIDE, WIDE), WIDE)
            for begin, rows, plain, turned in parts:
                into = slice(begin * C, (begin + rows) * C)
                base = side * FRAME * C
                value = dot(
                    turned[:, side * rows * C : (side + 1) * rows * C],
                    frame[base + begin * C : base + (begin + rows) * C, at],
                )
                y[into, at] = y[into, at] + value if side else value
            return carry

        return forward

    rotate_src, rotate_tgt = rotate_from(xs, 0), rotate_from(xf, FRAME)
    forward_src, forward_tgt = forward_from(0), forward_from(1)

    for copy in loads:
        copy.wait()
    lax.fori_loop(0, w0.shape[0] // BLOCK, flip_zero, 0)
    flow.relay(0)
    for step, copy in zip((1, 3, 2), rows):
        copy.wait_recv()
        sibling.append(net.push(gs.at[4 - step, 0], gs.at[4 - step, 1], net.sibling))
    flip_order(w2, full2, flip2)
    flow.relay(3)
    flow.relay(1)
    flip_order(w1, full1, flip1)
    for copy in sibling:
        copy.wait_recv()
    gather_src()
    flow.relay(2)
    lax.fori_loop(0, steps, rotate_src, 0)
    lax.fori_loop(0, E // WIDE, forward_src, 0)
    flow.finish()
    gather_tgt()
    lax.fori_loop(0, steps, rotate_tgt, 0)
    lax.fori_loop(0, E // WIDE, forward_tgt, 0)

    def gate(i, carry):
        lanes, rows = tile_at(i)
        scalar = y[rows(0), lanes]
        gating = jax.nn.sigmoid(scalar)
        slope = gating * (1.0 - gating)
        total = jnp.zeros((GROUP, LANES), F32)
        lowest = None
        for degree in range(5):
            cols = degree_cols(degree)
            values = [xc[rows(j), lanes].astype(F32) for j in cols]
            for k in frame_rows(degree):
                value = None
                for n, j in enumerate(cols):
                    term = factor_of(k * COEF + j, lanes) * values[n]
                    value = term if value is None else value + term
                if k == 0:
                    lowest = value
                else:
                    total = total + value * y[rows(k), lanes]
                    grad_y[rows(k), lanes] = (gating * value).astype(BF16)
        grad_y[rows(0), lanes] = (lowest * (gating + scalar * slope) + total * slope).astype(BF16)
        return carry

    lax.fori_loop(0, steps, gate, 0)

    def backward(i, carry):
        at = pl.ds(pl.multiple_of(i * WIDE, WIDE), WIDE)
        for begin, rows, weights, turned in parts:
            frame[2 * begin * C : 2 * (begin + rows) * C, at] = dot(
                weights[...], grad_y[begin * C : (begin + rows) * C, at]
            ).astype(BF16)
        return carry

    lax.fori_loop(0, E // WIDE, backward, 0)

    def unrotate_into(grads, side, first_j, last_j):
        def unrotate(i, carry):
            lanes, rows = tile_at(i)
            for degree in range(5):
                js = [j for j in degree_cols(degree) if first_j <= j < last_j]
                if not js:
                    continue
                ks = frame_rows(degree)
                values = [frame[rows(2 * k + side), lanes].astype(F32) for k in ks]
                for j in js:
                    value = None
                    for n, k in enumerate(ks):
                        term = factor_of(k * COEF + j, lanes) * values[n]
                        value = term if value is None else value + term
                    grads[rows(j), lanes] = value.astype(BF16)
            return carry

        return unrotate

    def scatter(marks, grads, to, lead, first_j, last_j):
        for p in range(first_j // 2, (last_j + 1) // 2):
            both = dot_t(marks[...], grads[2 * p * C : 2 * (p + 1) * C, :])
            for j in (2 * p, 2 * p + 1):
                if j < COEF:
                    value = both[:, (j % 2) * C : (j % 2 + 1) * C]
                    value = value.reshape(lead + (A, C)).astype(BF16)
                    if len(lead) == 3:
                        to[:, :, :, j] = value
                    else:
                        to[:, :, j] = value

    unrotate_src = unrotate_into(xs, 0, 0, COEF)
    unrotate_high = unrotate_into(xf, 1, *HALVES[1])
    unrotate_low = unrotate_into(xf, 1, *HALVES[0])
    back = Reduction(net, tgt_sum, src_sum, out, reduce_scratch)
    lax.fori_loop(0, steps, unrotate_src, 0)
    scatter(mark_s, xs, src_sum, (4, 2), 0, COEF)
    back.start_rows()
    lax.fori_loop(0, steps, unrotate_high, 0)
    scatter(mark_t, xf, tgt_sum, (4, 2, 4), *HALVES[1])
    back.start(1)
    lax.fori_loop(0, steps, unrotate_low, 0)
    back.send_rows()
    scatter(mark_t, xf, tgt_sum, (4, 2, 4), *HALVES[0])
    back.start(0)
    back.join(1)
    net.settle(back.before)
    back.join(0)
    final_high = back.spread(1)
    final_low = back.spread(0)
    back.add_rows()
    net.settle(len(net.copies))
    back.close(1, final_high)
    back.close(0, final_low)


def fused(count, src_ids, tgt_ids, rot, feats, cots, w0, w1, w2):
    def buffer(*lead):
        return pltpu.VMEM(lead + (A, C), BF16)

    scratch = [
        pltpu.VMEM((4, 2, 4, COEF, A, 2 * C), BF16),
        buffer(4, 2, COEF),
        pltpu.VMEM(w0.shape, BF16),
        pltpu.VMEM((2 * w1.shape[1], 2 * w1.shape[2]), BF16),
        pltpu.VMEM((2 * w2.shape[1], 2 * w2.shape[2]), BF16),
        pltpu.VMEM(w0.shape[::-1], BF16),
        pltpu.VMEM((2 * w1.shape[2], 2 * w1.shape[1]), BF16),
        pltpu.VMEM((2 * w2.shape[2], 2 * w2.shape[1]), BF16),
        pltpu.VMEM((FRAME * COEF, E), F32),
        pltpu.VMEM((TGT, E), BF16),
        pltpu.VMEM((SRC, E), BF16),
        pltpu.VMEM((PAIRS * 2 * C, E), BF16),
        pltpu.VMEM((PAIRS * 2 * C, E), BF16),
        pltpu.VMEM((PAIRS * 2 * C, E), BF16),
        pltpu.VMEM((FRAME * 2 * C, E), BF16),
        pltpu.VMEM((FRAME * C, E), BF16),
        pltpu.VMEM((FRAME * C, E), F32),
        buffer(4, 2, 4, COEF),
        buffer(4, 2, COEF),
        pltpu.SemaphoreType.DMA((12,)),
        pltpu.SemaphoreType.DMA((MESSAGES,)),
        pltpu.SemaphoreType.DMA((MESSAGES,)),
        buffer(4, COEF),
        buffer(4, COEF),
        buffer(4, COEF),
        pltpu.VMEM((COEF, A, C), F32),
    ]
    for h, lead in ((0, (2, 4)), (1, (4, 2))):
        whole = length(HALVES[h])
        plus, minus = length(QUARTERS[2 * h]), length(QUARTERS[2 * h + 1])
        scratch += [
            buffer(*lead, plus),
            buffer(*lead, minus),
            buffer(*lead, plus),
            buffer(*lead, minus),
            buffer(*lead, whole),
            buffer(*lead, whole),
            buffer(4, 2, whole),
            buffer(4, 2, whole),
        ]
    vmem = pl.BlockSpec(memory_space=pltpu.VMEM)
    hbm = pl.BlockSpec(memory_space=pl.ANY)
    return pl.pallas_call(
        fused_kernel,
        out_shape=jax.ShapeDtypeStruct((COEF, A, C), F32),
        in_specs=[pl.BlockSpec(memory_space=pltpu.SMEM)] + [vmem] * 5 + [hbm] * 3,
        out_specs=vmem,
        scratch_shapes=scratch,
        compiler_params=pltpu.CompilerParams(
            collective_id=0, has_side_effects=True, vmem_limit_bytes=VMEM_LIMIT
        ),
        name="edge_gradients",
    )(count, src_ids, tgt_ids, rot, feats, cots, w0, w1, w2)


def local(node_feats, grad_out, edge_src, edge_tgt, edge_counts, wigner, w_zero, w_one, w_two):
    total = fused(
        edge_counts,
        edge_src[0],
        edge_tgt[0],
        jnp.transpose(wigner[0, 0]),
        jnp.transpose(node_feats, (1, 0, 2)),
        jnp.transpose(grad_out, (1, 0, 2)),
        w_zero,
        w_one,
        w_two,
    )
    return jnp.transpose(total, (1, 0, 2))


def solution(mesh):
    placed = (
        P(("row", "col"), None, None),
        P(("row", "col"), None, None),
        P("row", "col", None),
        P("row", "col", None),
        P("row", "col"),
        P("row", "col", None, None),
        P(),
        P(),
        P(),
    )
    return jax.shard_map(
        local, mesh=mesh, in_specs=placed, out_specs=P(("row", "col"), None, None), check_vma=False
    )
```
